32 devices in a mesh: dp: 8 (over z, y), mp: 4 (over x, core).
Axes of the slice: x: 2, y: 2, z: 4, core: 2. Of those that a mesh axis runs over, the one named last changes fastest.
Arguments:
- tokens: bfloat16 [16384, 768], P(('dp', 'mp')), may hold values from -6 to 6
- cotangent: bfloat16 [16384, 768], P(('dp', 'mp')), may hold values from -6 to 6
- doc_lengths: int32 [16, 4], P('dp'), may hold values from 1 to 512, 1024 in all within a row
- time_index: int32 [16], P('dp'), may hold values from 0 to 999
- attention_norm_gain: float32 [768], replicated, may hold values from 0.5 to 1.5
- qkv_weight: bfloat16 [768, 2304], P(None, 'mp'), may hold values from -0.21875 to 0.21875
- out_weight: bfloat16 [768, 768], P('mp'), may hold values from -0.875 to 0.875
- feedforward_norm_gain: float32 [768], replicated, may hold values from 0.5 to 1.5
- up_weight: bfloat16 [768, 3072], P(None, 'mp'), may hold values from -0.21875 to 0.21875
- up_bias: bfloat16 [3072], P('mp'), may hold values from -3 to 3
- down_weight: bfloat16 [3072, 768], P('mp'), may hold values from -0.109375 to 0.109375
- down_bias: float32 [768], replicated, may hold values from -2 to 2
- ada_weight: float32 [128, 4608], replicated, may hold values from -0.5 to 0.5
- ada_bias: float32 [4608], replicated, may hold values from -3 to 3
Outputs:
- block_out: bfloat16 [16384, 768], P(('dp', 'mp'))
- input_gradient: float32 [16384, 768], P(('dp', 'mp'))
- attention_norm_gain_gradient: float32 [768], replicated
- qkv_grad: float32 [768, 2304], P(None, 'mp')
- out_grad: float32 [768, 768], P('mp')
- feedforward_norm_gain_gradient: float32 [768], replicated
- up_grad: float32 [768, 3072], P(None, 'mp')
- up_bias_grad: float32 [3072], P('mp')
- down_grad: float32 [3072, 768], P('mp')
- down_bias_grad: float32 [768], replicated
- ada_grad: float32 [128, 4608], replicated
- ada_bias_grad: float32 [4608], replicated
The draws below stay inside these ranges and needn't reach their ends.
Inputs may be any that keep to these rules, and one draw needn't show every extreme that they name: `doc_lengths`: in every slot the 4 lengths sum to 1024, and the longest has 512 tokens.
All inputs are finite; a program needn't handle non-finite values.
Results may differ from the reference program's by a relative error of at most 0.023.
Values may be sent and summed in bfloat16 or wider, within the bound.
No kernel may reach another device: no remote copies, remote signals or barrier semaphores. Data moves between devices by JAX's collectives and lax.ppermute only.
A program may use at most 128 MiB of HBM per device.

```python
import math
import jax
import jax.numpy as jnp
import numpy as np
from jax import lax

D = 768
HEADS = 12
HEAD_DIM = 64
FF = 3072
COND = 128
SLOT = 1024
DOCS = 4
SLOTS = 16
TOKENS = 16384


def set_ends(entries, rng, low, high):
    longest = entries.shape.index(max(entries.shape))
    spots = []
    for shift in (0, 1):
        where = [jax.random.randint(jax.random.fold_in(rng, axis), (), 0, length) for axis, length in enumerate(entries.shape)]
        where[longest] = (where[longest] + shift) % entries.shape[longest]
        spots.append(tuple(where))
    return entries.at[spots[0]].set(low).at[spots[1]].set(high)


def block_scale(key, shape, shards, least, top_value):
    level, own = 1.0, jax.random.fold_in(key, 6)
    for dim, shards_of in shards:
        steps = jnp.exp(jax.random.uniform(jax.random.fold_in(own, dim), (shards_of,), jnp.float32, least / len(shards), top_value / len(shards)))
        level = level * jnp.repeat(steps, shape[dim] // shards_of).reshape([-1 if axis == dim else 1 for axis in range(len(shape))])
    return level


def profile(number_of, total, bound, skew):
    portions = [(1 << 20) // math.isqrt(rank ** skew) + 1 for rank in range(2, number_of + 1)]
    spare, holding = total - bound - (number_of - 1), [1] * (number_of - 1)
    while spare > 0:
        candidates = [i for i in range(number_of - 1) if holding[i] < bound]
        pool, left = sum([portions[i] for i in candidates]), spare
        for i in candidates:
            extra = min(bound - holding[i], max(1, left * portions[i] // pool), spare)
            holding[i] = holding[i] + extra
            spare = spare - extra
    return np.array([bound] + holding)


def uneven_parts(stream_key, count, total, bound, slope):
    if count == 2:
        one = jax.random.randint(stream_key, (), max(1, total - bound), min(bound, total - 1) + 1)
        return jnp.stack([one, total - one])
    lengths = jnp.asarray(profile(count, total, bound, slope), jnp.int32)
    twos = (count - 1) // 2
    source_of, taker = lengths[1:1 + 2 * twos:2], lengths[2:2 + 2 * twos:2]
    slack = jnp.minimum(source_of - 1, bound - taker)
    passed = jax.random.randint(jax.random.fold_in(stream_key, 1), (twos,), 0, 1 << 20) % (slack + 1)
    lengths = lengths.at[1:1 + 2 * twos:2].set(source_of - passed).at[2:2 + 2 * twos:2].set(taker + passed)
    return lengths[jax.random.permutation(jax.random.fold_in(stream_key, 2), count)]


def noise(stream_key, dims, scale, most, cuts=(), kind=jnp.bfloat16):
    result = jax.random.normal(stream_key, dims, jnp.float32) * scale
    if len(cuts) > 0:
        result = block_scale(stream_key, dims, cuts, -0.22, 0.18) * result
    return jnp.clip(result, min=-most, max=most).astype(kind)


def setup_inputs(seed: int = 0) -> dict:
    key_list = jax.random.split(jax.random.key(seed), 15)
    return {
        "tokens": noise(key_list[0], (TOKENS, D), 1.0, 6.0, ((0, 32),)),
        "cotangent": noise(key_list[1], (TOKENS, D), 1.0, 6.0, ((0, 32),)),
        "doc_lengths": jax.vmap(lambda own: uneven_parts(own, DOCS, SLOT, SLOT // 2, 2))(jax.random.split(key_list[2], SLOTS)).reshape((SLOTS, DOCS)).astype(jnp.int32),
        "time_index": set_ends(jax.random.randint(key_list[3], (SLOTS,), 0, 1000), jax.random.fold_in(key_list[3], 1), 0, 999).astype(jnp.int32),
        "attention_norm_gain": jnp.clip(1.0 + 0.1 * jax.random.normal(key_list[4], (D,), jnp.float32), 0.5, 1.5),
        "qkv_weight": noise(key_list[5], (D, 3 * D), D ** -0.5, 0.21875, ((1, 4),)),
        "out_weight": noise(key_list[6], (D, D), (D // 16) ** -0.5, 0.875, ((0, 4),)),
        "feedforward_norm_gain": jnp.clip(1.0 + 0.1 * jax.random.normal(key_list[7], (D,), jnp.float32), 0.5, 1.5),
        "up_weight": noise(key_list[8], (D, FF), D ** -0.5, 0.21875, ((1, 4),)),
        "up_bias": noise(key_list[9], (FF,), 0.5, 3.0, ((0, 4),)),
        "down_weight": noise(key_list[10], (FF, D), FF ** -0.5, 0.109375, ((0, 4),)),
        "down_bias": noise(key_list[11], (D,), 0.3, 2.0, (), jnp.float32),
        "ada_weight": noise(key_list[12], (COND, 6 * D), COND ** -0.5, 0.5, (), jnp.float32),
        "ada_bias": noise(key_list[13], (6 * D,), 0.5, 3.0, (), jnp.float32),
    }


@jax.custom_vjp
def low(v):
    return lax.optimization_barrier(v.astype(jnp.bfloat16)).astype(jnp.float32)

@jax.custom_vjp
def low_back(v):
    return v

def low_keep(v):
    return (low(v), None)

def low_pass(kept, grad):
    return (grad,)

def back_keep(v):
    return (v, None)

def back_low(kept, grad):
    return (low(grad),)
low.defvjp(low_keep, low_pass)
low_back.defvjp(back_keep, back_low)

def time_features(time_index):
    half_width = COND // 2
    ladder = jnp.arange(half_width).astype(jnp.float32)
    frequency = jnp.exp(ladder * (-math.log(10000.0) / half_width))
    angles = time_index.astype(jnp.float32)[:, None] * frequency[None, :]
    return jax.nn.silu(jnp.concatenate([jnp.cos(angles), jnp.sin(angles)], axis=1))

def segment_ids(doc_lengths, slot_length):
    doc_ends = jnp.cumsum(doc_lengths, axis=1).astype(jnp.int32)
    places = jnp.arange(slot_length).astype(jnp.int32)
    return lax.optimization_barrier(jnp.sum((places[None, :, None] >= doc_ends[:, None, :]).astype(jnp.int32), axis=2)).astype(jnp.int32)

def normalize(values, gain):
    center = values - lax.optimization_barrier(jnp.mean(values, axis=-1, keepdims=True))
    spread = lax.optimization_barrier(jnp.mean(center * center, axis=-1, keepdims=True))
    return center * lax.rsqrt(spread + 1e-05) * gain

def attend_slot(slot_inputs):
    precise = lax.Precision.HIGHEST
    projected, segments = slot_inputs
    queries = projected[:, :, 0]
    key_rows = projected[:, :, 1]
    value_rows = projected[:, :, 2]
    scores = jnp.einsum('qhe,khe->hqk', queries, key_rows, precision=precise) * HEAD_DIM ** (-0.5)
    scores = low_back(scores)
    allowed = segments[:, None] == segments[None, :]
    scores = jnp.where(allowed[None], scores, -1e+30)
    weights = jnp.exp(scores - lax.optimization_barrier(jnp.max(scores, axis=-1, keepdims=True)))
    weights = weights / lax.optimization_barrier(jnp.sum(weights, axis=-1, keepdims=True))
    mixture = jnp.einsum('hqk,khe->qhe', low(weights), value_rows, precision=precise)
    return mixture.reshape(SLOT, D)

def forward(input_rows, attention_norm_gain, qkv_weight, out_weight, feedforward_norm_gain, up_weight, up_bias, down_weight, down_bias, ada_weight, ada_bias, features, segments):
    precise = lax.Precision.HIGHEST
    modulation = jnp.dot(features, ada_weight, precision=precise) + ada_bias
    pieces = [modulation[:, column * D:(column + 1) * D][:, None, :] for column in range(6)]
    shift_one, scale_one, gate_one, shift_two, scale_two, gate_two = pieces
    stream = input_rows.reshape(SLOTS, SLOT, D)
    entry_one = low(normalize(stream, attention_norm_gain) * (1.0 + scale_one) + shift_one)
    projected = jnp.einsum('std,de->ste', entry_one, qkv_weight, precision=precise)
    projected = low_back(low(projected)).reshape(SLOTS, SLOT, HEADS, 3, HEAD_DIM)
    mixture = lax.map(jax.checkpoint(attend_slot), (projected, segments))
    mixture = low_back(low(mixture))
    branch_one = low_back(jnp.einsum('ste,ed->std', mixture, out_weight, precision=precise))
    middle_state = stream + gate_one * branch_one
    entry_two = low(normalize(middle_state, feedforward_norm_gain) * (1.0 + scale_two) + shift_two)
    hidden_pre = low_back(jnp.einsum('std,df->stf', entry_two, up_weight, precision=precise) + up_bias)
    hidden = low(jax.nn.gelu(hidden_pre, approximate=True))
    branch_two = low_back(jnp.einsum('stf,fd->std', hidden, down_weight, precision=precise) + down_bias)
    return (middle_state + gate_two * branch_two).reshape(SLOTS * SLOT, D)

def reference(tokens, cotangent, doc_lengths, time_index, attention_norm_gain, qkv_weight, out_weight, feedforward_norm_gain, up_weight, up_bias, down_weight, down_bias, ada_weight, ada_bias):
    features = time_features(time_index)
    segments = segment_ids(doc_lengths, SLOT)

    def layer_forward(input_rows, gain_one, weight_qkv, weight_out, gain_two, weight_up, bias_up, weight_down, bias_down, weight_ada, bias_ada):
        return forward(input_rows, gain_one, weight_qkv, weight_out, gain_two, weight_up, bias_up, weight_down, bias_down, weight_ada, bias_ada, features, segments)
    output, pullback = jax.vjp(layer_forward, tokens.astype(jnp.float32), attention_norm_gain, qkv_weight.astype(jnp.float32), out_weight.astype(jnp.float32), feedforward_norm_gain, up_weight.astype(jnp.float32), up_bias.astype(jnp.float32), down_weight.astype(jnp.float32), down_bias, ada_weight, ada_bias)
    gradients = pullback(cotangent.astype(jnp.float32))
    return (output.astype(jnp.bfloat16), gradients[0], gradients[1], gradients[2], gradients[3], gradients[4], gradients[5], gradients[6], gradients[7], gradients[8], gradients[9], gradients[10])
```

```python
from functools import partial
import math

import jax
import jax.numpy as jnp
from jax import lax
from jax.experimental import pallas as pl
from jax.experimental.pallas import tpu as pltpu
from jax.sharding import PartitionSpec as P

HEAD_DIM = 64
COND = 128
BLOCK = 256
BF16 = jnp.bfloat16
F32 = jnp.float32


def swap(value, axis, bit):
    size = lax.axis_size(axis)
    return lax.ppermute(value, axis, [(i, i ^ bit) for i in range(size)])


def time_features(time_index, cond_width):
    half_width = cond_width // 2
    ladder = jnp.arange(half_width).astype(F32)
    frequency = jnp.exp(ladder * (-math.log(10000.0) / half_width))
    angles = time_index.astype(F32)[:, None] * frequency[None, :]
    return jax.nn.silu(jnp.concatenate([jnp.cos(angles), jnp.sin(angles)], axis=1))


def standard_score_rows(values):
    center = values - jnp.mean(values, axis=-1, keepdims=True)
    inverse_deviation = lax.rsqrt(jnp.mean(center * center, axis=-1, keepdims=True) + 1e-05)
    return (center * inverse_deviation, inverse_deviation)


def norm_reverse_pass(incoming_gradient, centered_scaled, inverse_deviation):
    return inverse_deviation * (
        incoming_gradient
        - jnp.mean(incoming_gradient, axis=-1, keepdims=True)
        - centered_scaled * jnp.mean(incoming_gradient * centered_scaled, axis=-1, keepdims=True)
    )


def dot(a, b):
    return jnp.dot(a, b, preferred_element_type=F32)


def contract_rows(a, b):
    return lax.dot_general(a, b, (((0,), (0,)), ((), ())), preferred_element_type=F32)


def times_transposed(a, b):
    return lax.dot_general(a, b, (((1,), (1,)), ((), ())), preferred_element_type=F32)


def gelu_grad(values, incoming_gradient):
    return jax.vjp(lambda inner: jax.nn.gelu(inner, approximate=True), values)[1](
        incoming_gradient
    )[0]


def window_sizes(slot_length):
    return tuple(range(2 * BLOCK // 2, slot_length + 1, BLOCK // 2))


def augmented(columns, extra):
    return jnp.concatenate([columns, extra], axis=1)


def attend_forward_kernel(start_ref, size_ref, qkv_ref, key_extra_ref, query_extra_ref, out_ref, lse_ref, key_ref, query_ref, value_ref):
    slot_length = qkv_ref.shape[0]
    heads = out_ref.shape[1] // HEAD_DIM
    sizes = window_sizes(slot_length)
    for head in range(heads):
        at = 3 * HEAD_DIM * head
        query_ref[head] = augmented(qkv_ref[:, at : at + HEAD_DIM] * 0.125, query_extra_ref[...])
        key_ref[head] = augmented(qkv_ref[:, at + HEAD_DIM : at + 2 * HEAD_DIM], key_extra_ref[...])
        value_ref[head] = qkv_ref[:, at + 2 * HEAD_DIM : at + 3 * HEAD_DIM].T

    def one_block(block, carry):
        rows = pl.ds(pl.multiple_of(block * BLOCK, BLOCK), BLOCK)
        start = pl.multiple_of(start_ref[block], BLOCK // 2)
        for size in sizes:

            @pl.when(size_ref[block] == size)
            def _():
                mixed = []
                for head in range(heads):
                    scores = times_transposed(key_ref[head, pl.ds(start, size), :], query_ref[head, rows, :])
                    highest = jnp.max(scores, axis=0, keepdims=True)
                    raised = jnp.exp(scores - highest)
                    total = jnp.sum(raised, axis=0, keepdims=True)
                    mixture = dot(value_ref[head, :, pl.ds(start, size)], raised.astype(BF16))
                    mixed.append(mixture / total)
                    lse_ref[head : head + 1, rows] = highest + jnp.log(total)
                out_ref[rows, :] = jnp.concatenate(mixed, axis=0).T.astype(BF16)

        return carry

    lax.fori_loop(0, slot_length // BLOCK, one_block, 0)


def attend_backward_kernel(
    start_ref, size_ref, qkv_ref, key_extra_ref, query_extra_ref, out_ref, lse_ref, up_ref, grad_ref,
    key_ref, query_ref, value_ref, key_turned_ref, up_head_ref, query_grad_ref, key_grad_ref, value_grad_ref,
):
    slot_length = qkv_ref.shape[0]
    heads = out_ref.shape[1] // HEAD_DIM
    sizes = window_sizes(slot_length)
    for head in range(heads):
        at = 3 * HEAD_DIM * head
        query_ref[head] = augmented(qkv_ref[:, at : at + HEAD_DIM] * 0.125, query_extra_ref[...])
        keys = qkv_ref[:, at + HEAD_DIM : at + 2 * HEAD_DIM]
        key_ref[head] = augmented(keys, key_extra_ref[...])
        key_turned_ref[head] = keys.T
        value_ref[head] = qkv_ref[:, at + 2 * HEAD_DIM : at + 3 * HEAD_DIM]
        up_head_ref[head] = up_ref[:, head * HEAD_DIM : (head + 1) * HEAD_DIM]
    key_grad_ref[...] = jnp.zeros_like(key_grad_ref)
    value_grad_ref[...] = jnp.zeros_like(value_grad_ref)

    def one_block(block, carry):
        rows = pl.ds(pl.multiple_of(block * BLOCK, BLOCK), BLOCK)
        start = pl.multiple_of(start_ref[block], BLOCK // 2)
        inner = (out_ref[rows, :].astype(F32) * up_ref[rows, :].astype(F32)).T
        for size in sizes:

            @pl.when(size_ref[block] == size)
            def _():
                span = pl.ds(start, size)
                query_grads = []
                for head in range(heads):
                    query = query_ref[head, rows, :]
                    upstream = up_head_ref[head, rows, :]
                    scores = times_transposed(key_ref[head, span, :], query)
                    weights = jnp.exp(scores - lse_ref[head : head + 1, rows])
                    weight_grad = times_transposed(value_ref[head, span, :], upstream)
                    inner_sum = jnp.sum(inner[head * HEAD_DIM : (head + 1) * HEAD_DIM], axis=0, keepdims=True)
                    score_grad = (weights * (weight_grad - inner_sum)).astype(BF16)
                    value_grad_ref[head, span, :] += dot(weights.astype(BF16), upstream)
                    key_grad_ref[head, span, :] += dot(score_grad, query[:, :HEAD_DIM])
                    query_grads.append(dot(key_turned_ref[head, :, span], score_grad))
                query_grad_ref[rows, :] = (jnp.concatenate(query_grads, axis=0) * 0.125).T.astype(BF16)

        return carry

    lax.fori_loop(0, slot_length // BLOCK, one_block, 0)
    parts = []
    for head in range(heads):
        parts.append(query_grad_ref[:, head * HEAD_DIM : (head + 1) * HEAD_DIM])
        parts.append(key_grad_ref[head].astype(BF16))
        parts.append(value_grad_ref[head].astype(BF16))
    grad_ref[...] = jnp.concatenate(parts, axis=1)


def whole():
    return pl.BlockSpec(memory_space=pltpu.VMEM)


def scalars():
    return pl.BlockSpec(memory_space=pltpu.SMEM)


def attend_forward(qkv, spans):
    length = qkv.shape[0]
    heads = qkv.shape[1] // (3 * HEAD_DIM)
    starts, sizes, key_extra, query_extra = spans
    return pl.pallas_call(
        attend_forward_kernel,
        out_shape=(
            jax.ShapeDtypeStruct((length, heads * HEAD_DIM), BF16),
            jax.ShapeDtypeStruct((8, length), F32),
        ),
        in_specs=[scalars(), scalars(), whole(), whole(), whole()],
        out_specs=(whole(), whole()),
        scratch_shapes=[
            pltpu.VMEM((heads, length, 2 * HEAD_DIM), BF16),
            pltpu.VMEM((heads, length, 2 * HEAD_DIM), BF16),
            pltpu.VMEM((heads, HEAD_DIM, length), BF16),
        ],
        compiler_params=pltpu.CompilerParams(vmem_limit_bytes=40 * 2**20),
        cost_estimate=pl.CostEstimate(flops=heads * length * length * 512, bytes_accessed=4 * 2**20, transcendentals=heads * length * length // 2),
        name="attend_forward",
    )(starts, sizes, qkv, key_extra, query_extra)


def attend_backward(qkv, spans, mixture, lse, upstream):
    length = qkv.shape[0]
    heads = qkv.shape[1] // (3 * HEAD_DIM)
    starts, sizes, key_extra, query_extra = spans
    return pl.pallas_call(
        attend_backward_kernel,
        out_shape=jax.ShapeDtypeStruct(qkv.shape, BF16),
        in_specs=[scalars(), scalars()] + [whole()] * 6,
        out_specs=whole(),
        scratch_shapes=[
            pltpu.VMEM((heads, length, 2 * HEAD_DIM), BF16),
            pltpu.VMEM((heads, length, 2 * HEAD_DIM), BF16),
            pltpu.VMEM((heads, length, HEAD_DIM), BF16),
            pltpu.VMEM((heads, HEAD_DIM, length), BF16),
            pltpu.VMEM((heads, length, HEAD_DIM), BF16),
            pltpu.VMEM((length, heads * HEAD_DIM), BF16),
            pltpu.VMEM((heads, length, HEAD_DIM), F32),
            pltpu.VMEM((heads, length, HEAD_DIM), F32),
        ],
        compiler_params=pltpu.CompilerParams(vmem_limit_bytes=40 * 2**20),
        cost_estimate=pl.CostEstimate(flops=heads * length * length * 1280, bytes_accessed=6 * 2**20, transcendentals=heads * length * length // 2),
        name="attend_backward",
    )(starts, sizes, qkv, key_extra, query_extra, mixture, lse, upstream)


def attention_spans(lengths, slot_length):
    ends = jnp.cumsum(lengths)
    places = jnp.arange(slot_length, dtype=jnp.int32)
    segments = jnp.sum((places[:, None] >= ends[None, :]).astype(jnp.int32), axis=1)
    first = jnp.arange(0, slot_length, BLOCK, dtype=jnp.int32)
    last = first + (BLOCK - 1)
    low = jnp.max(jnp.where(ends[None, :] <= first[:, None], ends[None, :], 0), axis=1)
    high = jnp.min(jnp.where(ends[None, :] > last[:, None], ends[None, :], slot_length), axis=1)
    step = BLOCK // 2
    low = low // step * step
    sizes = jnp.maximum((high - low + step - 1) // step * step, 2 * step)
    starts = jnp.minimum(low, slot_length - sizes)
    lanes = jnp.arange(HEAD_DIM, dtype=jnp.int32)[None, :]
    same = lanes == segments[:, None]
    documents = lengths.shape[0]
    query_extra = jnp.where(same, 1.0, 0.0).astype(BF16)
    key_extra = jnp.where((lanes < documents) & ~same, -1e30, 0.0).astype(BF16)
    return starts.astype(jnp.int32), sizes.astype(jnp.int32), key_extra, query_extra


def sum_over_dp(value):
    index = lax.axis_index("dp")
    bits = []
    bit = 1
    while bit < lax.axis_size("dp"):
        bits.append(bit)
        bit *= 2
    for bit in bits:
        half = value.shape[0] // 2
        mine = (index // bit) % 2
        kept = lax.dynamic_slice_in_dim(value, mine * half, half, 0)
        sent = lax.dynamic_slice_in_dim(value, (1 - mine) * half, half, 0)
        value = (kept.astype(F32) + swap(sent, "dp", bit).astype(F32)).astype(BF16)
    for bit in reversed(bits):
        other = swap(value, "dp", bit)
        mine = (index // bit) % 2
        value = jnp.where(
            mine == 0,
            jnp.concatenate([value, other], axis=0),
            jnp.concatenate([other, value], axis=0),
        )
    return value.astype(F32)


def gather_small(value):
    for axis, bit in small_hops():
        other = swap(value, axis, bit)
        mine = (lax.axis_index(axis) // bit) % 2
        value = jnp.where(
            mine == 0,
            jnp.concatenate([value, other], axis=0),
            jnp.concatenate([other, value], axis=0),
        )
    return value


def small_hops():
    hops = [("mp", 2)]
    bit = 1
    while bit < lax.axis_size("dp"):
        hops.append(("dp", bit))
        bit *= 2
    return hops


def per_device(
    tokens,
    cotangent,
    doc_lengths,
    time_index,
    attention_norm_gain,
    qkv_weight,
    out_weight,
    feedforward_norm_gain,
    up_weight,
    up_bias,
    down_weight,
    down_bias,
    ada_weight,
    ada_bias,
):
    rows, width = tokens.shape
    length = 2 * rows
    core = lax.axis_index("mp") % 2
    slot = lax.axis_index("mp") // 2

    qkv_weight_x = swap(qkv_weight, "mp", 2)
    out_weight_x = swap(out_weight, "mp", 2)
    up_weight_x = swap(up_weight, "mp", 2)
    down_weight_x = swap(down_weight, "mp", 2)
    up_bias_x = swap(up_bias, "mp", 2)

    def both(own):
        other = swap(own, "mp", 1)
        return jnp.where(core == 0, jnp.concatenate([own, other], axis=0), jnp.concatenate([other, own], axis=0))

    def own_sum(partial_rows):
        sent = lax.dynamic_slice_in_dim(partial_rows, (1 - core) * rows, rows, 0).astype(BF16)
        kept = lax.dynamic_slice_in_dim(partial_rows, core * rows, rows, 0)
        return kept + swap(sent, "mp", 1).astype(F32)

    features = time_features(lax.dynamic_slice_in_dim(time_index, slot, 1, 0), COND)
    modulation = jnp.sum(features[0][:, None] * ada_weight, axis=0) + ada_bias
    shift_one, scale_one, gate_one, shift_two, scale_two, gate_two = jnp.split(modulation[None, :], 6, axis=1)
    lengths = lax.dynamic_slice_in_dim(doc_lengths, slot, 1, 0)[0]
    spans = attention_spans(lengths, length)

    input_rows = tokens.astype(F32)
    incoming = cotangent.astype(F32)
    scored_one, inverse_one = standard_score_rows(input_rows)
    normed_one = scored_one * attention_norm_gain
    entry_one = both((normed_one * (1.0 + scale_one) + shift_one).astype(BF16))
    branch_grad = (gate_two * incoming).astype(BF16)
    branch_grad_both = both(branch_grad)

    qkv = dot(entry_one, qkv_weight).astype(BF16)
    mixture, lse = attend_forward(qkv, spans)
    qkv_x = dot(entry_one, qkv_weight_x).astype(BF16)
    mixture_x, lse_x = attend_forward(qkv_x, spans)
    branch_one = own_sum(dot(mixture, out_weight) + dot(mixture_x, out_weight_x))
    middle = input_rows + gate_one * branch_one
    scored_two, inverse_two = standard_score_rows(middle)
    normed_two = scored_two * feedforward_norm_gain
    entry_two = both((normed_two * (1.0 + scale_two) + shift_two).astype(BF16))

    def hidden_part(weight_up, bias_up, weight_down):
        pre = dot(entry_two, weight_up) + bias_up.astype(F32)
        hidden = jax.nn.gelu(pre, approximate=True).astype(BF16)
        hidden_grad = times_transposed(branch_grad_both, weight_down)
        pre_grad = gelu_grad(pre, hidden_grad).astype(BF16)
        entry_grad = times_transposed(pre_grad, weight_up)
        up_grad = contract_rows(entry_two, pre_grad)
        down_grad = contract_rows(hidden, branch_grad_both)
        bias_grad = jnp.sum(pre_grad.astype(F32), axis=0)
        return dot(hidden, weight_down), entry_grad, up_grad, down_grad, bias_grad

    out_own, entry_grad_own, up_grad, down_grad, up_bias_grad = hidden_part(up_weight, up_bias, down_weight)
    out_x, entry_grad_x, up_grad_x, down_grad_x, up_bias_grad_x = hidden_part(up_weight_x, up_bias_x, down_weight_x)
    entry_two_grad = own_sum(entry_grad_own + entry_grad_x)
    branch_two = own_sum(out_own + out_x) + down_bias
    output = (middle + gate_two * branch_two).astype(BF16)

    def pair_sum(own, for_neighbour):
        return (own + swap(for_neighbour.astype(BF16), "mp", 2).astype(F32)).astype(BF16)

    up_grad = sum_over_dp(pair_sum(up_grad, up_grad_x))
    down_grad = sum_over_dp(pair_sum(down_grad, down_grad_x))

    second_grad = entry_two_grad * (1.0 + scale_two)
    middle_grad = incoming + norm_reverse_pass(second_grad * feedforward_norm_gain, scored_two, inverse_two)
    attn_grad = both((gate_one * middle_grad).astype(BF16))
    mixture_grad = times_transposed(attn_grad, out_weight).astype(BF16)
    mixture_grad_x = times_transposed(attn_grad, out_weight_x).astype(BF16)
    out_grad = contract_rows(mixture, attn_grad)
    out_grad_x = contract_rows(mixture_x, attn_grad)
    out_grad = sum_over_dp(pair_sum(out_grad, out_grad_x))
    qkv_back_x = attend_backward(qkv_x, spans, mixture_x, lse_x, mixture_grad_x)
    qkv_grad_x = contract_rows(entry_one, qkv_back_x)
    qkv_back = attend_backward(qkv, spans, mixture, lse, mixture_grad)
    qkv_grad = contract_rows(entry_one, qkv_back)
    qkv_grad = sum_over_dp(pair_sum(qkv_grad, qkv_grad_x))
    entry_one_grad = own_sum(times_transposed(qkv_back, qkv_weight) + times_transposed(qkv_back_x, qkv_weight_x))
    first_grad = entry_one_grad * (1.0 + scale_one)
    input_gradient = middle_grad + norm_reverse_pass(first_grad * attention_norm_gain, scored_one, inverse_one)

    def column(term):
        return jnp.sum(term, axis=0, keepdims=True)

    sums = jnp.concatenate(
        [
            column(entry_one_grad),
            column(entry_one_grad * normed_one),
            column(middle_grad * branch_one),
            column(entry_two_grad),
            column(entry_two_grad * normed_two),
            column(incoming * branch_two),
            column(first_grad * scored_one),
            column(second_grad * scored_two),
            column(branch_grad.astype(F32)),
        ],
        axis=0,
    )
    sums = sums + swap(sums, "mp", 1)
    extra = jnp.pad(features, ((0, 0), (0, width - COND)))
    table = jnp.concatenate([sums, extra], axis=0)[None]
    table = gather_small(table)
    slots = table.shape[0]
    modulation_grad = table[:, :6].reshape(slots, 6 * width)
    ada_grad = lax.dot_general(
        table[:, 9, :COND], modulation_grad, (((0,), (0,)), ((), ())), precision=lax.Precision.HIGHEST, preferred_element_type=F32
    )
    totals = jnp.sum(table[:, :9], axis=0)
    bias = up_bias_grad + swap(up_bias_grad_x, "mp", 2)
    bit = 1
    while bit < lax.axis_size("dp"):
        bias = bias + swap(bias, "dp", bit)
        bit *= 2
    return (
        output,
        input_gradient,
        totals[6],
        qkv_grad,
        out_grad,
        totals[7],
        up_grad,
        bias,
        down_grad,
        totals[8],
        ada_grad,
        totals[:6].reshape(6 * width),
    )


def solution(mesh):
    in_specs = (
        P(("dp", "mp"), None),
        P(("dp", "mp"), None),
        P("dp", None),
        P("dp"),
        P(),
        P(None, "mp"),
        P("mp", None),
        P(),
        P(None, "mp"),
        P("mp"),
        P("mp", None),
        P(),
        P(),
        P(),
    )
    out_specs = (
        P(("dp", "mp"), None),
        P(("dp", "mp"), None),
        P(),
        P(None, "mp"),
        P("mp", None),
        P(),
        P(None, "mp"),
        P("mp"),
        P("mp", None),
        P(),
        P(),
        P(),
    )
    return jax.shard_map(
        per_device, mesh=mesh, in_specs=in_specs, out_specs=out_specs, check_vma=False
    )
```

```python
from functools import partial
import math

import jax
import jax.numpy as jnp
from jax import lax
from jax.experimental import pallas as pl
from jax.experimental.pallas import tpu as pltpu
from jax.sharding import PartitionSpec as P

HEAD_DIM = 64
COND = 128
BLOCK = 256
STEP = 128
LANES = 128
BF16 = jnp.bfloat16
F32 = jnp.float32
TANH_SCALE = math.sqrt(2 / math.pi)
TANH_CUBE = 0.044715


def swap(value, axis, bit):
    size = lax.axis_size(axis)
    return lax.ppermute(value, axis, [(i, i ^ bit) for i in range(size)])


def time_features(time, axis, cond_width):
    half_width = cond_width // 2
    dims = (cond_width, 1) if axis == 0 else (1, cond_width)
    place = lax.broadcasted_iota(jnp.int32, dims, axis)
    second = place >= half_width
    ladder = jnp.where(second, place - half_width, place).astype(F32)
    angles = time.astype(F32) * jnp.exp(ladder * (-math.log(10000.0) / half_width))
    waves = jnp.where(second, jnp.sin(angles), jnp.cos(angles))
    return waves / (1.0 + jnp.exp(-waves))


def standard_score_rows(values):
    center = values - jnp.mean(values, axis=-1, keepdims=True)
    inverse_deviation = lax.rsqrt(jnp.mean(center * center, axis=-1, keepdims=True) + 1e-05)
    return (center * inverse_deviation, inverse_deviation)


def norm_reverse_pass(incoming_gradient, centered_scaled, inverse_deviation):
    return inverse_deviation * (
        incoming_gradient
        - jnp.mean(incoming_gradient, axis=-1, keepdims=True)
        - centered_scaled * jnp.mean(incoming_gradient * centered_scaled, axis=-1, keepdims=True)
    )


def dot(a, b):
    return jnp.dot(a, b, preferred_element_type=F32)


def contract_rows(a, b):
    return lax.dot_general(a, b, (((0,), (0,)), ((), ())), preferred_element_type=F32)


def times_transposed(a, b):
    return lax.dot_general(a, b, (((1,), (1,)), ((), ())), preferred_element_type=F32)


def one_line(lines_ref, first, width):
    return jnp.concatenate([lines_ref[first + k : first + k + 1, :] for k in range(width // LANES)], axis=1)


def in_vmem():
    return pl.BlockSpec(memory_space=pltpu.VMEM)


def in_smem():
    return pl.BlockSpec(memory_space=pltpu.SMEM)


def shape(dims, kind):
    return jax.ShapeDtypeStruct(dims, kind)


def cost(micros, size):
    return pl.CostEstimate(flops=int(micros * 1.1e9), bytes_accessed=size, transcendentals=0)


def parameters(mebibytes):
    return pltpu.CompilerParams(vmem_limit_bytes=mebibytes * 2**20)


def anywhere():
    return pl.BlockSpec(memory_space=pl.ANY)


def after(value, *tokens):
    return lax.optimization_barrier((value, *tokens))[0]


def rows_at(index, count):
    return pl.ds(pl.multiple_of(index * count, count), count)


def joined(target, first, second, which):
    half = target.shape[0] // 2
    target[rows_at(which, half), :] = first[:half, :]
    target[rows_at(1 - which, half), :] = second[:half, :]


def window_sizes(slot_length):
    return tuple(range(2 * STEP, slot_length + 1, STEP))


def block_window(lengths_ref, slot, block, slot_length):
    first = block * BLOCK
    last = first + BLOCK - 1
    end = jnp.int32(0)
    low = jnp.int32(0)
    high = jnp.int32(slot_length)
    for document in range(lengths_ref.shape[1]):
        end = end + lengths_ref[slot, document]
        low = jnp.where(end <= first, jnp.maximum(low, end), low)
        high = jnp.where(end > last, jnp.minimum(high, end), high)
    low = lax.div(low, jnp.int32(STEP)) * STEP
    size = jnp.maximum(lax.div(high - low + (STEP - 1), jnp.int32(STEP)) * STEP, 2 * STEP)
    return pl.multiple_of(jnp.minimum(low, slot_length - size), STEP), size


def mask_features(lengths_ref, slot, first, rows):
    documents = lengths_ref.shape[1]
    place = first + lax.broadcasted_iota(jnp.int32, (rows, HEAD_DIM), 0)
    lanes = lax.broadcasted_iota(jnp.int32, (rows, HEAD_DIM), 1)
    segment = jnp.zeros((rows, HEAD_DIM), jnp.int32)
    end = jnp.int32(0)
    for document in range(documents):
        end = end + lengths_ref[slot, document]
        segment = segment + jnp.where(place >= end, 1, 0)
    same = lanes == segment
    one = (lanes >= documents) & (lanes < documents + 3)
    key = jnp.where((lanes < documents) & jnp.logical_not(same), -1e30, jnp.where(one, 1.0, 0.0))
    return key.astype(BF16), jnp.where(same, 1.0, 0.0).astype(BF16)


def three_parts(value, lanes, at):
    first = value.astype(BF16).astype(F32)
    rest = value - first
    second = rest.astype(BF16).astype(F32)
    third = rest - second
    return jnp.where(lanes == at, first, jnp.where(lanes == at + 1, second, jnp.where(lanes == at + 2, third, 0.0)))


def attend_forward_kernel(place_ref, lengths_ref, own_ref, other_ref, *refs, fetched, keep):
    refs = list(refs)
    weight_ref = refs.pop(0)
    if fetched:
        second_ref = refs.pop(0)
    query_ref, key_ref, value_ref, out_ref = refs[:4]
    refs = refs[4:]
    slot = place_ref[3]
    documents = lengths_ref.shape[1]
    if keep:
        kept_ref = refs.pop(0)
    if fetched:
        joined_ref = refs.pop(0)
        joined(joined_ref, weight_ref, second_ref, place_ref[1])
        weight_ref = joined_ref
    rows = own_ref.shape[0]
    length = 2 * rows
    heads = weight_ref.shape[0] // (3 * HEAD_DIM)
    core = place_ref[0]
    lanes = lax.broadcasted_iota(jnp.int32, (rows, HEAD_DIM), 1)
    ones = jnp.where(lanes < 3, 1.0, 0.0).astype(BF16)
    for source, at in ((own_ref, core), (other_ref, 1 - core)):
        here = rows_at(at, rows)
        key_extra, query_extra = mask_features(lengths_ref, slot, at * rows, rows)
        if keep:
            kept_ref[here, :] = source[...]
        qkv = times_transposed(source[...], weight_ref[...]).astype(BF16)
        for head in range(heads):
            at = 3 * HEAD_DIM * head
            query = qkv[:, at : at + HEAD_DIM] * 0.125
            key = qkv[:, at + HEAD_DIM : at + 2 * HEAD_DIM]
            value = qkv[:, at + 2 * HEAD_DIM : at + 3 * HEAD_DIM]
            query_ref[head, here, :] = jnp.concatenate([query, query_extra], axis=1)
            key_ref[head, here, :] = jnp.concatenate([key, key_extra], axis=1)
            value_ref[head, here, :] = jnp.concatenate([value, ones], axis=1)

    def one_block(block, carry):
        here = rows_at(block, BLOCK)
        start, window = block_window(lengths_ref, slot, block, length)
        for size in window_sizes(length):

            @pl.when(window == size)
            def _():
                every = range(heads)
                span = pl.ds(start, size)
                queries = [query_ref[head, here, :] for head in every]
                scores = [times_transposed(queries[head], key_ref[head, span, :]) for head in every]
                highest = [jnp.max(score, axis=1, keepdims=True) for score in scores]
                raised = [jnp.exp(score - most) for score, most in zip(scores, highest)]
                totals = [jnp.sum(value, axis=1, keepdims=True) for value in raised]
                mixed = [
                    dot(raised[head].astype(BF16), value_ref[head, span, :])[:, :HEAD_DIM] / totals[head]
                    for head in every
                ]
                wide = lax.broadcasted_iota(jnp.int32, (BLOCK, LANES), 1)
                for head in every:
                    lse = highest[head] + jnp.log(totals[head])
                    extra = three_parts(lse, wide, HEAD_DIM + documents)
                    query_ref[head, here, :] = (queries[head].astype(F32) - extra).astype(BF16)
                out_ref[here, :] = jnp.concatenate(mixed, axis=1).astype(BF16)

        return carry

    lax.fori_loop(0, length // BLOCK, one_block, 0)


def attend_forward(place, lengths, own, other, weights, keep):
    rows, width = own.shape
    fetched = len(weights) == 2
    columns = weights[0].shape[0] * len(weights)
    heads = columns // (3 * HEAD_DIM)
    length = 2 * rows
    head_wise = shape((heads, length, LANES), BF16)
    outs = [head_wise] * 3 + [shape((length, heads * HEAD_DIM), BF16)]
    if keep:
        outs.append(shape((length, width), BF16))
    return pl.pallas_call(
        partial(attend_forward_kernel, fetched=fetched, keep=keep),
        out_shape=tuple(outs),
        in_specs=[in_smem()] * 2 + [in_vmem()] * (2 + len(weights)),
        out_specs=(in_vmem(),) * len(outs),
        scratch_shapes=[pltpu.VMEM((columns, width), BF16)] if fetched else [],
        compiler_params=parameters(24),
        cost_estimate=cost(9, 2**22),
        name="attend_forward",
    )(place, lengths, own, other, *weights)


def attend_backward_kernel(place_ref, lengths_ref, *refs, first, heads):
    slot = place_ref[3]
    every = range(2 * heads)
    inputs = []
    for side in range(2):
        for head in range(heads):
            arrays = [refs[5 * side + k].at[head] for k in range(3)]
            inputs.append((*arrays, refs[5 * side + 3], refs[5 * side + 4], first + head))
    entry_ref = refs[10]
    outs = refs[11:15]
    key_turned_ref, upstream_ref, sum_ref, query_grad_ref, right_ref = refs[15:]
    length = entry_ref.shape[0]
    lanes = lax.broadcasted_iota(jnp.int32, (length, HEAD_DIM), 1)
    zero = jnp.zeros((length, HEAD_DIM), BF16)
    for item in every:
        query_ref, key_ref, value_ref, mixed_ref, grad_ref, head = inputs[item]
        columns = slice(head * HEAD_DIM, (head + 1) * HEAD_DIM)
        upstream = grad_ref[:, columns]
        inner = jnp.sum(mixed_ref[:, columns].astype(F32) * upstream.astype(F32), axis=1, keepdims=True)
        upstream_ref[item] = jnp.concatenate([upstream, -three_parts(inner, lanes, 0).astype(BF16)], axis=1)
        key_turned_ref[item] = key_ref[:, :HEAD_DIM].T
        right_ref[item, 0] = jnp.concatenate([upstream, zero], axis=1)
        right_ref[item, 1] = jnp.concatenate([zero, query_ref[:, :HEAD_DIM]], axis=1)
    sum_ref[...] = jnp.zeros_like(sum_ref)

    def one_block(block, carry):
        here = rows_at(block, BLOCK)
        start, window = block_window(lengths_ref, slot, block, length)
        for size in window_sizes(length):

            @pl.when(window == size)
            def _():
                span = pl.ds(start, size)
                weights = [jnp.exp(times_transposed(inputs[s][1][span, :], inputs[s][0][here, :])) for s in every]
                raised = [times_transposed(inputs[s][2][span, :], upstream_ref[s, here, :]) for s in every]
                score_grads = [(a * b).astype(BF16) for a, b in zip(weights, raised)]
                for s in every:
                    left = jnp.concatenate([weights[s].astype(BF16), score_grads[s]], axis=1)
                    right = jnp.concatenate([right_ref[s, 0, here, :], right_ref[s, 1, here, :]], axis=0)
                    sum_ref[s, span, :] += dot(left, right)
                turned = [dot(key_turned_ref[s, :, span], score_grads[s]) for s in every]
                turned = (jnp.concatenate(turned, axis=0) * 0.125).T
                for s in every:
                    query_grad_ref[s, here, :] = turned[:, s * HEAD_DIM : (s + 1) * HEAD_DIM].astype(BF16)

        return carry

    lax.fori_loop(0, length // BLOCK, one_block, 0)
    for side in (1, 0):
        for head in range(heads):
            item = side * heads + head
            sums = sum_ref[item]
            grads = jnp.concatenate(
                [query_grad_ref[item], sums[:, HEAD_DIM:].astype(BF16), sums[:, :HEAD_DIM].astype(BF16)], axis=1
            )
            outs[2 * side][head] = grads
            part = 3 * HEAD_DIM
            outs[2 * side + 1][head * part : (head + 1) * part, :] = contract_rows(grads, entry_ref[...]).astype(BF16)


def attend_backward(place, lengths, first, heads, sides, entry):
    length, width = entry.shape
    part = pl.BlockSpec((heads, length, LANES), lambda *_: (first // heads, 0, 0))
    flat = [array for side in sides for array in side]
    outs = [shape((heads, length, 3 * HEAD_DIM), BF16), shape((heads * 3 * HEAD_DIM, width), BF16)] * 2
    count = 2 * heads
    return pl.pallas_call(
        partial(attend_backward_kernel, first=first, heads=heads),
        grid=(1,),
        out_shape=tuple(outs),
        in_specs=[in_smem()] * 2 + ([part] * 3 + [in_vmem()] * 2) * 2 + [in_vmem()],
        out_specs=(in_vmem(),) * len(outs),
        scratch_shapes=[
            pltpu.VMEM((count, HEAD_DIM, length), BF16),
            pltpu.VMEM((count, length, LANES), BF16),
            pltpu.VMEM((count, length, LANES), F32),
            pltpu.VMEM((count, length, HEAD_DIM), BF16),
            pltpu.VMEM((count, 2, length, LANES), BF16),
        ],
        compiler_params=parameters(24),
        cost_estimate=cost(9 * heads, 2**22),
        name="attend_backward",
    )(place, lengths, *flat, entry)


def project_out_kernel(place_ref, mixed_ref, mixed_x_ref, weight_ref, weight_x_ref, own_ref, other_ref):
    rows = own_ref.shape[0]
    for target, at in ((other_ref, 1 - place_ref[0]), (own_ref, place_ref[0])):
        here = rows_at(at, rows)
        total = dot(mixed_ref[here, :], weight_ref[...]) + dot(mixed_x_ref[here, :], weight_x_ref[...])
        target[...] = total.astype(target.dtype)


def project_out(place, mixed, mixed_x, weight, weight_x):
    rows = mixed.shape[0] // 2
    width = weight.shape[1]
    return pl.pallas_call(
        project_out_kernel,
        out_shape=(shape((rows, width), F32), shape((rows, width), BF16)),
        in_specs=[in_smem()] + [in_vmem()] * 4,
        out_specs=(in_vmem(),) * 2,
        compiler_params=parameters(12),
        cost_estimate=cost(2, 2**22),
        name="project_out",
    )(place, mixed, mixed_x, weight, weight_x)


def project_back_kernel(
    place_ref, own_ref, other_ref, mixed_ref, mixed_x_ref, weight_ref, weight_x_ref,
    grad_ref, grad_x_ref, out_ref, out_x_ref, rows_ref,
):
    rows = own_ref.shape[0]
    rows_ref[rows_at(place_ref[0], rows), :] = own_ref[...]
    rows_ref[rows_at(1 - place_ref[0], rows), :] = other_ref[...]
    out_x_ref[...] = contract_rows(mixed_x_ref[...], rows_ref[...]).astype(BF16)
    out_ref[...] = contract_rows(mixed_ref[...], rows_ref[...]).astype(BF16)
    grad_ref[...] = times_transposed(rows_ref[...], weight_ref[...]).astype(BF16)
    grad_x_ref[...] = times_transposed(rows_ref[...], weight_x_ref[...]).astype(BF16)


def project_back(place, own, other, mixed, mixed_x, weight, weight_x):
    rows, width = own.shape
    return pl.pallas_call(
        project_back_kernel,
        out_shape=(shape(mixed.shape, BF16),) * 2 + (shape(weight.shape, BF16),) * 2,
        in_specs=[in_smem()] + [in_vmem()] * 6,
        out_specs=(in_vmem(),) * 4,
        scratch_shapes=[pltpu.VMEM((2 * rows, width), BF16)],
        compiler_params=parameters(14),
        cost_estimate=cost(3, 2**22),
        name="project_back",
    )(place, own, other, mixed, mixed_x, weight, weight_x)


def entry_back_kernel(place_ref, *refs, groups):
    grads = [[ref.at[k] for ref in refs[side * groups : (side + 1) * groups] for k in range(ref.shape[0])] for side in (0, 1)]
    weight_ref, first_ref, second_ref, own_ref, other_ref, joined_ref = refs[2 * groups :]
    rows = own_ref.shape[0]
    joined(joined_ref, first_ref, second_ref, place_ref[1])
    for target, at in ((other_ref, 1 - place_ref[0]), (own_ref, place_ref[0])):
        here = rows_at(at, rows)
        left = jnp.concatenate([grad[here, :] for grad in grads[0]], axis=1)
        left_x = jnp.concatenate([grad[here, :] for grad in grads[1]], axis=1)
        total = dot(left, weight_ref[...]) + dot(left_x, joined_ref[...])
        target[...] = total.astype(target.dtype)


def entry_back(place, grads, grads_x, weight, weights_x):
    rows = grads[0].shape[1] // 2
    width = weight.shape[1]
    groups = len(grads)
    return pl.pallas_call(
        partial(entry_back_kernel, groups=groups),
        out_shape=(shape((rows, width), F32), shape((rows, width), BF16)),
        in_specs=[in_smem()] + [in_vmem()] * (2 * groups + 3),
        out_specs=(in_vmem(),) * 2,
        scratch_shapes=[pltpu.VMEM(weight.shape, BF16)],
        compiler_params=parameters(16),
        cost_estimate=cost(4, 2**22),
        name="entry_back",
    )(place, *grads, *grads_x, weight, *weights_x)


EXTRA_ROWS = 64


def hidden_kernel(place_ref, *refs, fetched, final):
    refs = list(refs)
    entries = refs[:2]
    upstreams = refs[2:4]
    up_ref, down_ref = refs[4:6]
    refs = refs[6:]
    if fetched:
        up_second_ref, down_second_ref = refs[:2]
        refs = refs[2:]
    bias_ref = refs.pop(0)
    if final:
        base_out, base_grad = refs[:2], refs[2:4]
        refs = refs[4:]
    outs, grads = refs[:2], refs[2:4]
    up_sum_ref, kept_ref, sent_ref, hidden_ref, pre_grad_ref, down_sum_ref = refs[4:10]
    refs = refs[10:]
    if fetched:
        joined(refs[0], up_ref, up_second_ref, place_ref[1])
        joined(refs[1], down_ref, down_second_ref, place_ref[1])
        up_ref, down_ref = refs[:2]
    rows, width = entries[0].shape
    units = up_ref.shape[1]
    up_sum_ref[width:, :] = jnp.zeros((EXTRA_ROWS, units), BF16)
    bias_sum = [jnp.zeros((1, BLOCK), F32) for _ in range(units // BLOCK)]
    bias = one_line(bias_ref, 0, units).astype(F32)
    for part in range(2):

        def tile(step, carry, part=part):
            here = rows_at(step, BLOCK)
            there = pl.ds(pl.multiple_of(part * rows + step * BLOCK, BLOCK), BLOCK)
            entry = entries[part][here, :]
            upstream = upstreams[part][here, :]
            carry = list(carry)
            for block in range(units // BLOCK):
                cut = slice(block * BLOCK, (block + 1) * BLOCK)
                pre = dot(entry, up_ref[:, cut]) + bias[:, cut]
                hidden_grad = times_transposed(upstream, down_ref[cut, :])
                square = pre * pre
                half = 0.5 + 0.5 * jnp.tanh(pre * (TANH_SCALE + (TANH_SCALE * TANH_CUBE) * square))
                hidden = pre * half
                slope = half + (hidden - hidden * half) * (2 * TANH_SCALE + (6 * TANH_SCALE * TANH_CUBE) * square)
                pre_grad = (hidden_grad * slope).astype(BF16)
                hidden_ref[there, cut] = hidden.astype(BF16)
                pre_grad_ref[there, cut] = pre_grad
                carry[block] = carry[block] + jnp.sum(pre_grad.astype(F32), axis=0, keepdims=True)
            return tuple(carry)

        bias_sum = lax.fori_loop(0, rows // BLOCK, tile, tuple(bias_sum))
    for block in range(units // BLOCK):
        up_sum_ref[width : width + 1, block * BLOCK : (block + 1) * BLOCK] = bias_sum[block].astype(BF16)
    for part in (1, 0):

        def back(step, carry, part=part):
            here = rows_at(step, BLOCK)
            there = pl.ds(pl.multiple_of(part * rows + step * BLOCK, BLOCK), BLOCK)
            grad = times_transposed(pre_grad_ref[there, :], up_ref[...])
            out = dot(hidden_ref[there, :], down_ref[...])
            if final:
                grad = grad + base_grad[part][here, :]
                out = out + base_out[part][here, :]
            grads[part][here, :] = grad.astype(grads[part].dtype)
            outs[part][here, :] = out.astype(outs[part].dtype)
            return carry

        lax.fori_loop(0, rows // BLOCK, back, 0)
    for block in range(units // BLOCK):
        cut = slice(block * BLOCK, (block + 1) * BLOCK)
        up_sum = contract_rows(entries[0][...], pre_grad_ref[:rows, cut]) + contract_rows(entries[1][...], pre_grad_ref[rows:, cut])
        up_sum_ref[:width, cut] = up_sum.astype(BF16)
        down_sum = contract_rows(hidden_ref[:rows, cut], upstreams[0][...]) + contract_rows(hidden_ref[rows:, cut], upstreams[1][...])
        down_sum_ref[cut, :] = down_sum.astype(BF16)
    half = units // 2
    kept_ref[...] = down_sum_ref[rows_at(place_ref[1], half), :]
    sent_ref[...] = down_sum_ref[rows_at(1 - place_ref[1], half), :]


def hidden_part(place, entries, upstreams, weights, bias, base):
    rows, width = entries[0].shape
    units = bias.shape[0] * LANES
    fetched = len(weights) == 4
    final = base is not None
    second = BF16 if final else F32
    partial_rows = (shape((rows, width), F32), shape((rows, width), second))
    inputs = [*entries, *upstreams, *weights, bias, *(base or ())]
    scratch = [pltpu.VMEM((2 * rows, units), BF16)] * 2 + [pltpu.VMEM((units, width), BF16)]
    if fetched:
        scratch += [pltpu.VMEM((width, units), BF16), pltpu.VMEM((units, width), BF16)]
    return pl.pallas_call(
        partial(hidden_kernel, fetched=fetched, final=final),
        out_shape=partial_rows * 2 + (shape((width + EXTRA_ROWS, units), BF16),) + (shape((units // 2, width), BF16),) * 2,
        in_specs=[in_smem()] + [in_vmem()] * len(inputs),
        out_specs=(in_vmem(),) * 7,
        scratch_shapes=scratch,
        compiler_params=parameters(32),
        cost_estimate=cost(12, 2**23),
        name="hidden_part",
    )(place, *inputs)


ROWS = 128


def row_wise(body, name, row_inputs, whole_inputs, row_outs, sums, micros):
    rows, width = row_inputs[0].shape
    block = pl.BlockSpec((ROWS, width), lambda i: (i, 0))
    whole = [pl.BlockSpec(array.shape, lambda i: (0, 0)) for array in whole_inputs]
    outs = [shape((rows, width), kind) for kind in row_outs]
    out_specs = [block] * len(outs)
    if sums:
        outs.append(shape((8, width), F32))
        out_specs.append(pl.BlockSpec((8, width), lambda i: (0, 0)))

    def kernel(*refs):
        refs = list(refs)
        row_refs = [refs.pop(0) for _ in row_inputs]
        whole_refs = [refs.pop(0) for _ in whole_inputs]
        results, terms = body(*[ref[...] for ref in row_refs], *whole_refs)
        for ref, result in zip(refs, results):
            ref[...] = result.astype(ref.dtype)
        if sums:
            total = jnp.concatenate(
                [jnp.sum(term, axis=0, keepdims=True) for term in terms] + [jnp.zeros((8 - sums, width), F32)], axis=0
            )
            first = pl.program_id(0) == 0

            @pl.when(first)
            def _():
                refs[-1][...] = total

            @pl.when(jnp.logical_not(first))
            def _():
                refs[-1][...] += total

    return pl.pallas_call(
        kernel,
        grid=(rows // ROWS,),
        out_shape=tuple(outs),
        in_specs=[block] * len(row_inputs) + whole,
        out_specs=tuple(out_specs),
        compiler_params=parameters(12),
        cost_estimate=cost(micros, 2**20),
        name=name,
    )(*row_inputs, *whole_inputs)


def enter_kernel(place_ref, time_ref, tokens_ref, cotangent_ref, weight_ref, *refs):
    vectors, (table_ref, entry_ref, grad_ref) = refs[:-3], refs[-3:]
    rows, width = tokens_ref.shape
    table_ref[...] = jnp.zeros_like(table_ref)
    row = 0
    for vector in vectors:
        for at in range(0, vector.shape[0], width // LANES):
            table_ref[row : row + 1, :] = one_line(vector, at, width)
            row += 1
    features = time_features(time_ref[place_ref[3]], 0, COND)
    for piece in range(6):
        cut = slice(piece * width, (piece + 1) * width)
        table_ref[piece : piece + 1, :] += jnp.sum(features * weight_ref[:, cut], axis=0, keepdims=True)
    table_ref[row : row + 1, :COND] = time_features(time_ref[place_ref[3]], 1, COND)
    table = table_ref[...]

    def tile(step, carry):
        here = rows_at(step, ROWS)
        scored, _ = standard_score_rows(tokens_ref[here, :].astype(F32))
        entry = scored * table[6:7] * (1.0 + table[1:2]) + table[0:1]
        entry_ref[here, :] = entry.astype(BF16)
        grad_ref[here, :] = (table[5:6] * cotangent_ref[here, :].astype(F32)).astype(BF16)
        return carry

    lax.fori_loop(0, rows // ROWS, tile, 0)


def enter(place, time_index, tokens, cotangent, weight, vectors):
    vectors = [vector.reshape(-1, LANES) for vector in vectors]
    rows, width = tokens.shape
    return pl.pallas_call(
        enter_kernel,
        out_shape=(shape((16, width), F32), shape((rows, width), BF16), shape((rows, width), BF16)),
        in_specs=[in_smem()] * 2 + [in_vmem()] * (3 + len(vectors)),
        out_specs=(in_vmem(),) * 3,
        compiler_params=parameters(14),
        cost_estimate=cost(4, 2**22),
        name="enter",
    )(place, time_index, tokens, cotangent, weight, *vectors)


def enter_second(tokens, branch_own, branch_other, modulation):
    branch = branch_own + branch_other.astype(F32)
    middle = tokens.astype(F32) + modulation[2:3, :] * branch
    scored, _ = standard_score_rows(middle)
    entry = scored * modulation[7:8, :] * (1.0 + modulation[4:5, :]) + modulation[3:4, :]
    return (middle, entry), ()


def leave(middle, cotangent, out_own, out_other, modulation):
    branch = out_own + out_other.astype(F32) + modulation[8:9, :]
    incoming = cotangent.astype(F32)
    branch_grad = (modulation[5:6, :] * incoming).astype(BF16).astype(F32)
    return (middle + modulation[5:6, :] * branch,), (incoming * branch, branch_grad)


def back_second(middle, cotangent, grad_own, grad_other, branch_own, branch_other, modulation):
    gain = modulation[7:8, :]
    scored, inverse = standard_score_rows(middle)
    entry_grad = grad_own + grad_other.astype(F32)
    normed_grad = entry_grad * (1.0 + modulation[4:5, :])
    middle_grad = cotangent.astype(F32) + norm_reverse_pass(normed_grad * gain, scored, inverse)
    branch = branch_own + branch_other.astype(F32)
    terms = (middle_grad * branch, entry_grad, entry_grad * (scored * gain), normed_grad * scored)
    return (modulation[2:3, :] * middle_grad, middle_grad), terms


def back_first(tokens, grad_own, grad_other, middle_grad, modulation):
    gain = modulation[6:7, :]
    scored, inverse = standard_score_rows(tokens.astype(F32))
    entry_grad = grad_own + grad_other.astype(F32)
    normed_grad = entry_grad * (1.0 + modulation[1:2, :])
    grad = middle_grad + norm_reverse_pass(normed_grad * gain, scored, inverse)
    return (grad,), (entry_grad, entry_grad * (scored * gain), normed_grad * scored)


def sum_kernel(place_ref, a_ref, b_ref, *refs, pieces):
    a_rows = a_ref.shape[0] // pieces
    if pieces == 4:
        mine = place_ref[1] * 2 + place_ref[2]
        order = [mine, lax.rem(mine + 2, 4), mine + 1 - 2 * place_ref[2], 3 - mine]
    elif pieces == 2:
        order = [place_ref[2], 1 - place_ref[2]]
    else:
        order = [0]
    for out, index in zip(refs, order):
        here = rows_at(index, a_rows) if pieces > 1 else slice(None)
        out[...] = (a_ref[here, :].astype(F32) + b_ref[here, :].astype(F32)).astype(BF16)


def summed(place, a, b, pieces):
    rows, width = a.shape
    outs = (shape((rows // pieces, width), BF16),) * pieces
    return pl.pallas_call(
        partial(sum_kernel, pieces=pieces),
        out_shape=outs,
        in_specs=[in_smem(), in_vmem(), in_vmem()],
        out_specs=(in_vmem(),) * pieces,
        compiler_params=parameters(8),
        cost_estimate=cost(1.5, 2**20),
        name="summed",
    )(place, a, b)


def total_kernel(*refs):
    total = refs[0][...].astype(F32)
    for ref in refs[1:-1]:
        total = total + ref[...].astype(F32)
    refs[-1][...] = total.astype(BF16)


def total_of(*parts):
    return pl.pallas_call(
        total_kernel,
        out_shape=shape(parts[0].shape, BF16),
        in_specs=[in_vmem()] * len(parts),
        out_specs=in_vmem(),
        compiler_params=parameters(8),
        cost_estimate=cost(0.7, 2**19),
        name="total_of",
    )(*parts)


def lay_kernel(place_ref, *refs):
    rows = refs[0].shape[0]
    mine = place_ref[1] * 2 + place_ref[2]
    order = [mine, lax.rem(mine + 2, 4), mine + 1 - 2 * place_ref[2], 3 - mine]
    for ref, index in zip(refs, order):
        refs[-1][rows_at(index, rows), :] = ref[...].astype(F32)


def lay(place, parts):
    rows, width = parts[0].shape
    return pl.pallas_call(
        lay_kernel,
        out_shape=shape((4 * rows, width), F32),
        in_specs=[in_smem()] + [in_vmem()] * 4,
        out_specs=in_vmem(),
        compiler_params=parameters(8),
        cost_estimate=cost(2, 2**20),
        name="lay",
    )(place, *parts)


def dp_bits():
    bits = []
    bit = 1
    while bit < lax.axis_size("dp"):
        bits.append(bit)
        bit *= 2
    return bits


def beyond(value):
    for bit in dp_bits()[2:]:
        value = total_of(value, swap(value, "dp", bit))
    return value


def around(value):
    return [swap(value, "dp", bit) for bit in (1, 2, 3)]


def scatter_four(pieces):
    return total_of(pieces[0], *[swap(piece, "dp", bit) for piece, bit in zip(pieces[1:], (1, 2, 3))])


def give_back(place, value):
    return lay(place, [value, *around(value)])


def laid(own, other, mine):
    return jnp.where(mine == 0, jnp.concatenate([own, other], axis=0), jnp.concatenate([other, own], axis=0))


def gather_small(value):
    for axis, bit in [("mp", 2)] + [("dp", bit) for bit in dp_bits()]:
        value = laid(value, swap(value, axis, bit), (lax.axis_index(axis) // bit) % 2)
    return value


def per_device(
    tokens,
    cotangent,
    doc_lengths,
    time_index,
    attention_norm_gain,
    qkv_weight,
    out_weight,
    feedforward_norm_gain,
    up_weight,
    up_bias,
    down_weight,
    down_bias,
    ada_weight,
    ada_bias,
):
    rows, width = tokens.shape
    core = lax.axis_index("mp") % 2
    slot = lax.axis_index("mp") // 2
    index = lax.axis_index("dp")
    side = index % 2
    place = jnp.stack([core, side, index // 2 % 2, slot]).astype(jnp.int32)

    def near(value):
        return swap(value, "mp", 1)

    def across(value):
        return swap(value, "mp", 2)

    def half_of(weight):
        half = weight.shape[0] // 2
        return lax.dynamic_slice_in_dim(weight, side * half, half, 0)

    def relay(piece):
        return swap(piece, "dp", 1)

    qkv_turned = qkv_weight.T
    qkv_a = across(half_of(qkv_turned))
    table, entry_one, branch_grad = enter(
        place,
        time_index,
        tokens,
        cotangent,
        ada_weight,
        (ada_bias, attention_norm_gain, feedforward_norm_gain, down_bias),
    )
    entry_one_near = near(entry_one)
    out_weight_x = across(after(out_weight, entry_one))
    up_bias_x = across(after(up_bias, entry_one))
    branch_grads = (branch_grad, near(branch_grad))
    qkv_b = relay(qkv_a)
    up_half = half_of(after(up_weight, qkv_a))
    down_half = half_of(after(down_weight, qkv_a))
    up_a = across(up_half)
    down_a = across(down_half)

    query, key, value, mixture, entry_one_all = attend_forward(
        place, doc_lengths, entry_one, after(entry_one_near, up_half, down_half), (qkv_turned,), True
    )
    query_x, key_x, value_x, mixture_x = attend_forward(
        place, doc_lengths, entry_one, after(entry_one_near, mixture), (qkv_a, qkv_b), False
    )
    branch_own, branch_other = project_out(place, mixture, after(mixture_x, up_a), out_weight, out_weight_x)
    up_b = relay(after(up_a, mixture_x))
    branch_other = near(branch_other)
    middle, entry_two = row_wise(
        enter_second, "enter_second", (tokens, branch_own, branch_other), (table,), (F32, BF16), 0, 3
    )
    down_b = relay(after(down_a, entry_two))
    entries_two = (entry_two, after(near(entry_two), down_a))

    lines = (-1, LANES)
    *base, up_own, down_kept, down_sent = hidden_part(
        place, entries_two, branch_grads, (up_weight, down_weight), up_bias.reshape(lines), None
    )
    down_got = swap(down_sent, "dp", 1)
    out_own, out_other, grad_own, grad_other, up_x, down_kept_x, down_sent_x = hidden_part(
        place, entries_two, branch_grads, (up_a, down_a, up_b, down_b), up_bias_x.reshape(lines), base
    )
    up_got = across(up_x)
    down_got_x = swap(down_sent_x, "dp", 1)
    attn_grad, middle_grad, sums_two = row_wise(
        back_second,
        "back_second",
        (middle, cotangent, grad_own, near(grad_other), branch_own, branch_other),
        (table,),
        (BF16, F32),
        4,
        4,
    )
    out_other = near(after(out_other, attn_grad))
    mixture_grad, mixture_grad_x, out_sum, out_sum_x = project_back(
        place, attn_grad, near(attn_grad), mixture, mixture_x, out_weight, out_weight_x
    )

    heads = qkv_weight.shape[1] // (3 * HEAD_DIM)
    back, back_x, head_sums, head_gots = [], [], [], []
    token = mixture_grad
    for head in range(heads):
        sides = ((query, key, value, mixture, mixture_grad), (query_x, key_x, value_x, mixture_x, mixture_grad_x))
        grad, grad_sum, grad_x, grad_sum_x = attend_backward(
            place, doc_lengths, head, 1, sides, after(entry_one_all, token)
        )
        back.append(grad)
        back_x.append(grad_x)
        if head == 0:
            grad_sum = jnp.concatenate([out_sum, grad_sum], axis=0)
            grad_sum_x = jnp.concatenate([out_sum_x, grad_sum_x], axis=0)
        head_sums.append(grad_sum)
        head_gots.append(across(grad_sum_x))
        token = grad
        if head == 0:
            down_part = total_of(after(down_kept, grad), down_got)
            down_part_x = total_of(after(down_kept_x, grad), down_got_x)
            down_part_got = across(down_part_x)
            token = down_part_x
        if head == 1:
            up_pieces = summed(place, up_own, after(up_got, grad), 4)
            token = up_pieces[0]
    first_own, first_other = entry_back(place, back, back_x, qkv_turned, (qkv_a, qkv_b))
    down_kept, down_sent = summed(place, down_part, after(down_part_got, first_own), 2)
    input_gradient, sums_one = row_wise(
        back_first, "back_first", (tokens, first_own, near(first_other), middle_grad), (table,), (F32,), 3, 3
    )
    output, sums_out = row_wise(
        leave, "leave", (middle, cotangent, out_own, out_other), (table,), (BF16,), 2, 3
    )
    column_sums = jnp.concatenate(
        [sums_one[:2], sums_two[:3], sums_out[:1], sums_one[2:3], sums_two[3:4], sums_out[1:2]], axis=0
    )
    column_sums = column_sums + near(column_sums)
    sums = gather_small(jnp.concatenate([column_sums, table[9:10]], axis=0)[None])

    up_grad = give_back(place, beyond(scatter_four(up_pieces)))
    down_grad = give_back(place, beyond(total_of(down_kept, swap(down_sent, "dp", 2))))
    totals_qkv = [
        give_back(place, beyond(scatter_four(summed(place, own, after(got, first_own), 4))))
        for own, got in zip(head_sums, head_gots)
    ]
    out_rows = out_weight.shape[0]
    qkv_grad = jnp.concatenate([totals_qkv[0][out_rows:], *totals_qkv[1:]], axis=0).T

    slots = sums.shape[0]
    modulation_grad = sums[:, :6].reshape(slots, 6 * width)
    ada_grad = lax.dot_general(
        sums[:, 9, :COND], modulation_grad, (((0,), (0,)), ((), ())), precision=lax.Precision.HIGHEST, preferred_element_type=F32
    )
    totals = jnp.sum(sums[:, :9], axis=0)
    return (
        output,
        input_gradient,
        totals[6],
        qkv_grad,
        totals_qkv[0][:out_rows],
        totals[7],
        up_grad[:width],
        up_grad[width],
        down_grad,
        totals[8],
        ada_grad,
        totals[:6].reshape(6 * width),
    )


def solution(mesh):
    in_specs = (
        P(("dp", "mp"), None),
        P(("dp", "mp"), None),
        P("dp", None),
        P("dp"),
        P(),
        P(None, "mp"),
        P("mp", None),
        P(),
        P(None, "mp"),
        P("mp"),
        P("mp", None),
        P(),
        P(),
        P(),
    )
    out_specs = (
        P(("dp", "mp"), None),
        P(("dp", "mp"), None),
        P(),
        P(None, "mp"),
        P("mp", None),
        P(),
        P(None, "mp"),
        P("mp"),
        P("mp", None),
        P(),
        P(),
        P(),
    )
    return jax.shard_map(
        per_device, mesh=mesh, in_specs=in_specs, out_specs=out_specs, check_vma=False
    )
```

```python
from functools import partial
import math

import jax
import jax.numpy as jnp
from jax import lax
from jax.experimental import pallas as pl
from jax.experimental.pallas import tpu as pltpu
from jax.sharding import PartitionSpec as P

HEAD_DIM = 64
COND = 128
BLOCK = 256
STEP = 128
LANES = 128
BF16 = jnp.bfloat16
F32 = jnp.float32
TANH_SCALE = math.sqrt(2 / math.pi)
TANH_CUBE = 0.044715


def swap(value, axis, bit):
    size = lax.axis_size(axis)
    return lax.ppermute(value, axis, [(i, i ^ bit) for i in range(size)])


def time_features(time, axis, cond_width):
    half_width = cond_width // 2
    dims = (cond_width, 1) if axis == 0 else (1, cond_width)
    place = lax.broadcasted_iota(jnp.int32, dims, axis)
    second = place >= half_width
    ladder = jnp.where(second, place - half_width, place).astype(F32)
    angles = time.astype(F32) * jnp.exp(ladder * (-math.log(10000.0) / half_width))
    waves = jnp.where(second, jnp.sin(angles), jnp.cos(angles))
    return waves / (1.0 + jnp.exp(-waves))


def standard_score_rows(values):
    center = values - jnp.mean(values, axis=-1, keepdims=True)
    inverse_deviation = lax.rsqrt(jnp.mean(center * center, axis=-1, keepdims=True) + 1e-05)
    return (center * inverse_deviation, inverse_deviation)


def norm_reverse_pass(incoming_gradient, centered_scaled, inverse_deviation):
    return inverse_deviation * (
        incoming_gradient
        - jnp.mean(incoming_gradient, axis=-1, keepdims=True)
        - centered_scaled * jnp.mean(incoming_gradient * centered_scaled, axis=-1, keepdims=True)
    )


def dot(a, b):
    return jnp.dot(a, b, preferred_element_type=F32)


def contract_rows(a, b):
    return lax.dot_general(a, b, (((0,), (0,)), ((), ())), preferred_element_type=F32)


def times_transposed(a, b):
    return lax.dot_general(a, b, (((1,), (1,)), ((), ())), preferred_element_type=F32)


def one_line(lines_ref, first, width):
    return jnp.concatenate([lines_ref[first + k : first + k + 1, :] for k in range(width // LANES)], axis=1)


def in_vmem():
    return pl.BlockSpec(memory_space=pltpu.VMEM)


def in_smem():
    return pl.BlockSpec(memory_space=pltpu.SMEM)


def in_hbm(value):
    return pltpu.with_memory_space_constraint(value, pltpu.HBM)


def kept(dims, kind):
    return pltpu.VMEM(dims, kind)


def shape(dims, kind):
    return jax.ShapeDtypeStruct(dims, kind)


def cost(micros, size):
    return pl.CostEstimate(flops=int((micros + 12) * 1.1e9), bytes_accessed=size, transcendentals=0)


def parameters(mebibytes):
    return pltpu.CompilerParams(vmem_limit_bytes=mebibytes * 2**20)


def anywhere():
    return pl.BlockSpec(memory_space=pl.ANY)


def after(value, *tokens):
    return lax.optimization_barrier((value, *tokens))[0]


def rows_at(index, count):
    return pl.ds(pl.multiple_of(index * count, count), count)


def joined(target, pieces, mine, direct=0):
    rows = (target.shape[0] - direct) // 2
    for piece, index in zip(pieces, (mine, 1 - mine)):
        target[rows_at(index, rows), :] = piece[:rows, :]
    if direct:
        target[2 * rows :, :] = pieces[2][...]


def window_sizes(slot_length):
    return tuple(range(2 * STEP, slot_length + 1, STEP))


def block_window(lengths_ref, slot, block, slot_length):
    first = block * BLOCK
    last = first + BLOCK - 1
    end = jnp.int32(0)
    low = jnp.int32(0)
    high = jnp.int32(slot_length)
    for document in range(lengths_ref.shape[1]):
        end = end + lengths_ref[slot, document]
        low = jnp.where(end <= first, jnp.maximum(low, end), low)
        high = jnp.where(end > last, jnp.minimum(high, end), high)
    low = lax.div(low, jnp.int32(STEP)) * STEP
    size = jnp.maximum(lax.div(high - low + (STEP - 1), jnp.int32(STEP)) * STEP, 2 * STEP)
    return pl.multiple_of(jnp.minimum(low, slot_length - size), STEP), size


def mask_features(lengths_ref, slot, first, rows):
    documents = lengths_ref.shape[1]
    place = first + lax.broadcasted_iota(jnp.int32, (rows, HEAD_DIM), 0)
    lanes = lax.broadcasted_iota(jnp.int32, (rows, HEAD_DIM), 1)
    segment = jnp.zeros((rows, HEAD_DIM), jnp.int32)
    end = jnp.int32(0)
    for document in range(documents):
        end = end + lengths_ref[slot, document]
        segment = segment + jnp.where(place >= end, 1, 0)
    same = lanes == segment
    one = (lanes >= documents) & (lanes < documents + 3)
    key = jnp.where((lanes < documents) & jnp.logical_not(same), -1e30, jnp.where(one, 1.0, 0.0))
    return key.astype(BF16), jnp.where(same, 1.0, 0.0).astype(BF16)


def three_parts(value, lanes, at):
    first = value.astype(BF16).astype(F32)
    rest = value - first
    second = rest.astype(BF16).astype(F32)
    third = rest - second
    return jnp.where(lanes == at, first, jnp.where(lanes == at + 1, second, jnp.where(lanes == at + 2, third, 0.0)))


def attend_forward_kernel(place_ref, lengths_ref, own_ref, other_ref, *refs, fetched, keep):
    refs = list(refs)
    weight_refs = [refs.pop(0) for _ in range(2 if fetched else 1)]
    weight_ref = weight_refs[0]
    query_ref, key_ref, value_ref, out_ref = refs[:4]
    refs = refs[4:]
    slot = place_ref[3]
    documents = lengths_ref.shape[1]
    if keep:
        kept_ref = refs.pop(0)
    if fetched:
        joined_ref = refs.pop(0)
        joined(joined_ref, weight_refs, place_ref[1])
        weight_ref = joined_ref
    rows = own_ref.shape[0] // 2
    length = 2 * rows
    heads = weight_ref.shape[0] // (3 * HEAD_DIM)
    core = place_ref[0]
    lanes = lax.broadcasted_iota(jnp.int32, (rows, HEAD_DIM), 1)
    ones = jnp.where(lanes < 3, 1.0, 0.0).astype(BF16)
    for source, at in ((own_ref, core), (other_ref, 1 - core)):
        here = rows_at(at, rows)
        key_extra, query_extra = mask_features(lengths_ref, slot, at * rows, rows)
        if keep:
            kept_ref[here, :] = source[:rows, :]
        qkv = times_transposed(source[:rows, :], weight_ref[...]).astype(BF16)
        for head in range(heads):
            at = 3 * HEAD_DIM * head
            query = qkv[:, at : at + HEAD_DIM] * 0.125
            key = qkv[:, at + HEAD_DIM : at + 2 * HEAD_DIM]
            value = qkv[:, at + 2 * HEAD_DIM : at + 3 * HEAD_DIM]
            query_ref[head, here, :] = jnp.concatenate([query, query_extra], axis=1)
            key_ref[head, here, :] = jnp.concatenate([key, key_extra], axis=1)
            value_ref[head, here, :] = jnp.concatenate([value, ones], axis=1)

    def one_block(block, carry):
        here = rows_at(block, BLOCK)
        start, window = block_window(lengths_ref, slot, block, length)
        for size in window_sizes(length):

            @pl.when(window == size)
            def _():
                every = range(heads)
                span = pl.ds(start, size)
                queries = [query_ref[head, here, :] for head in every]
                scores = [times_transposed(queries[head], key_ref[head, span, :]) for head in every]
                highest = [jnp.max(score, axis=1, keepdims=True) for score in scores]
                raised = [jnp.exp(score - most) for score, most in zip(scores, highest)]
                totals = [jnp.sum(value, axis=1, keepdims=True) for value in raised]
                mixed = [
                    dot(raised[head].astype(BF16), value_ref[head, span, :])[:, :HEAD_DIM] / totals[head]
                    for head in every
                ]
                wide = lax.broadcasted_iota(jnp.int32, (BLOCK, LANES), 1)
                for head in every:
                    lse = highest[head] + jnp.log(totals[head])
                    extra = three_parts(lse, wide, HEAD_DIM + documents)
                    query_ref[head, here, :] = (queries[head].astype(F32) - extra).astype(BF16)
                out_ref[here, :] = jnp.concatenate(mixed, axis=1).astype(BF16)

        return carry

    lax.fori_loop(0, length // BLOCK, one_block, 0)


def attend_forward(place, lengths, own, other, weights, keep):
    length, width = own.shape
    fetched = len(weights) == 2
    columns = weights[0].shape[0] * len(weights)
    heads = columns // (3 * HEAD_DIM)
    head_wise = kept((heads, length, LANES), BF16)
    outs = [head_wise] * 3 + [kept((length, heads * HEAD_DIM), BF16)]
    if keep:
        outs.append(kept((length, width), BF16))
    return pl.pallas_call(
        partial(attend_forward_kernel, fetched=fetched, keep=keep),
        out_shape=tuple(outs),
        in_specs=[in_smem()] * 2 + [in_vmem()] * (2 + len(weights)),
        out_specs=(in_vmem(),) * len(outs),
        scratch_shapes=[pltpu.VMEM((columns, width), BF16)] if fetched else [],
        compiler_params=parameters(24),
        cost_estimate=cost(9, 2**22),
        name="attend_forward",
    )(place, lengths, own, other, *weights)


def attend_backward_kernel(place_ref, lengths_ref, *refs, first, heads, extra):
    slot = place_ref[3]
    every = range(2 * heads)
    inputs = []
    for side in range(2):
        for head in range(heads):
            arrays = [refs[5 * side + k].at[first + head] for k in range(3)]
            inputs.append((*arrays, refs[5 * side + 3], refs[5 * side + 4], first + head))
    entry_ref = refs[10]
    refs = refs[11:]
    if extra:
        extras = refs[:2]
        refs = refs[2:]
        for side in range(2):
            refs[2 * side + 1][:extra, :] = extras[side][...]
    outs = refs[:4]
    key_turned_ref, upstream_ref, sum_ref, query_grad_ref, right_ref = refs[4:]
    length = entry_ref.shape[0]
    lanes = lax.broadcasted_iota(jnp.int32, (length, HEAD_DIM), 1)
    zero = jnp.zeros((length, HEAD_DIM), BF16)
    for item in every:
        query_ref, key_ref, value_ref, mixed_ref, grad_ref, head = inputs[item]
        columns = slice(head * HEAD_DIM, (head + 1) * HEAD_DIM)
        upstream = grad_ref[:, columns]
        inner = jnp.sum(mixed_ref[:, columns].astype(F32) * upstream.astype(F32), axis=1, keepdims=True)
        upstream_ref[item] = jnp.concatenate([upstream, -three_parts(inner, lanes, 0).astype(BF16)], axis=1)
        key_turned_ref[item] = key_ref[:, :HEAD_DIM].T
        right_ref[item, 0] = jnp.concatenate([upstream, zero], axis=1)
        right_ref[item, 1] = jnp.concatenate([zero, query_ref[:, :HEAD_DIM]], axis=1)
    sum_ref[...] = jnp.zeros_like(sum_ref)

    def one_block(block, carry):
        here = rows_at(block, BLOCK)
        start, window = block_window(lengths_ref, slot, block, length)
        for size in window_sizes(length):

            @pl.when(window == size)
            def _():
                span = pl.ds(start, size)
                weights = [jnp.exp(times_transposed(inputs[s][1][span, :], inputs[s][0][here, :])) for s in every]
                raised = [times_transposed(inputs[s][2][span, :], upstream_ref[s, here, :]) for s in every]
                score_grads = [(a * b).astype(BF16) for a, b in zip(weights, raised)]
                for s in every:
                    left = jnp.concatenate([weights[s].astype(BF16), score_grads[s]], axis=1)
                    right = jnp.concatenate([right_ref[s, 0, here, :], right_ref[s, 1, here, :]], axis=0)
                    sum_ref[s, span, :] += dot(left, right)
                turned = [dot(key_turned_ref[s, :, span], score_grads[s]) for s in every]
                turned = (jnp.concatenate(turned, axis=0) * 0.125).T
                for s in every:
                    query_grad_ref[s, here, :] = turned[:, s * HEAD_DIM : (s + 1) * HEAD_DIM].astype(BF16)

        return carry

    lax.fori_loop(0, length // BLOCK, one_block, 0)
    for side in (1, 0):
        for head in range(heads):
            item = side * heads + head
            sums = sum_ref[item]
            grads = jnp.concatenate(
                [query_grad_ref[item], sums[:, HEAD_DIM:].astype(BF16), sums[:, :HEAD_DIM].astype(BF16)], axis=1
            )
            outs[2 * side][head] = grads
            part = 3 * HEAD_DIM
            outs[2 * side + 1][extra + head * part : extra + (head + 1) * part, :] = contract_rows(grads, entry_ref[...]).astype(BF16)


def attend_backward(place, lengths, first, heads, sides, entry, extras):
    extra = extras[0].shape[0] if extras else 0
    length, width = entry.shape
    flat = [array for side in sides for array in side]
    outs = [shape((heads, length, 3 * HEAD_DIM), BF16), shape((extra + heads * 3 * HEAD_DIM, width), BF16)] * 2
    count = 2 * heads
    return pl.pallas_call(
        partial(attend_backward_kernel, first=first, heads=heads, extra=extra),
        out_shape=tuple(outs),
        in_specs=[in_smem()] * 2 + [in_vmem()] * (11 + len(extras)),
        out_specs=(in_vmem(),) * len(outs),
        scratch_shapes=[
            pltpu.VMEM((count, HEAD_DIM, length), BF16),
            pltpu.VMEM((count, length, LANES), BF16),
            pltpu.VMEM((count, length, LANES), F32),
            pltpu.VMEM((count, length, HEAD_DIM), BF16),
            pltpu.VMEM((count, 2, length, LANES), BF16),
        ],
        compiler_params=parameters(24),
        cost_estimate=cost(9 * heads, 2**22),
        name="attend_backward",
    )(place, lengths, *flat, entry, *extras)


def project_out_kernel(place_ref, mixed_ref, mixed_x_ref, weight_ref, weight_x_ref, own_ref, other_ref):
    rows = own_ref.shape[0]
    for target, at in ((other_ref, 1 - place_ref[0]), (own_ref, place_ref[0])):
        here = rows_at(at, rows)
        total = dot(mixed_ref[here, :], weight_ref[...]) + dot(mixed_x_ref[here, :], weight_x_ref[...])
        target[...] = total.astype(target.dtype)


def project_out(place, mixed, mixed_x, weight, weight_x):
    rows = mixed.shape[0] // 2
    width = weight.shape[1]
    return pl.pallas_call(
        project_out_kernel,
        out_shape=(shape((rows, width), F32), shape((rows, width), BF16)),
        in_specs=[in_smem()] + [in_vmem()] * 4,
        out_specs=(in_vmem(),) * 2,
        compiler_params=parameters(12),
        cost_estimate=cost(2, 2**22),
        name="project_out",
    )(place, mixed, mixed_x, weight, weight_x)


def project_back_kernel(
    place_ref, own_ref, other_ref, mixed_ref, mixed_x_ref, weight_ref, weight_x_ref,
    grad_ref, grad_x_ref, out_ref, out_x_ref, rows_ref,
):
    rows = own_ref.shape[0]
    rows_ref[rows_at(place_ref[0], rows), :] = own_ref[...]
    rows_ref[rows_at(1 - place_ref[0], rows), :] = other_ref[...]
    out_x_ref[...] = contract_rows(mixed_x_ref[...], rows_ref[...]).astype(BF16)
    out_ref[...] = contract_rows(mixed_ref[...], rows_ref[...]).astype(BF16)
    grad_ref[...] = times_transposed(rows_ref[...], weight_ref[...]).astype(BF16)
    grad_x_ref[...] = times_transposed(rows_ref[...], weight_x_ref[...]).astype(BF16)


def project_back(place, own, other, mixed, mixed_x, weight, weight_x):
    rows, width = own.shape
    return pl.pallas_call(
        project_back_kernel,
        out_shape=(shape(mixed.shape, BF16),) * 2 + (shape(weight.shape, BF16),) * 2,
        in_specs=[in_smem()] + [in_vmem()] * 6,
        out_specs=(in_vmem(),) * 4,
        scratch_shapes=[pltpu.VMEM((2 * rows, width), BF16)],
        compiler_params=parameters(14),
        cost_estimate=cost(3, 2**22),
        name="project_back",
    )(place, own, other, mixed, mixed_x, weight, weight_x)


def entry_back_kernel(place_ref, *refs, groups):
    grads = [[ref.at[k] for ref in refs[side * groups : (side + 1) * groups] for k in range(ref.shape[0])] for side in (0, 1)]
    weight_ref, first_ref, second_ref, own_ref, other_ref, joined_ref = refs[2 * groups :]
    rows = own_ref.shape[0]
    joined(joined_ref, (first_ref, second_ref), place_ref[1])
    for target, at in ((other_ref, 1 - place_ref[0]), (own_ref, place_ref[0])):
        here = rows_at(at, rows)
        left = jnp.concatenate([grad[here, :] for grad in grads[0]], axis=1)
        left_x = jnp.concatenate([grad[here, :] for grad in grads[1]], axis=1)
        total = dot(left, weight_ref[...]) + dot(left_x, joined_ref[...])
        target[...] = total.astype(target.dtype)


def entry_back(place, grads, grads_x, weight, weights_x):
    rows = grads[0].shape[1] // 2
    width = weight.shape[1]
    groups = len(grads)
    return pl.pallas_call(
        partial(entry_back_kernel, groups=groups),
        out_shape=(shape((rows, width), F32), shape((rows, width), BF16)),
        in_specs=[in_smem()] + [in_vmem()] * (2 * groups + 3),
        out_specs=(in_vmem(),) * 2,
        scratch_shapes=[pltpu.VMEM(weight.shape, BF16)],
        compiler_params=parameters(16),
        cost_estimate=cost(4, 2**22),
        name="entry_back",
    )(place, *grads, *grads_x, weight, *weights_x)


EXTRA_ROWS = 64


def hidden_kernel(place_ref, *refs, fetched, final):
    refs = list(refs)
    entries = refs[:2]
    upstreams = refs[2:4]
    if fetched:
        up_refs, down_refs = refs[4:6], refs[6:9]
        refs = refs[9:]
    else:
        up_ref, down_ref, bias_ref = refs[4:7]
        refs = refs[7:]
    if final:
        base = refs[:2]
        refs = refs[2:]
    grads = refs[:2]
    hidden_ref, up_sum_ref, kept_ref, sent_ref = refs[2:6]
    if fetched:
        up_all_ref, down_all_ref = refs[6:8]
        pre_grad_ref, down_sum_ref = refs[8:10]
        direct = down_refs[2].shape[0]
        joined(up_all_ref, up_refs, place_ref[1])
        joined(down_all_ref, down_refs, place_ref[1], direct)
        up_ref, down_ref = up_all_ref, down_all_ref
    else:
        pre_grad_ref, down_sum_ref = refs[6:8]
    rows, width = entries[0].shape
    units = up_ref.shape[1]
    up_sum_ref[width:, :] = jnp.zeros((EXTRA_ROWS, units), BF16)
    bias_sum = [jnp.zeros((1, BLOCK), F32) for _ in range(units // BLOCK)]
    if fetched:
        at = (units - direct) // 2
        bias = down_refs[0][at : at + 16, :].astype(F32)[:1]
    else:
        bias = one_line(bias_ref, 0, units).astype(F32)
    for part in range(2):

        def tile(step, carry, part=part):
            here = rows_at(step, BLOCK)
            there = pl.ds(pl.multiple_of(part * rows + step * BLOCK, BLOCK), BLOCK)
            entry = entries[part][here, :]
            upstream = upstreams[part][pl.ds(pl.multiple_of(rows + step * BLOCK, BLOCK), BLOCK), :]
            carry = list(carry)
            for block in range(units // BLOCK):
                cut = slice(block * BLOCK, (block + 1) * BLOCK)
                pre = dot(entry, up_ref[:, cut]) + bias[:, cut]
                hidden_grad = times_transposed(upstream, down_ref[cut, :])
                square = pre * pre
                half = 0.5 + 0.5 * jnp.tanh(pre * (TANH_SCALE + (TANH_SCALE * TANH_CUBE) * square))
                hidden = pre * half
                slope = half + (hidden - hidden * half) * (2 * TANH_SCALE + (6 * TANH_SCALE * TANH_CUBE) * square)
                pre_grad = (hidden_grad * slope).astype(BF16)
                hidden_ref[there, cut] = hidden.astype(BF16)
                pre_grad_ref[there, cut] = pre_grad
                carry[block] = carry[block] + jnp.sum(pre_grad.astype(F32), axis=0, keepdims=True)
            return tuple(carry)

        bias_sum = lax.fori_loop(0, rows // BLOCK, tile, tuple(bias_sum))
    for block in range(units // BLOCK):
        up_sum_ref[width : width + 1, block * BLOCK : (block + 1) * BLOCK] = bias_sum[block].astype(BF16)
    for part in (1, 0):

        def back(step, carry, part=part):
            here = rows_at(step, BLOCK)
            there = pl.ds(pl.multiple_of(part * rows + step * BLOCK, BLOCK), BLOCK)
            grad = times_transposed(pre_grad_ref[there, :], up_ref[...])
            if final:
                grad = grad + base[part][here, :]
            grads[part][here, :] = grad.astype(grads[part].dtype)
            return carry

        lax.fori_loop(0, rows // BLOCK, back, 0)
    for block in range(units // BLOCK):
        cut = slice(block * BLOCK, (block + 1) * BLOCK)
        up_sum = contract_rows(entries[0][...], pre_grad_ref[:rows, cut]) + contract_rows(entries[1][...], pre_grad_ref[rows:, cut])
        up_sum_ref[:width, cut] = up_sum.astype(BF16)
        down_sum = contract_rows(hidden_ref[:rows, cut], upstreams[0][rows:, :]) + contract_rows(hidden_ref[rows:, cut], upstreams[1][rows:, :])
        down_sum_ref[cut, :] = down_sum.astype(BF16)
    half = units // 2
    kept_ref[...] = down_sum_ref[rows_at(place_ref[1], half), :]
    sent_ref[...] = down_sum_ref[rows_at(1 - place_ref[1], half), :]


def hidden_part(place, entries, upstreams, weights, base):
    rows, width = entries[0].shape
    units = weights[0].shape[1]
    final = base is not None
    fetched = final
    inputs = [*entries, *upstreams, *weights, *(base or ())]
    outs = [shape((rows, width), F32), shape((rows, width), BF16 if final else F32)]
    outs += [kept((2 * rows, units), BF16), shape((width + EXTRA_ROWS, units), BF16)]
    outs += [shape((units // 2, width), BF16)] * 2
    if fetched:
        outs += [kept((width, units), BF16), kept((units, width), BF16)]
    return pl.pallas_call(
        partial(hidden_kernel, fetched=fetched, final=final),
        out_shape=tuple(outs),
        in_specs=[in_smem()] + [in_vmem()] * len(inputs),
        out_specs=(in_vmem(),) * len(outs),
        scratch_shapes=[pltpu.VMEM((2 * rows, units), BF16), pltpu.VMEM((units, width), BF16)],
        compiler_params=parameters(24),
        cost_estimate=cost(10, 2**23),
        name="hidden_part",
    )(place, *inputs)


def hidden_out_kernel(hidden_ref, hidden_x_ref, down_ref, down_x_ref, own_ref, other_ref):
    rows = own_ref.shape[0]
    for part, target in ((1, other_ref), (0, own_ref)):

        def tile(step, carry, part=part, target=target):
            there = pl.ds(pl.multiple_of(part * rows + step * BLOCK, BLOCK), BLOCK)
            out = dot(hidden_ref[there, :], down_ref[...]) + dot(hidden_x_ref[there, :], down_x_ref[...])
            target[rows_at(step, BLOCK), :] = out.astype(target.dtype)
            return carry

        lax.fori_loop(0, rows // BLOCK, tile, 0)


def hidden_out(hidden, hidden_x, down, down_x):
    rows, width = hidden.shape[0] // 2, down.shape[1]
    return pl.pallas_call(
        hidden_out_kernel,
        out_shape=(shape((rows, width), F32), shape((rows, width), BF16)),
        in_specs=[in_vmem()] * 4,
        out_specs=(in_vmem(),) * 2,
        compiler_params=parameters(12),
        cost_estimate=cost(4, 2**22),
        name="hidden_out",
    )(hidden, hidden_x, down, down_x)


ROWS = 128


def row_wise(body, name, row_inputs, whole_inputs, row_outs, sums, micros):
    rows, width = row_inputs[0].shape
    block = pl.BlockSpec((ROWS, width), lambda i: (i, 0))
    whole = [pl.BlockSpec(array.shape, lambda i: (0, 0)) for array in whole_inputs]
    outs = [shape((rows, width), kind) for kind in row_outs]
    out_specs = [block] * len(outs)
    if sums:
        outs.append(shape((8, width), F32))
        out_specs.append(pl.BlockSpec((8, width), lambda i: (0, 0)))

    def kernel(*refs):
        refs = list(refs)
        row_refs = [refs.pop(0) for _ in row_inputs]
        whole_refs = [refs.pop(0) for _ in whole_inputs]
        results, terms = body(*[ref[...] for ref in row_refs], *whole_refs)
        for ref, result in zip(refs, results):
            ref[...] = result.astype(ref.dtype)
        if sums:
            total = jnp.concatenate(
                [jnp.sum(term, axis=0, keepdims=True) for term in terms] + [jnp.zeros((8 - sums, width), F32)], axis=0
            )
            first = pl.program_id(0) == 0

            @pl.when(first)
            def _():
                refs[-1][...] = total

            @pl.when(jnp.logical_not(first))
            def _():
                refs[-1][...] += total

    return pl.pallas_call(
        kernel,
        grid=(rows // ROWS,),
        out_shape=tuple(outs),
        in_specs=[block] * len(row_inputs) + whole,
        out_specs=tuple(out_specs),
        compiler_params=parameters(12),
        cost_estimate=cost(micros, 2**20),
        name=name,
    )(*row_inputs, *whole_inputs)


def enter_kernel(place_ref, time_ref, tokens_ref, cotangent_ref, weight_ref, *refs):
    vectors, (table_ref, both_ref) = refs[:-2], refs[-2:]
    rows, width = tokens_ref.shape
    table_ref[...] = jnp.zeros_like(table_ref)
    row = 0
    for vector in vectors:
        for at in range(0, vector.shape[0], width // LANES):
            table_ref[row : row + 1, :] = one_line(vector, at, width)
            row += 1
    features = time_features(time_ref[place_ref[3]], 0, COND)
    for piece in range(6):
        cut = slice(piece * width, (piece + 1) * width)
        table_ref[piece : piece + 1, :] += jnp.sum(features * weight_ref[:, cut], axis=0, keepdims=True)
    table_ref[row : row + 1, :COND] = time_features(time_ref[place_ref[3]], 1, COND)
    table = table_ref[...]

    def tile(step, carry):
        here = rows_at(step, ROWS)
        scored, _ = standard_score_rows(tokens_ref[here, :].astype(F32))
        entry = scored * table[6:7] * (1.0 + table[1:2]) + table[0:1]
        both_ref[here, :] = entry.astype(BF16)
        there = pl.ds(pl.multiple_of(rows + step * ROWS, ROWS), ROWS)
        both_ref[there, :] = (table[5:6] * cotangent_ref[here, :].astype(F32)).astype(BF16)
        return carry

    lax.fori_loop(0, rows // ROWS, tile, 0)


def enter(place, time_index, tokens, cotangent, weight, vectors):
    vectors = [vector.reshape(-1, LANES) for vector in vectors]
    rows, width = tokens.shape
    return pl.pallas_call(
        enter_kernel,
        out_shape=(shape((16, width), F32), shape((2 * rows, width), BF16)),
        in_specs=[in_smem()] * 2 + [in_vmem()] * (3 + len(vectors)),
        out_specs=(in_vmem(),) * 2,
        compiler_params=parameters(14),
        cost_estimate=cost(4, 2**22),
        name="enter",
    )(place, time_index, in_hbm(tokens), in_hbm(cotangent), in_hbm(weight), *[in_hbm(vector) for vector in vectors])


def enter_second(tokens, branch_own, branch_other, modulation):
    branch = branch_own + branch_other.astype(F32)
    middle = tokens.astype(F32) + modulation[2:3, :] * branch
    scored, _ = standard_score_rows(middle)
    entry = scored * modulation[7:8, :] * (1.0 + modulation[4:5, :]) + modulation[3:4, :]
    return (middle, entry), ()


def leave(middle, cotangent, out_own, out_other, modulation):
    branch = out_own + out_other.astype(F32) + modulation[8:9, :]
    incoming = cotangent.astype(F32)
    branch_grad = (modulation[5:6, :] * incoming).astype(BF16).astype(F32)
    return (middle + modulation[5:6, :] * branch,), (incoming * branch, branch_grad)


def back_second(middle, cotangent, grad_own, grad_other, branch_own, branch_other, modulation):
    gain = modulation[7:8, :]
    scored, inverse = standard_score_rows(middle)
    entry_grad = grad_own + grad_other.astype(F32)
    normed_grad = entry_grad * (1.0 + modulation[4:5, :])
    middle_grad = cotangent.astype(F32) + norm_reverse_pass(normed_grad * gain, scored, inverse)
    branch = branch_own + branch_other.astype(F32)
    terms = (middle_grad * branch, entry_grad, entry_grad * (scored * gain), normed_grad * scored)
    return (modulation[2:3, :] * middle_grad, middle_grad), terms


def back_first(tokens, grad_own, grad_other, middle_grad, modulation):
    gain = modulation[6:7, :]
    scored, inverse = standard_score_rows(tokens.astype(F32))
    entry_grad = grad_own + grad_other.astype(F32)
    normed_grad = entry_grad * (1.0 + modulation[1:2, :])
    grad = middle_grad + norm_reverse_pass(normed_grad * gain, scored, inverse)
    return (grad,), (entry_grad, entry_grad * (scored * gain), normed_grad * scored)


def piece_kernel(place_ref, source_ref, *refs, rows):
    if len(refs) == 2:
        refs[1][rows:, :] = jnp.zeros_like(refs[1][rows:, :])
        refs[1][rows : rows + 1, :] = one_line(refs[0], 0, refs[1].shape[1])
    refs[-1][:rows, :] = source_ref[rows_at(place_ref[1], rows), :]


def own_piece(place, source, rows, line=None):
    extra = [] if line is None else [line.reshape(-1, LANES)]
    return pl.pallas_call(
        partial(piece_kernel, rows=rows),
        out_shape=shape((rows + 16 * len(extra), source.shape[1]), source.dtype),
        in_specs=[in_smem()] + [in_vmem()] * (1 + len(extra)),
        out_specs=in_vmem(),
        compiler_params=parameters(8),
        cost_estimate=cost(1, 2**20),
        name="own_piece",
    )(place, in_hbm(source), *extra)


def lower_half(source):
    rows, width = source.shape

    def kernel(source_ref, out_ref):
        out_ref[...] = source_ref[rows // 2 :, :]

    return pl.pallas_call(
        kernel,
        out_shape=shape((rows // 2, width), source.dtype),
        in_specs=[in_vmem()],
        out_specs=in_vmem(),
        compiler_params=parameters(8),
        cost_estimate=cost(1, 2**20),
        name="lower_half",
    )(in_hbm(source))


def sum_kernel(place_ref, a_ref, b_ref, kept_ref, sent_ref, *, bit):
    half = kept_ref.shape[0]
    for out, index in ((sent_ref, 1 - place_ref[bit]), (kept_ref, place_ref[bit])):
        here = rows_at(index, half)
        out[...] = (a_ref[here, :].astype(F32) + b_ref[here, :].astype(F32)).astype(BF16)


def summed(place, a, b, bit):
    rows, width = a.shape
    return pl.pallas_call(
        partial(sum_kernel, bit=bit),
        out_shape=(shape((rows // 2, width), BF16),) * 2,
        in_specs=[in_smem(), in_vmem(), in_vmem()],
        out_specs=(in_vmem(),) * 2,
        compiler_params=parameters(8),
        cost_estimate=cost(1.5, 2**20),
        name="summed",
    )(place, a, b)


def total_kernel(a_ref, b_ref, out_ref):
    out_ref[...] = (a_ref[...].astype(F32) + b_ref[...].astype(F32)).astype(BF16)


def total_of(a, b):
    return pl.pallas_call(
        total_kernel,
        out_shape=shape(a.shape, BF16),
        in_specs=[in_vmem()] * 2,
        out_specs=in_vmem(),
        compiler_params=parameters(8),
        cost_estimate=cost(0.7, 2**19),
        name="total_of",
    )(a, b)


def pair_kernel(place_ref, a_ref, b_ref, kept_a_ref, kept_b_ref, sent_ref):
    half = kept_a_ref.shape[0]
    mine, other = rows_at(place_ref[1], half), rows_at(1 - place_ref[1], half)
    sent_ref[:half, :] = a_ref[other, :]
    sent_ref[half:, :] = b_ref[other, :]
    kept_a_ref[...] = a_ref[mine, :]
    kept_b_ref[...] = b_ref[mine, :]


def pair_halves(place, a, b):
    rows, width = a.shape
    half = shape((rows // 2, width), BF16)
    return pl.pallas_call(
        pair_kernel,
        out_shape=(half, half, shape((rows, width), BF16)),
        in_specs=[in_smem(), in_vmem(), in_vmem()],
        out_specs=(in_vmem(),) * 3,
        compiler_params=parameters(8),
        cost_estimate=cost(1, 2**19),
        name="pair_halves",
    )(place, a, b)


def pair_total_kernel(a_ref, b_ref, got_ref, out_a_ref, out_b_ref):
    half = a_ref.shape[0]
    out_b_ref[...] = (b_ref[...].astype(F32) + got_ref[half:, :].astype(F32)).astype(BF16)
    out_a_ref[...] = (a_ref[...].astype(F32) + got_ref[:half, :].astype(F32)).astype(BF16)


def pair_total(a, b, got):
    return pl.pallas_call(
        pair_total_kernel,
        out_shape=(shape(a.shape, BF16),) * 2,
        in_specs=[in_vmem()] * 3,
        out_specs=(in_vmem(),) * 2,
        compiler_params=parameters(8),
        cost_estimate=cost(1, 2**19),
        name="pair_total",
    )(a, b, got)


def lay_kernel(place_ref, *refs, bit, cuts, ahead):
    if ahead:
        before_ref, *refs = refs
    outs, whole_ref = refs[2:-1], refs[-1]
    rows = refs[0].shape[0]
    for ref, index in zip(refs, (place_ref[bit], 1 - place_ref[bit])):
        whole_ref[rows_at(index, rows), :] = ref[...].astype(whole_ref.dtype)
    for out, (first, last) in zip(outs, cuts):
        at = out.shape[0] - (last - first)
        if at:
            out[:at, :] = before_ref[...]
        out[at:, :] = whole_ref[first:last, :]


def lay_straight_kernel(place_ref, own_ref, other_ref, out_ref, *, bit):
    rows = own_ref.shape[0]
    for ref, index in ((own_ref, place_ref[bit]), (other_ref, 1 - place_ref[bit])):
        out_ref[rows_at(index, rows), :] = ref[...].astype(out_ref.dtype)


def lay(place, own, other, bit, kind, cuts=None, before=None):
    rows, width = own.shape
    total = 2 * rows
    straight = cuts is None and before is None
    cuts = cuts or ((0, total),)
    at = 0 if before is None else before.shape[0]
    outs = [shape((last - first + (at if k == 0 else 0), width), kind) for k, (first, last) in enumerate(cuts)]
    inputs = [*([] if before is None else [before]), own, other]
    kernel = partial(lay_straight_kernel, bit=bit) if straight else partial(lay_kernel, bit=bit, cuts=cuts, ahead=before is not None)
    return pl.pallas_call(
        kernel,
        out_shape=tuple(outs),
        in_specs=[in_smem()] + [in_vmem()] * len(inputs),
        out_specs=(in_vmem(),) * len(outs),
        scratch_shapes=[] if straight else [pltpu.VMEM((total, width), kind)],
        compiler_params=parameters(14),
        cost_estimate=cost(2, 2**20),
        name="lay",
    )(place, *inputs)


TABLE = 16


def tabulate_kernel(first_ref, second_ref, last_ref, table_ref, out_ref):
    rows = [first_ref[0:2, :], second_ref[0:3, :], last_ref[0:1, :], first_ref[2:3, :], second_ref[3:4, :], last_ref[1:2, :]]
    rows += [table_ref[9:10, :], jnp.zeros((TABLE - 10, out_ref.shape[1]), F32)]
    out_ref[...] = jnp.concatenate(rows, axis=0)


def tabulate(first, second, last, table):
    return pl.pallas_call(
        tabulate_kernel,
        out_shape=shape(table.shape, F32),
        in_specs=[in_vmem()] * 4,
        out_specs=in_vmem(),
        compiler_params=parameters(8),
        cost_estimate=cost(1, 2**18),
        name="tabulate",
    )(first, second, last, table)


def slot_kernel(own_ref, other_ref, out_ref):
    out_ref[...] = own_ref[...]
    out_ref[0:9, :] = own_ref[0:9, :] + other_ref[0:9, :]


def slot_table(own, other):
    return pl.pallas_call(
        slot_kernel,
        out_shape=shape(own.shape, F32),
        in_specs=[in_vmem()] * 2,
        out_specs=in_vmem(),
        compiler_params=parameters(8),
        cost_estimate=cost(1, 2**18),
        name="slot_table",
    )(own, other)


def finish_kernel(table_ref, grad_ref, totals_ref, line_ref):
    slots, width = table_ref.shape[0] // TABLE, table_ref.shape[1]

    def one_slot(slot, carry):
        lines = table_ref[rows_at(slot, TABLE), :]
        for row in range(10):
            line_ref[row, pl.ds(slot, 1), :] = lines[row : row + 1]
        return carry

    lax.fori_loop(0, slots, one_slot, 0)
    features = line_ref[9][:, :COND]
    totals_ref[...] = jnp.zeros_like(totals_ref)
    for piece in range(9):
        terms = line_ref[piece]
        totals_ref[piece : piece + 1, :] = jnp.sum(terms, axis=0, keepdims=True)
        if piece < 6:
            grad_ref[:, piece * width : (piece + 1) * width] = lax.dot_general(
                features, terms, (((0,), (0,)), ((), ())), precision=lax.Precision.HIGHEST, preferred_element_type=F32
            )


def finish(table):
    width = table.shape[1]
    return pl.pallas_call(
        finish_kernel,
        out_shape=(shape((COND, 6 * width), F32), shape((TABLE, width), F32)),
        in_specs=[in_vmem()],
        out_specs=(in_vmem(),) * 2,
        scratch_shapes=[pltpu.VMEM((10, table.shape[0] // TABLE, width), F32)],
        compiler_params=parameters(20),
        cost_estimate=cost(3, 2**20),
        name="finish",
    )(table)


class Order:
    def __init__(self):
        self.token = ()

    def __call__(self, value):
        return after(value, *self.token) if self.token else value

    def done(self, result):
        self.token = (result[-1] if isinstance(result, (tuple, list)) else result,)
        return result


def dp_bits():
    bits = []
    bit = 1
    while bit < lax.axis_size("dp"):
        bits.append(bit)
        bit *= 2
    return bits


def per_device(
    tokens,
    cotangent,
    doc_lengths,
    time_index,
    attention_norm_gain,
    qkv_weight,
    out_weight,
    feedforward_norm_gain,
    up_weight,
    up_bias,
    down_weight,
    down_bias,
    ada_weight,
    ada_bias,
):
    rows, width = tokens.shape
    core = lax.axis_index("mp") % 2
    slot = lax.axis_index("mp") // 2
    index = lax.axis_index("dp")
    bits = dp_bits()
    place = [core, index % 2, index // 2 % 2, slot] + [index // bit % 2 for bit in bits[2:]]
    place = jnp.stack(place).astype(jnp.int32)
    order = Order()

    def near(value):
        return swap(value, "mp", 1)

    def across(value):
        return swap(value, "mp", 2)

    def relayed(value):
        return swap(value, "dp", 1)

    qkv_turned = qkv_weight.T
    qkv_half = order.done(own_piece(place, qkv_turned, qkv_turned.shape[0] // 2))
    qkv_a = across(qkv_half)
    table, both = order.done(
        enter(
            place,
            time_index,
            order(tokens),
            cotangent,
            ada_weight,
            (ada_bias, attention_norm_gain, feedforward_norm_gain, down_bias),
        )
    )
    both_near = near(both)
    out_weight_x = across(order(out_weight))
    up_half = order.done(own_piece(place, after(order(up_weight), qkv_a), width // 2))
    up_a = across(up_half)
    qkv_b = relayed(qkv_a)

    query, key, value, mixture, entry_one_all = order.done(
        attend_forward(place, doc_lengths, order(both), after(both_near, qkv_a), (qkv_turned,), True)
    )
    query_x, key_x, value_x, mixture_x = order.done(
        attend_forward(place, doc_lengths, order(both), both_near, (qkv_a, qkv_b), False)
    )
    branch_own, branch_other = order.done(project_out(place, mixture, order(mixture_x), out_weight, out_weight_x))
    branch_other = near(branch_other)
    quarter = down_weight.shape[0] // 4
    down_a = across(order.done(own_piece(place, order(down_weight), quarter, up_bias)))
    up_b = relayed(after(up_a, branch_own))
    middle, entry_two = order.done(
        row_wise(
            enter_second, "enter_second", (order(tokens), branch_own, after(branch_other, up_a)), (table,), (F32, BF16), 0, 3
        )
    )
    entry_two_near = near(entry_two)
    down_straight = across(order.done(lower_half(order(down_weight))))
    down_b = relayed(after(down_a, entry_two))
    entries_two = (entry_two, after(entry_two_near, down_a))

    lines = (-1, LANES)
    grad_base, grad_base_other, hidden, up_own, down_kept, down_sent = order.done(
        hidden_part(
            place,
            entries_two,
            (order(both), both_near),
            (up_weight, down_weight, up_bias.reshape(lines)),
            None,
        )
    )
    down_got = swap(down_sent, "dp", 1)
    grad_own, grad_other, hidden_x, up_x, down_kept_x, down_sent_x, _, down_weight_x = order.done(
        hidden_part(
            place,
            (order(entries_two[0]), entries_two[1]),
            (both, both_near),
            (up_a, up_b, down_a, down_b, down_straight),
            (grad_base, grad_base_other),
        )
    )
    grad_other = near(grad_other)
    up_got = across(up_x)
    down_got_x = swap(down_sent_x, "dp", 1)
    down_part = order.done(total_of(order(down_kept), down_got))
    out_own, out_other = order.done(hidden_out(order(hidden), hidden_x, down_weight, down_weight_x))
    out_other = near(out_other)
    attn_grad, middle_grad, sums_two = order.done(
        row_wise(
            back_second,
            "back_second",
            (order(middle), cotangent, grad_own, grad_other, branch_own, branch_other),
            (table,),
            (BF16, F32),
            4,
            4,
        )
    )
    attn_grad_near = near(attn_grad)
    output, sums_out = order.done(
        row_wise(leave, "leave", (order(middle), cotangent, out_own, out_other), (table,), (BF16,), 2, 3)
    )
    mixture_grad, mixture_grad_x, out_sum, out_sum_x = order.done(
        project_back(place, order(attn_grad), attn_grad_near, mixture, mixture_x, out_weight, out_weight_x)
    )

    sides = ((query, key, value, mixture, mixture_grad), (query_x, key_x, value_x, mixture_x, mixture_grad_x))

    def backward(head, extras):
        return order.done(
            attend_backward(place, doc_lengths, head, 1, sides, order(entry_one_all), extras)
        )

    back_0, first_sum, back_x_0, first_sum_x = backward(0, (out_sum, out_sum_x))
    down_part_x = order.done(total_of(order(down_kept_x), down_got_x))
    down_got = across(down_part_x)
    back_1, head_sum, back_x_1, head_sum_x = backward(1, ())
    up_kept, up_sent = order.done(summed(place, order(up_own), up_got, 2))
    up_got = swap(up_sent, "dp", 2)
    first_got = across(order(first_sum_x))
    back_2, rest_sum, back_x_2, rest_sum_x = backward(2, (head_sum, head_sum_x))
    rest_kept, rest_kept_x, rest_sent = order.done(pair_halves(place, order(rest_sum), rest_sum_x))
    rest_got = swap(rest_sent, "dp", 1)
    first_own, first_other = order.done(
        entry_back(
            place, (order(back_0), back_1, back_2), (back_x_0, back_x_1, back_x_2), qkv_turned, (qkv_a, qkv_b)
        )
    )
    first_other = near(first_other)
    down_kept, down_sent = order.done(summed(place, order(down_part), down_got, 2))
    down_got = swap(down_sent, "dp", 2)
    input_gradient, sums_one = order.done(
        row_wise(
            back_first, "back_first", (order(tokens), first_own, first_other, middle_grad), (table,), (F32,), 3, 3
        )
    )
    sums = order.done(tabulate(order(sums_one), sums_two, sums_out, table))
    sums_near = near(sums)

    def on(value, step=0):
        return swap(value, "dp", bits[2 + step])

    def doubled(value, got):
        for step in range(len(bits) - 2):
            value = order.done(total_of(order(value), got))
            if step + 3 < len(bits):
                got = on(value, step + 1)
        return value

    up_kept, up_sent = order.done(summed(place, order(up_kept), up_got, 1))
    up_got = swap(up_sent, "dp", 1)
    sums = order.done(slot_table(order(sums), sums_near))
    sums_got = across(sums)
    down_value = order.done(total_of(order(down_kept), down_got))
    down_got = on(down_value)
    rest_part_x, rest_part = order.done(pair_total(order(rest_kept), rest_kept_x, rest_got)[::-1])
    rest_got = across(rest_part_x)
    first_kept, first_sent = order.done(summed(place, order(first_sum), first_got, 1))
    first_got = swap(first_sent, "dp", 1)
    up_value = order.done(total_of(order(up_kept), up_got))
    up_got = on(up_value)
    (sums,) = order.done(lay(place, order(sums), sums_got, 3, F32))
    sums_got = swap(sums, "dp", 1)
    first_kept, first_sent = order.done(summed(place, order(first_kept), first_got, 2))
    first_got = swap(first_sent, "dp", 2)
    rest_kept, rest_sent = order.done(summed(place, order(rest_part), rest_got, 2))
    rest_got = swap(rest_sent, "dp", 2)
    (sums,) = order.done(lay(place, order(sums), sums_got, 1, F32))
    sums_got = swap(sums, "dp", 2)
    down_value = doubled(down_value, down_got)
    down_got = swap(down_value, "dp", 2)
    first_value = order.done(total_of(order(first_kept), first_got))
    first_got = on(first_value)
    rest_value = order.done(total_of(order(rest_kept), rest_got))
    rest_got = on(rest_value)
    up_value = doubled(up_value, up_got)
    up_got = swap(up_value, "dp", 1)
    (sums,) = order.done(lay(place, order(sums), sums_got, 2, F32))
    sums_got = on(sums)
    (down_value,) = order.done(lay(place, order(down_value), down_got, 2, BF16))
    down_got = swap(down_value, "dp", 1)
    first_value = doubled(first_value, first_got)
    first_got = swap(first_value, "dp", 2)
    rest_value = doubled(rest_value, rest_got)
    rest_got = swap(rest_value, "dp", 2)
    (up_value,) = order.done(lay(place, order(up_value), up_got, 1, BF16))
    up_got = swap(up_value, "dp", 2)
    for step in range(len(bits) - 2):
        (sums,) = order.done(lay(place, order(sums), sums_got, 4 + step, F32))
        if step + 3 < len(bits):
            sums_got = on(sums, step + 1)
    ada_grad, totals = order.done(finish(order(sums)))
    (first_value,) = order.done(lay(place, order(first_value), first_got, 2, BF16))
    first_got = swap(first_value, "dp", 1)
    (rest_value,) = order.done(lay(place, order(rest_value), rest_got, 2, BF16))
    rest_got = swap(rest_value, "dp", 1)
    (down_grad,) = order.done(lay(place, order(down_value), down_got, 1, F32))
    up_grad, bias_grad = order.done(
        lay(place, order(up_value), up_got, 2, F32, cuts=((0, width), (width, width + 8)))
    )
    out_rows = out_weight.shape[0]
    out_grad, head_grad = order.done(
        lay(place, order(first_value), first_got, 1, F32, cuts=((0, out_rows), (out_rows, first_sum.shape[0])))
    )
    (qkv_grad,) = order.done(lay(place, order(rest_value), rest_got, 1, F32, before=head_grad))
    return (
        output,
        input_gradient,
        totals[6],
        qkv_grad.T,
        out_grad,
        totals[7],
        up_grad,
        bias_grad[0],
        down_grad,
        totals[8],
        ada_grad,
        totals[:6].reshape(6 * width),
    )


def solution(mesh):
    in_specs = (
        P(("dp", "mp"), None),
        P(("dp", "mp"), None),
        P("dp", None),
        P("dp"),
        P(),
        P(None, "mp"),
        P("mp", None),
        P(),
        P(None, "mp"),
        P("mp"),
        P("mp", None),
        P(),
        P(),
        P(),
    )
    out_specs = (
        P(("dp", "mp"), None),
        P(("dp", "mp"), None),
        P(),
        P(None, "mp"),
        P("mp", None),
        P(),
        P(None, "mp"),
        P("mp"),
        P("mp", None),
        P(),
        P(),
        P(),
    )
    return jax.shard_map(
        per_device, mesh=mesh, in_specs=in_specs, out_specs=out_specs, check_vma=False
    )
```

```python
from functools import partial
import math

import jax
import jax.numpy as jnp
from jax import lax
from jax.experimental import pallas as pl
from jax.experimental.pallas import tpu as pltpu
from jax.sharding import PartitionSpec as P

HEAD_DIM = 64
COND = 128
BLOCK = 256
STEP = 128
LANES = 128
BF16 = jnp.bfloat16
F32 = jnp.float32
TANH_SCALE = math.sqrt(2 / math.pi)
TANH_CUBE = 0.044715


def swap(value, axis, bit):
    size = lax.axis_size(axis)
    return lax.ppermute(value, axis, [(i, i ^ bit) for i in range(size)])


def time_features(time, axis, cond_width):
    half_width = cond_width // 2
    dims = (cond_width, 1) if axis == 0 else (1, cond_width)
    place = lax.broadcasted_iota(jnp.int32, dims, axis)
    second = place >= half_width
    ladder = jnp.where(second, place - half_width, place).astype(F32)
    angles = time.astype(F32) * jnp.exp(ladder * (-math.log(10000.0) / half_width))
    waves = jnp.where(second, jnp.sin(angles), jnp.cos(angles))
    return waves / (1.0 + jnp.exp(-waves))


def standard_score_rows(values):
    center = values - jnp.mean(values, axis=-1, keepdims=True)
    inverse_deviation = lax.rsqrt(jnp.mean(center * center, axis=-1, keepdims=True) + 1e-05)
    return (center * inverse_deviation, inverse_deviation)


def norm_reverse_pass(incoming_gradient, centered_scaled, inverse_deviation):
    return inverse_deviation * (
        incoming_gradient
        - jnp.mean(incoming_gradient, axis=-1, keepdims=True)
        - centered_scaled * jnp.mean(incoming_gradient * centered_scaled, axis=-1, keepdims=True)
    )


def dot(a, b):
    return jnp.dot(a, b, preferred_element_type=F32)


def contract_rows(a, b):
    return lax.dot_general(a, b, (((0,), (0,)), ((), ())), preferred_element_type=F32)


def times_transposed(a, b):
    return lax.dot_general(a, b, (((1,), (1,)), ((), ())), preferred_element_type=F32)


def one_line(lines_ref, first, width):
    return jnp.concatenate([lines_ref[first + k : first + k + 1, :] for k in range(width // LANES)], axis=1)


def in_vmem():
    return pl.BlockSpec(memory_space=pltpu.VMEM)


def in_smem():
    return pl.BlockSpec(memory_space=pltpu.SMEM)


def in_hbm(value):
    return pltpu.with_memory_space_constraint(value, pltpu.HBM)


def kept(dims, kind):
    return pltpu.VMEM(dims, kind)


def shape(dims, kind):
    return jax.ShapeDtypeStruct(dims, kind)


def cost(micros, size):
    return pl.CostEstimate(flops=int((micros + 12) * 1.1e9), bytes_accessed=size, transcendentals=0)


def small_cost(micros=0.001):
    return pl.CostEstimate(flops=int(micros * 1.1e9), bytes_accessed=10**4, transcendentals=0)


def parameters(mebibytes):
    return pltpu.CompilerParams(vmem_limit_bytes=mebibytes * 2**20)


def anywhere():
    return pl.BlockSpec(memory_space=pl.ANY)


def after(value, *tokens):
    return lax.optimization_barrier((value, *tokens))[0]


def rows_at(index, count):
    return pl.ds(pl.multiple_of(index * count, count), count)


def joined(target, pieces, mine, direct=0):
    rows = (target.shape[0] - direct) // 2
    for piece, index in zip(pieces, (mine, 1 - mine)):
        target[rows_at(index, rows), :] = piece[:rows, :]
    if direct:
        target[2 * rows :, :] = pieces[2][...]


def window_sizes(slot_length):
    return tuple(range(2 * STEP, slot_length + 1, STEP))


def block_window(lengths_ref, slot, block, slot_length):
    first = block * BLOCK
    last = first + BLOCK - 1
    end = jnp.int32(0)
    low = jnp.int32(0)
    high = jnp.int32(slot_length)
    for document in range(lengths_ref.shape[1]):
        end = end + lengths_ref[slot, document]
        low = jnp.where(end <= first, jnp.maximum(low, end), low)
        high = jnp.where(end > last, jnp.minimum(high, end), high)
    low = lax.div(low, jnp.int32(STEP)) * STEP
    size = jnp.maximum(lax.div(high - low + (STEP - 1), jnp.int32(STEP)) * STEP, 2 * STEP)
    return pl.multiple_of(jnp.minimum(low, slot_length - size), STEP), size


def mask_features(lengths_ref, slot, first, rows):
    documents = lengths_ref.shape[1]
    place = first + lax.broadcasted_iota(jnp.int32, (rows, HEAD_DIM), 0)
    lanes = lax.broadcasted_iota(jnp.int32, (rows, HEAD_DIM), 1)
    segment = jnp.zeros((rows, HEAD_DIM), jnp.int32)
    end = jnp.int32(0)
    for document in range(documents):
        end = end + lengths_ref[slot, document]
        segment = segment + jnp.where(place >= end, 1, 0)
    same = lanes == segment
    one = (lanes >= documents) & (lanes < documents + 3)
    key = jnp.where((lanes < documents) & jnp.logical_not(same), -1e30, jnp.where(one, 1.0, 0.0))
    return key.astype(BF16), jnp.where(same, 1.0, 0.0).astype(BF16)


def three_parts(value, lanes, at):
    first = value.astype(BF16).astype(F32)
    rest = value - first
    second = rest.astype(BF16).astype(F32)
    third = rest - second
    return jnp.where(lanes == at, first, jnp.where(lanes == at + 1, second, jnp.where(lanes == at + 2, third, 0.0)))


def attend_forward_kernel(place_ref, lengths_ref, own_ref, other_ref, *refs, fetched, keep):
    refs = list(refs)
    weight_refs = [refs.pop(0) for _ in range(2 if fetched else 1)]
    weight_ref = weight_refs[0]
    query_ref, key_ref, value_ref, out_ref = refs[:4]
    refs = refs[4:]
    slot = place_ref[3]
    documents = lengths_ref.shape[1]
    if keep:
        kept_ref = refs.pop(0)
    if fetched:
        joined_ref = refs.pop(0)
        joined(joined_ref, weight_refs, place_ref[1])
        weight_ref = joined_ref
    rows = own_ref.shape[0] // 2
    length = 2 * rows
    heads = weight_ref.shape[0] // (3 * HEAD_DIM)
    core = place_ref[0]
    lanes = lax.broadcasted_iota(jnp.int32, (rows, HEAD_DIM), 1)
    ones = jnp.where(lanes < 3, 1.0, 0.0).astype(BF16)
    for source, at in ((own_ref, core), (other_ref, 1 - core)):
        here = rows_at(at, rows)
        key_extra, query_extra = mask_features(lengths_ref, slot, at * rows, rows)
        if keep:
            kept_ref[here, :] = source[:rows, :]
        qkv = times_transposed(source[:rows, :], weight_ref[...]).astype(BF16)
        for head in range(heads):
            at = 3 * HEAD_DIM * head
            query = qkv[:, at : at + HEAD_DIM] * 0.125
            key = qkv[:, at + HEAD_DIM : at + 2 * HEAD_DIM]
            value = qkv[:, at + 2 * HEAD_DIM : at + 3 * HEAD_DIM]
            query_ref[head, here, :] = jnp.concatenate([query, query_extra], axis=1)
            key_ref[head, here, :] = jnp.concatenate([key, key_extra], axis=1)
            value_ref[head, here, :] = jnp.concatenate([value, ones], axis=1)

    def one_block(block, carry):
        here = rows_at(block, BLOCK)
        start, window = block_window(lengths_ref, slot, block, length)
        for size in window_sizes(length):

            @pl.when(window == size)
            def _():
                every = range(heads)
                span = pl.ds(start, size)
                queries = [query_ref[head, here, :] for head in every]
                scores = [times_transposed(queries[head], key_ref[head, span, :]) for head in every]
                wide = lax.broadcasted_iota(jnp.int32, (BLOCK, LANES), 1)
                mixed = []
                for head in every:
                    highest = jnp.max(scores[head], axis=1, keepdims=True)
                    raised = jnp.exp(scores[head] - highest).astype(BF16)
                    product = dot(raised, value_ref[head, span, :])
                    total = product[:, HEAD_DIM : HEAD_DIM + 1]
                    mixed.append(product[:, :HEAD_DIM] / total)
                    extra = three_parts(highest + jnp.log(total), wide, HEAD_DIM + documents)
                    query_ref[head, here, :] = (queries[head].astype(F32) - extra).astype(BF16)
                out_ref[here, :] = jnp.concatenate(mixed, axis=1).astype(BF16)

        return carry

    lax.fori_loop(0, length // BLOCK, one_block, 0)


def attend_forward(place, lengths, own, other, weights, keep):
    length, width = own.shape
    fetched = len(weights) == 2
    columns = weights[0].shape[0] * len(weights)
    heads = columns // (3 * HEAD_DIM)
    head_wise = kept((heads, length, LANES), BF16)
    outs = [head_wise] * 3 + [kept((length, heads * HEAD_DIM), BF16)]
    if keep:
        outs.append(kept((length, width), BF16))
    return pl.pallas_call(
        partial(attend_forward_kernel, fetched=fetched, keep=keep),
        out_shape=tuple(outs),
        in_specs=[in_smem()] * 2 + [in_vmem()] * (2 + len(weights)),
        out_specs=(in_vmem(),) * len(outs),
        scratch_shapes=[pltpu.VMEM((columns, width), BF16)] if fetched else [],
        compiler_params=parameters(24),
        cost_estimate=cost(9, 2**22),
        name="attend_forward",
    )(place, lengths, own, other, *weights)


def attend_backward_kernel(place_ref, lengths_ref, *refs, first, heads, extra):
    slot = place_ref[3]
    every = range(2 * heads)
    inputs = []
    for side in range(2):
        for head in range(heads):
            arrays = [refs[5 * side + k].at[first + head] for k in range(3)]
            inputs.append((*arrays, refs[5 * side + 3], refs[5 * side + 4], first + head))
    entry_ref = refs[10]
    refs = refs[11:]
    if extra:
        extras = refs[:2]
        refs = refs[2:]
        for side in range(2):
            refs[2 * side + 1][:extra, :] = extras[side][...]
    outs = refs[:4]
    key_turned_ref, upstream_ref, sum_ref, query_grad_ref, right_ref = refs[4:]
    length = entry_ref.shape[0]
    lanes = lax.broadcasted_iota(jnp.int32, (length, HEAD_DIM), 1)
    zero = jnp.zeros((length, HEAD_DIM), BF16)
    for item in every:
        query_ref, key_ref, value_ref, mixed_ref, grad_ref, head = inputs[item]
        columns = slice(head * HEAD_DIM, (head + 1) * HEAD_DIM)
        upstream = grad_ref[:, columns]
        inner = jnp.sum(mixed_ref[:, columns].astype(F32) * upstream.astype(F32), axis=1, keepdims=True)
        upstream_ref[item] = jnp.concatenate([upstream, -three_parts(inner, lanes, 0).astype(BF16)], axis=1)
        key_turned_ref[item] = key_ref[:, :HEAD_DIM].T
        right_ref[item, 0] = jnp.concatenate([upstream, zero], axis=1)
        right_ref[item, 1] = jnp.concatenate([zero, query_ref[:, :HEAD_DIM]], axis=1)
    sum_ref[...] = jnp.zeros_like(sum_ref)

    def one_block(block, carry):
        here = rows_at(block, BLOCK)
        start, window = block_window(lengths_ref, slot, block, length)
        for size in window_sizes(length):

            @pl.when(window == size)
            def _():
                span = pl.ds(start, size)
                queries = [inputs[s][0][here, :] for s in every]
                upstreams = [upstream_ref[s, here, :] for s in every]
                rights = [
                    jnp.concatenate([right_ref[s, 0, here, :], right_ref[s, 1, here, :]], axis=0) for s in every
                ]
                weights = [jnp.exp(times_transposed(inputs[s][1][span, :], queries[s])) for s in every]
                raised = [times_transposed(inputs[s][2][span, :], upstreams[s]) for s in every]
                score_grads = [(a * b).astype(BF16) for a, b in zip(weights, raised)]
                turned = []
                for s in every:
                    left = jnp.concatenate([weights[s].astype(BF16), score_grads[s]], axis=1)
                    sum_ref[s, span, :] += dot(left, rights[s])
                    turned.append(dot(key_turned_ref[s, :, span], score_grads[s]))
                turned = (jnp.concatenate(turned, axis=0) * 0.125).T
                for s in every:
                    query_grad_ref[s, here, :] = turned[:, s * HEAD_DIM : (s + 1) * HEAD_DIM].astype(BF16)

        return carry

    lax.fori_loop(0, length // BLOCK, one_block, 0)
    for side in (1, 0):
        for head in range(heads):
            item = side * heads + head
            sums = sum_ref[item]
            grads = jnp.concatenate(
                [query_grad_ref[item], sums[:, HEAD_DIM:].astype(BF16), sums[:, :HEAD_DIM].astype(BF16)], axis=1
            )
            outs[2 * side][head] = grads
            part = 3 * HEAD_DIM
            outs[2 * side + 1][extra + head * part : extra + (head + 1) * part, :] = contract_rows(grads, entry_ref[...]).astype(BF16)


def attend_backward(place, lengths, first, heads, sides, entry, extras):
    extra = extras[0].shape[0] if extras else 0
    length, width = entry.shape
    flat = [array for side in sides for array in side]
    outs = [shape((heads, length, 3 * HEAD_DIM), BF16), shape((extra + heads * 3 * HEAD_DIM, width), BF16)] * 2
    count = 2 * heads
    return pl.pallas_call(
        partial(attend_backward_kernel, first=first, heads=heads, extra=extra),
        out_shape=tuple(outs),
        in_specs=[in_smem()] * 2 + [in_vmem()] * (11 + len(extras)),
        out_specs=(in_vmem(),) * len(outs),
        scratch_shapes=[
            pltpu.VMEM((count, HEAD_DIM, length), BF16),
            pltpu.VMEM((count, length, LANES), BF16),
            pltpu.VMEM((count, length, LANES), F32),
            pltpu.VMEM((count, length, HEAD_DIM), BF16),
            pltpu.VMEM((count, 2, length, LANES), BF16),
        ],
        compiler_params=parameters(24),
        cost_estimate=cost(9 * heads, 2**22),
        name="attend_backward",
    )(place, lengths, *flat, entry, *extras)


def project_out_kernel(place_ref, mixed_ref, mixed_x_ref, weight_ref, weight_x_ref, own_ref, other_ref):
    rows = own_ref.shape[0]
    for target, at in ((other_ref, 1 - place_ref[0]), (own_ref, place_ref[0])):
        here = rows_at(at, rows)
        total = dot(mixed_ref[here, :], weight_ref[...]) + dot(mixed_x_ref[here, :], weight_x_ref[...])
        target[...] = total.astype(target.dtype)


def project_out(place, mixed, mixed_x, weight, weight_x):
    rows = mixed.shape[0] // 2
    width = weight.shape[1]
    return pl.pallas_call(
        project_out_kernel,
        out_shape=(shape((rows, width), F32), shape((rows, width), BF16)),
        in_specs=[in_smem()] + [in_vmem()] * 4,
        out_specs=(in_vmem(),) * 2,
        compiler_params=parameters(12),
        cost_estimate=cost(2, 2**22),
        name="project_out",
    )(place, mixed, mixed_x, weight, weight_x)


def project_back_kernel(
    place_ref, own_ref, other_ref, mixed_ref, mixed_x_ref, weight_ref, weight_x_ref,
    grad_ref, grad_x_ref, out_ref, out_x_ref, rows_ref,
):
    rows = own_ref.shape[0]
    rows_ref[rows_at(place_ref[0], rows), :] = own_ref[...]
    rows_ref[rows_at(1 - place_ref[0], rows), :] = other_ref[...]
    out_x_ref[...] = contract_rows(mixed_x_ref[...], rows_ref[...]).astype(BF16)
    out_ref[...] = contract_rows(mixed_ref[...], rows_ref[...]).astype(BF16)
    grad_ref[...] = times_transposed(rows_ref[...], weight_ref[...]).astype(BF16)
    grad_x_ref[...] = times_transposed(rows_ref[...], weight_x_ref[...]).astype(BF16)


def project_back(place, own, other, mixed, mixed_x, weight, weight_x):
    rows, width = own.shape
    return pl.pallas_call(
        project_back_kernel,
        out_shape=(shape(mixed.shape, BF16),) * 2 + (shape(weight.shape, BF16),) * 2,
        in_specs=[in_smem()] + [in_vmem()] * 6,
        out_specs=(in_vmem(),) * 4,
        scratch_shapes=[pltpu.VMEM((2 * rows, width), BF16)],
        compiler_params=parameters(14),
        cost_estimate=cost(3, 2**22),
        name="project_back",
    )(place, own, other, mixed, mixed_x, weight, weight_x)


def entry_back_kernel(place_ref, *refs, groups):
    grads = [[ref.at[k] for ref in refs[side * groups : (side + 1) * groups] for k in range(ref.shape[0])] for side in (0, 1)]
    weight_ref, first_ref, second_ref, own_ref, other_ref, joined_ref = refs[2 * groups :]
    rows = own_ref.shape[0]
    joined(joined_ref, (first_ref, second_ref), place_ref[1])
    for target, at in ((other_ref, 1 - place_ref[0]), (own_ref, place_ref[0])):
        here = rows_at(at, rows)
        left = jnp.concatenate([grad[here, :] for grad in grads[0]], axis=1)
        left_x = jnp.concatenate([grad[here, :] for grad in grads[1]], axis=1)
        total = dot(left, weight_ref[...]) + dot(left_x, joined_ref[...])
        target[...] = total.astype(target.dtype)


def entry_back(place, grads, grads_x, weight, weights_x):
    rows = grads[0].shape[1] // 2
    width = weight.shape[1]
    groups = len(grads)
    return pl.pallas_call(
        partial(entry_back_kernel, groups=groups),
        out_shape=(shape((rows, width), F32), shape((rows, width), BF16)),
        in_specs=[in_smem()] + [in_vmem()] * (2 * groups + 3),
        out_specs=(in_vmem(),) * 2,
        scratch_shapes=[pltpu.VMEM(weight.shape, BF16)],
        compiler_params=parameters(16),
        cost_estimate=cost(4, 2**22),
        name="entry_back",
    )(place, *grads, *grads_x, weight, *weights_x)


def hidden_grad(both, down):
    rows = both.shape[0] // 2
    units = down.shape[0]

    def kernel(both_ref, down_ref, out_ref):
        out_ref[...] = times_transposed(both_ref[rows:, :], down_ref[...])

    return pl.pallas_call(
        kernel,
        out_shape=kept((rows, units), F32),
        in_specs=[in_vmem()] * 2,
        out_specs=in_vmem(),
        compiler_params=parameters(8),
        cost_estimate=cost(1, 2**21),
        name="hidden_grad",
    )(both, down)


def hidden_kernel(place_ref, *refs, fetched):
    refs = list(refs)
    entries = refs[:2]
    upstreams = refs[2:4]
    if fetched:
        up_refs, down_refs = refs[4:6], refs[6:9]
        base = refs[9:11]
        refs = refs[11:]
    else:
        up_ref, bias_ref = refs[4:6]
        hidden_grads = refs[6:8]
        refs = refs[8:]
    grads = refs[:2]
    hidden_ref, bias_sum_ref = refs[2:4]
    if fetched:
        up_kept_ref, up_sent_ref, down_kept_ref, down_sent_ref = refs[4:8]
        up_all_ref, down_all_ref = refs[8:10]
        pre_grad_ref, sum_ref = refs[10:12]
        up_sum_ref = down_sum_ref = sum_ref
        direct = down_refs[2].shape[0]
        joined(up_all_ref, up_refs, place_ref[1])
        joined(down_all_ref, down_refs, place_ref[2], direct)
        up_ref, down_ref = up_all_ref, down_all_ref
    else:
        up_sum_ref, down_sum_ref, pre_grad_ref = refs[4:7]
    rows, width = entries[0].shape
    units = up_ref.shape[1]
    bias_sum = [jnp.zeros((1, BLOCK), F32) for _ in range(units // BLOCK)]
    if fetched:
        at = (units - direct) // 2
        bias = down_refs[0][at : at + 16, :].astype(F32)[:1]
    else:
        bias = one_line(bias_ref, 0, units).astype(F32)
    for part in range(2):

        def tile(step, carry, part=part):
            here = rows_at(step, BLOCK)
            there = pl.ds(pl.multiple_of(part * rows + step * BLOCK, BLOCK), BLOCK)
            entry = entries[part][here, :]
            if fetched:
                upstream = upstreams[part][pl.ds(pl.multiple_of(rows + step * BLOCK, BLOCK), BLOCK), :]
            carry = list(carry)
            for block in range(units // BLOCK):
                cut = slice(block * BLOCK, (block + 1) * BLOCK)
                pre = dot(entry, up_ref[:, cut]) + bias[:, cut]
                if fetched:
                    given = times_transposed(upstream, down_ref[cut, :])
                else:
                    given = hidden_grads[part][here, cut]
                square = pre * pre
                half = 0.5 + 0.5 * jnp.tanh(pre * (TANH_SCALE + (TANH_SCALE * TANH_CUBE) * square))
                hidden = pre * half
                slope = half + (hidden - hidden * half) * (2 * TANH_SCALE + (6 * TANH_SCALE * TANH_CUBE) * square)
                pre_grad = (given * slope).astype(BF16)
                hidden_ref[there, cut] = hidden.astype(BF16)
                pre_grad_ref[there, cut] = pre_grad
                carry[block] = carry[block] + jnp.sum(pre_grad.astype(F32), axis=0, keepdims=True)
            return tuple(carry)

        bias_sum = lax.fori_loop(0, rows // BLOCK, tile, tuple(bias_sum))
    bias_sum_ref[...] = jnp.zeros_like(bias_sum_ref)
    bias_sum_ref[0:1, :] = jnp.concatenate(bias_sum, axis=1)
    for part in (1, 0):

        def back(step, carry, part=part):
            here = rows_at(step, BLOCK)
            there = pl.ds(pl.multiple_of(part * rows + step * BLOCK, BLOCK), BLOCK)
            grad = times_transposed(pre_grad_ref[there, :], up_ref[...])
            if fetched:
                grad = grad + base[part][here, :]
            grads[part][here, :] = grad.astype(grads[part].dtype)
            return carry

        lax.fori_loop(0, rows // BLOCK, back, 0)
    half = units // 2
    for block in range(units // BLOCK):
        cut = slice(block * BLOCK, (block + 1) * BLOCK)
        total = contract_rows(entries[0][...], pre_grad_ref[:rows, cut]) + contract_rows(entries[1][...], pre_grad_ref[rows:, cut])
        up_sum_ref[:, cut] = total.astype(BF16)
    if fetched:
        up_sent_ref[...] = sum_ref[rows_at(1 - place_ref[2], width // 2), :]
        up_kept_ref[...] = sum_ref[rows_at(place_ref[2], width // 2), :]
    for block in range(units // BLOCK):
        cut = slice(block * BLOCK, (block + 1) * BLOCK)
        total = contract_rows(hidden_ref[:rows, cut], upstreams[0][rows:, :]) + contract_rows(hidden_ref[rows:, cut], upstreams[1][rows:, :])
        down_sum_ref[cut, :] = total.astype(BF16)
    if fetched:
        down_sent_ref[...] = sum_ref[rows_at(1 - place_ref[1], half), :]
        down_kept_ref[...] = sum_ref[rows_at(place_ref[1], half), :]


def hidden_part(place, entries, upstreams, weights, others, fetched):
    rows, width = entries[0].shape
    units = weights[0].shape[1]
    inputs = [*entries, *upstreams, *weights, *others]
    outs = [kept((rows, width), F32), shape((rows, width), BF16) if fetched else kept((rows, width), F32)]
    outs += [kept((2 * rows, units), BF16), shape((8, units), F32)]
    if fetched:
        outs += [kept((width // 2, units), BF16), shape((width // 2, units), BF16)]
        outs += [kept((units // 2, width), BF16), shape((units // 2, width), BF16)]
        outs += [kept((width, units), BF16), kept((units, width), BF16)]
    else:
        outs += [kept((width, units), BF16), kept((units, width), BF16)]
    return pl.pallas_call(
        partial(hidden_kernel, fetched=fetched),
        out_shape=tuple(outs),
        in_specs=[in_smem()] + [in_vmem()] * len(inputs),
        out_specs=(in_vmem(),) * len(outs),
        scratch_shapes=[pltpu.VMEM((2 * rows, units), BF16)] + [pltpu.VMEM((width, units), BF16)] * fetched,
        compiler_params=parameters(24),
        cost_estimate=cost(10, 2**23),
        name="hidden_part",
    )(place, *inputs)


def hidden_out_kernel(hidden_ref, hidden_x_ref, down_ref, down_x_ref, out_ref, *, part):
    rows = out_ref.shape[0]

    def tile(step, carry):
        there = pl.ds(pl.multiple_of(part * rows + step * BLOCK, BLOCK), BLOCK)
        out = dot(hidden_ref[there, :], down_ref[...]) + dot(hidden_x_ref[there, :], down_x_ref[...])
        out_ref[rows_at(step, BLOCK), :] = out.astype(out_ref.dtype)
        return carry

    lax.fori_loop(0, rows // BLOCK, tile, 0)


def hidden_out(hidden, hidden_x, down, down_x, part, kind):
    rows, width = hidden.shape[0] // 2, down.shape[1]
    return pl.pallas_call(
        partial(hidden_out_kernel, part=part),
        out_shape=shape((rows, width), kind),
        in_specs=[in_vmem()] * 4,
        out_specs=in_vmem(),
        compiler_params=parameters(12),
        cost_estimate=cost(2, 2**22),
        name="hidden_out",
    )(hidden, hidden_x, down, down_x)


ROWS = 128


def row_wise(body, name, row_inputs, whole_inputs, row_outs, sums, micros):
    rows, width = row_inputs[0].shape
    block = pl.BlockSpec((ROWS, width), lambda i: (i, 0))
    whole = [pl.BlockSpec(array.shape, lambda i: (0, 0)) for array in whole_inputs]
    outs = [shape((rows, width), kind) for kind in row_outs]
    out_specs = [block] * len(outs)
    if sums:
        outs.append(shape((8, width), F32))
        out_specs.append(pl.BlockSpec((8, width), lambda i: (0, 0)))

    def kernel(*refs):
        refs = list(refs)
        row_refs = [refs.pop(0) for _ in row_inputs]
        whole_refs = [refs.pop(0) for _ in whole_inputs]
        results, terms = body(*[ref[...] for ref in row_refs], *whole_refs)
        for ref, result in zip(refs, results):
            ref[...] = result.astype(ref.dtype)
        if sums:
            total = jnp.concatenate(
                [jnp.sum(term, axis=0, keepdims=True) for term in terms] + [jnp.zeros((8 - sums, width), F32)], axis=0
            )
            first = pl.program_id(0) == 0

            @pl.when(first)
            def _():
                refs[-1][...] = total

            @pl.when(jnp.logical_not(first))
            def _():
                refs[-1][...] += total

    return pl.pallas_call(
        kernel,
        grid=(rows // ROWS,),
        out_shape=tuple(outs),
        in_specs=[block] * len(row_inputs) + whole,
        out_specs=tuple(out_specs),
        compiler_params=parameters(12),
        cost_estimate=cost(micros, 2**20),
        name=name,
    )(*row_inputs, *whole_inputs)


def enter_kernel(place_ref, time_ref, tokens_ref, cotangent_ref, weight_ref, *refs):
    vectors, (table_ref, both_ref) = refs[:-2], refs[-2:]
    rows, width = tokens_ref.shape
    table_ref[...] = jnp.zeros_like(table_ref)
    row = 0
    for vector in vectors:
        for at in range(0, vector.shape[0], width // LANES):
            table_ref[row : row + 1, :] = one_line(vector, at, width)
            row += 1
    features = time_features(time_ref[place_ref[3]], 0, COND)
    for piece in range(6):
        cut = slice(piece * width, (piece + 1) * width)
        table_ref[piece : piece + 1, :] += jnp.sum(features * weight_ref[:, cut], axis=0, keepdims=True)
    table_ref[row : row + 1, :COND] = time_features(time_ref[place_ref[3]], 1, COND)
    table = table_ref[...]

    def tile(step, carry):
        here = rows_at(step, ROWS)
        scored, _ = standard_score_rows(tokens_ref[here, :].astype(F32))
        entry = scored * table[6:7] * (1.0 + table[1:2]) + table[0:1]
        both_ref[here, :] = entry.astype(BF16)
        there = pl.ds(pl.multiple_of(rows + step * ROWS, ROWS), ROWS)
        both_ref[there, :] = (table[5:6] * cotangent_ref[here, :].astype(F32)).astype(BF16)
        return carry

    lax.fori_loop(0, rows // ROWS, tile, 0)


def enter(place, time_index, tokens, cotangent, weight, vectors):
    vectors = [vector.reshape(-1, LANES) for vector in vectors]
    rows, width = tokens.shape
    return pl.pallas_call(
        enter_kernel,
        out_shape=(shape((16, width), F32), shape((2 * rows, width), BF16)),
        in_specs=[in_smem()] * 2 + [in_vmem()] * (3 + len(vectors)),
        out_specs=(in_vmem(),) * 2,
        compiler_params=parameters(14),
        cost_estimate=cost(4, 2**22),
        name="enter",
    )(place, time_index, in_hbm(tokens), in_hbm(cotangent), in_hbm(weight), *[in_hbm(vector) for vector in vectors])


def enter_second(tokens, branch_own, branch_other, modulation):
    branch = branch_own + branch_other.astype(F32)
    middle = tokens.astype(F32) + modulation[2:3, :] * branch
    scored, _ = standard_score_rows(middle)
    entry = scored * modulation[7:8, :] * (1.0 + modulation[4:5, :]) + modulation[3:4, :]
    return (middle, entry), ()


def leave(middle, cotangent, out_own, out_other, modulation):
    branch = out_own + out_other.astype(F32) + modulation[8:9, :]
    incoming = cotangent.astype(F32)
    branch_grad = (modulation[5:6, :] * incoming).astype(BF16).astype(F32)
    return (middle + modulation[5:6, :] * branch,), (incoming * branch, branch_grad)


def back_second(middle, cotangent, grad_own, grad_other, branch_own, branch_other, modulation):
    gain = modulation[7:8, :]
    scored, inverse = standard_score_rows(middle)
    entry_grad = grad_own + grad_other.astype(F32)
    normed_grad = entry_grad * (1.0 + modulation[4:5, :])
    middle_grad = cotangent.astype(F32) + norm_reverse_pass(normed_grad * gain, scored, inverse)
    branch = branch_own + branch_other.astype(F32)
    terms = (middle_grad * branch, entry_grad, entry_grad * (scored * gain), normed_grad * scored)
    return (modulation[2:3, :] * middle_grad, middle_grad), terms


def back_first(tokens, grad_own, grad_other, middle_grad, modulation):
    gain = modulation[6:7, :]
    scored, inverse = standard_score_rows(tokens.astype(F32))
    entry_grad = grad_own + grad_other.astype(F32)
    normed_grad = entry_grad * (1.0 + modulation[1:2, :])
    grad = middle_grad + norm_reverse_pass(normed_grad * gain, scored, inverse)
    return (grad,), (entry_grad, entry_grad * (scored * gain), normed_grad * scored)


def piece_kernel(place_ref, source_ref, *refs, rows, bit):
    if len(refs) == 2:
        refs[1][rows:, :] = jnp.zeros_like(refs[1][rows:, :])
        refs[1][rows : rows + 1, :] = one_line(refs[0], 0, refs[1].shape[1])
    refs[-1][:rows, :] = source_ref[rows_at(place_ref[bit], rows), :]


def own_piece(place, source, rows, bit, line=None):
    extra = [] if line is None else [line.reshape(-1, LANES)]
    return pl.pallas_call(
        partial(piece_kernel, rows=rows, bit=bit),
        out_shape=shape((rows + 16 * len(extra), source.shape[1]), source.dtype),
        in_specs=[in_smem()] + [in_vmem()] * (1 + len(extra)),
        out_specs=in_vmem(),
        compiler_params=parameters(8),
        cost_estimate=small_cost(),
        name="own_piece",
    )(place, in_hbm(source), *extra)


def lower_half(source):
    rows, width = source.shape

    def kernel(source_ref, out_ref):
        out_ref[...] = source_ref[rows // 2 :, :]

    return pl.pallas_call(
        kernel,
        out_shape=shape((rows // 2, width), source.dtype),
        in_specs=[in_vmem()],
        out_specs=in_vmem(),
        compiler_params=parameters(8),
        cost_estimate=small_cost(),
        name="lower_half",
    )(in_hbm(source))


def place_kernel(place_ref, token_ref, out_ref):
    for k in range(out_ref.shape[0]):
        out_ref[k] = place_ref[k]


def place_after(place, token):
    return pl.pallas_call(
        place_kernel,
        out_shape=shape(place.shape, place.dtype),
        in_specs=[in_smem(), anywhere()],
        out_specs=in_smem(),
        compiler_params=parameters(8),
        cost_estimate=cost(10, 2**18),
        name="place_after",
    )(place, token)


def sum_kernel(place_ref, a_ref, b_ref, kept_ref, sent_ref, *, bit):
    half = kept_ref.shape[0]
    for out, index in ((sent_ref, 1 - place_ref[bit]), (kept_ref, place_ref[bit])):
        here = rows_at(index, half)
        out[...] = (a_ref[here, :].astype(F32) + b_ref[here, :].astype(F32)).astype(BF16)


def summed(place, a, b, bit):
    rows, width = a.shape
    return pl.pallas_call(
        partial(sum_kernel, bit=bit),
        out_shape=(shape((rows // 2, width), BF16),) * 2,
        in_specs=[in_smem(), in_vmem(), in_vmem()],
        out_specs=(in_vmem(),) * 2,
        compiler_params=parameters(8),
        cost_estimate=small_cost(3),
        name="summed",
    )(place, a, b)


def total_kernel(a_ref, b_ref, out_ref):
    out_ref[...] = (a_ref[...].astype(F32) + b_ref[...].astype(F32)).astype(BF16)


def total_of(a, b):
    return pl.pallas_call(
        total_kernel,
        out_shape=shape(a.shape, BF16),
        in_specs=[in_vmem()] * 2,
        out_specs=in_vmem(),
        compiler_params=parameters(8),
        cost_estimate=small_cost(3),
        name="total_of",
    )(a, b)


def pair_kernel(place_ref, a_ref, b_ref, kept_a_ref, kept_b_ref, sent_ref, *, bit):
    half = kept_a_ref.shape[0]
    mine, other = rows_at(place_ref[bit], half), rows_at(1 - place_ref[bit], half)
    sent_ref[:half, :] = a_ref[other, :]
    sent_ref[half:, :] = b_ref[other, :]
    kept_a_ref[...] = a_ref[mine, :]
    kept_b_ref[...] = b_ref[mine, :]


def pair_halves(place, a, b, bit):
    rows, width = a.shape
    half = shape((rows // 2, width), BF16)
    return pl.pallas_call(
        partial(pair_kernel, bit=bit),
        out_shape=(half, half, shape((rows, width), BF16)),
        in_specs=[in_smem(), in_vmem(), in_vmem()],
        out_specs=(in_vmem(),) * 3,
        compiler_params=parameters(8),
        cost_estimate=small_cost(3),
        name="pair_halves",
    )(place, a, b)


def halves_kernel(place_ref, source_ref, kept_ref, sent_ref, *, bit):
    half = kept_ref.shape[0]
    sent_ref[...] = source_ref[rows_at(1 - place_ref[bit], half), :]
    kept_ref[...] = source_ref[rows_at(place_ref[bit], half), :]


def halves(place, source, bit):
    rows, width = source.shape
    return pl.pallas_call(
        partial(halves_kernel, bit=bit),
        out_shape=(shape((rows // 2, width), BF16),) * 2,
        in_specs=[in_smem(), in_vmem()],
        out_specs=(in_vmem(),) * 2,
        compiler_params=parameters(8),
        cost_estimate=small_cost(3),
        name="halves",
    )(place, source)


def pair_total_kernel(a_ref, b_ref, got_ref, out_a_ref, out_b_ref):
    half = a_ref.shape[0]
    out_b_ref[...] = (b_ref[...].astype(F32) + got_ref[half:, :].astype(F32)).astype(BF16)
    out_a_ref[...] = (a_ref[...].astype(F32) + got_ref[:half, :].astype(F32)).astype(BF16)


def pair_total(a, b, got):
    return pl.pallas_call(
        pair_total_kernel,
        out_shape=(shape(a.shape, BF16),) * 2,
        in_specs=[in_vmem()] * 3,
        out_specs=(in_vmem(),) * 2,
        compiler_params=parameters(8),
        cost_estimate=small_cost(3),
        name="pair_total",
    )(a, b, got)


def two_totals_kernel(a_ref, b_ref, c_ref, d_ref, first_ref, second_ref):
    first_ref[...] = (a_ref[...].astype(F32) + b_ref[...].astype(F32)).astype(BF16)
    second_ref[...] = (c_ref[...].astype(F32) + d_ref[...].astype(F32)).astype(BF16)


def two_totals(a, b, c, d):
    return pl.pallas_call(
        two_totals_kernel,
        out_shape=(shape(a.shape, BF16), shape(c.shape, BF16)),
        in_specs=[in_vmem()] * 4,
        out_specs=(in_vmem(),) * 2,
        compiler_params=parameters(8),
        cost_estimate=small_cost(3),
        name="two_totals",
    )(a, b, c, d)


def lay_kernel(place_ref, *refs, bit, cuts, ahead):
    if ahead:
        before_ref, *refs = refs
    outs, whole_ref = refs[2:-1], refs[-1]
    rows = refs[0].shape[0]
    for ref, index in zip(refs, (place_ref[bit], 1 - place_ref[bit])):
        whole_ref[rows_at(index, rows), :] = ref[...].astype(whole_ref.dtype)
    for out, (first, last) in zip(outs, cuts):
        at = out.shape[0] - (last - first)
        if at:
            out[:at, :] = before_ref[...]
        out[at:, :] = whole_ref[first:last, :]


def lay_straight_kernel(place_ref, own_ref, other_ref, out_ref, *, bit):
    rows = own_ref.shape[0]
    for ref, index in ((own_ref, place_ref[bit]), (other_ref, 1 - place_ref[bit])):
        out_ref[rows_at(index, rows), :] = ref[...].astype(out_ref.dtype)


def lay(place, own, other, bit, kind, cuts=None, before=None):
    rows, width = own.shape
    total = 2 * rows
    straight = cuts is None and before is None
    cuts = cuts or ((0, total),)
    at = 0 if before is None else before.shape[0]
    outs = [shape((last - first + (at if k == 0 else 0), width), kind) for k, (first, last) in enumerate(cuts)]
    inputs = [*([] if before is None else [before]), own, other]
    kernel = partial(lay_straight_kernel, bit=bit) if straight else partial(lay_kernel, bit=bit, cuts=cuts, ahead=before is not None)
    return pl.pallas_call(
        kernel,
        out_shape=tuple(outs),
        in_specs=[in_smem()] + [in_vmem()] * len(inputs),
        out_specs=(in_vmem(),) * len(outs),
        scratch_shapes=[] if straight else [pltpu.VMEM((total, width), kind)],
        compiler_params=parameters(14),
        cost_estimate=small_cost(3),
        name="lay",
    )(place, *inputs)


TABLE = 16


def tabulate_kernel(first_ref, second_ref, last_ref, table_ref, bias_ref, bias_x_ref, out_ref):
    rows = [first_ref[0:2, :], second_ref[0:3, :], last_ref[0:1, :], first_ref[2:3, :], second_ref[3:4, :], last_ref[1:2, :]]
    rows += [table_ref[9:10, :], bias_ref[0:1, :], bias_x_ref[0:1, :], jnp.zeros((TABLE - 12, out_ref.shape[1]), F32)]
    out_ref[...] = jnp.concatenate(rows, axis=0)


def tabulate(*parts):
    return pl.pallas_call(
        tabulate_kernel,
        out_shape=shape((TABLE, parts[0].shape[1]), F32),
        in_specs=[in_vmem()] * 6,
        out_specs=in_vmem(),
        compiler_params=parameters(8),
        cost_estimate=cost(1, 2**18),
        name="tabulate",
    )(*parts)


def lay_table(out_ref, at, own, other, side):
    rows = own.shape[0]
    out_ref[pl.ds(pl.multiple_of(at + side * rows, TABLE), rows), :] = own
    out_ref[pl.ds(pl.multiple_of(at + (1 - side) * rows, TABLE), rows), :] = other


def ride_first_kernel(kept_ref, kept_x_ref, got_ref, own_ref, near_ref, part_ref, table_ref, out_ref):
    half = kept_ref.shape[0]
    own = own_ref[...]
    row = lax.broadcasted_iota(jnp.int32, own.shape, 0)
    table = jnp.where(row < 9, own + near_ref[...], own).astype(BF16)
    out_ref[:half, :] = (kept_x_ref[...].astype(F32) + got_ref[half:, :].astype(F32)).astype(BF16)
    out_ref[half:, :] = table
    table_ref[...] = table
    part_ref[...] = (kept_ref[...].astype(F32) + got_ref[:half, :].astype(F32)).astype(BF16)


def ride_half_kernel(place_ref, part_ref, got_ref, table_ref, kept_ref, next_ref, out_ref):
    half, rows = kept_ref.shape[0], table_ref.shape[0]
    mine, other = rows_at(place_ref[2], half), rows_at(1 - place_ref[2], half)
    out_ref[:half, :] = (part_ref[other, :].astype(F32) + got_ref[other, :].astype(F32)).astype(BF16)
    kept_ref[...] = (part_ref[mine, :].astype(F32) + got_ref[mine, :].astype(F32)).astype(BF16)
    lay_table(next_ref, 0, table_ref[...], got_ref[2 * half :, :], place_ref[3])
    out_ref[half:, :] = next_ref[...]


def ride_add_kernel(place_ref, value_ref, got_ref, table_ref, sum_ref, next_ref, *outs, bit):
    rows = value_ref.shape[0]
    total = (value_ref[...].astype(F32) + got_ref[:rows, :].astype(F32)).astype(BF16)
    sum_ref[...] = total
    lay_table(next_ref, 0, table_ref[...], got_ref[rows:, :], place_ref[bit])
    for out in outs:
        out[:rows, :] = total
        out[rows:, :] = next_ref[...]


def ride_lay_kernel(place_ref, own_ref, other_ref, table_ref, out_ref):
    rows = own_ref.shape[0]
    for ref, index in ((own_ref, place_ref[2]), (other_ref, 1 - place_ref[2])):
        out_ref[rows_at(index, rows), :] = ref[...]
    out_ref[2 * rows :, :] = table_ref[...]


def ride(kernel, name, outs, *inputs):
    scalars = [in_smem()] if inputs[0].ndim == 1 else []
    return pl.pallas_call(
        kernel,
        out_shape=tuple(shape(dims, BF16) for dims in outs),
        in_specs=scalars + [in_vmem()] * (len(inputs) - len(scalars)),
        out_specs=(in_vmem(),) * len(outs),
        compiler_params=parameters(8),
        cost_estimate=small_cost(3),
        name=name,
    )(*inputs)


def hold_kernel(source_ref, out_ref):
    out_ref[...] = source_ref[...]


def hold(value):
    return pl.pallas_call(
        hold_kernel,
        out_shape=kept(value.shape, value.dtype),
        in_specs=[in_vmem()],
        out_specs=in_vmem(),
        compiler_params=parameters(8),
        cost_estimate=cost(3, 2**18),
        name="hold",
    )(value)


def finish_kernel(place_ref, own_ref, got_ref, before_ref, sum_ref, grad_ref, totals_ref, line_ref, *, half):
    ahead = before_ref.shape[0]
    sum_ref[:ahead, :] = before_ref[...]
    for ref, index in ((own_ref, place_ref[1]), (got_ref, 1 - place_ref[1])):
        sum_ref[pl.ds(pl.multiple_of(ahead + index * half, 16), half), :] = ref[:half, :].astype(F32)
    slots, width = (own_ref.shape[0] - half) // TABLE, own_ref.shape[1]
    for ref, index in ((own_ref, place_ref[1]), (got_ref, 1 - place_ref[1])):

        def one_slot(slot, carry, ref=ref, index=index):
            lines = ref[pl.ds(pl.multiple_of(half + slot * TABLE, TABLE), TABLE), :].astype(F32)
            for row in range(12):
                line_ref[row, pl.ds(index * slots + slot, 1), :] = lines[row : row + 1]
            return carry

        lax.fori_loop(0, slots, one_slot, 0)
    features = line_ref[9][:, :COND].astype(BF16)
    totals_ref[...] = jnp.zeros_like(totals_ref)
    for piece in range(9):
        terms = line_ref[piece]
        totals_ref[piece : piece + 1, :] = jnp.sum(terms, axis=0, keepdims=True)
        if piece < 6:
            grad_ref[:, piece * width : (piece + 1) * width] = contract_rows(features, terms.astype(BF16))
    slot = lax.broadcasted_iota(jnp.int32, (2 * slots, width), 0)
    mine = lax.rem(slot, 2) == place_ref[3]
    totals_ref[9:10, :] = jnp.sum(jnp.where(mine, line_ref[10], line_ref[11]), axis=0, keepdims=True)


def finish(place, own, got, before, half):
    width = own.shape[1]
    slots = 2 * (own.shape[0] - half) // TABLE
    return pl.pallas_call(
        partial(finish_kernel, half=half),
        out_shape=(
            shape((before.shape[0] + 2 * half, width), F32),
            shape((COND, 6 * width), F32),
            shape((TABLE, width), F32),
        ),
        in_specs=[in_smem()] + [in_vmem()] * 3,
        out_specs=(in_vmem(),) * 3,
        scratch_shapes=[pltpu.VMEM((12, slots, width), F32)],
        compiler_params=parameters(20),
        cost_estimate=cost(3, 2**20),
        name="finish",
    )(place, own, got, before)


class Order:
    def __init__(self):
        self.token = ()

    def __call__(self, value):
        return after(value, *self.token) if self.token else value

    def done(self, result):
        self.token = (result[-1] if isinstance(result, (tuple, list)) else result,)
        return result


def dp_bits():
    bits = []
    bit = 1
    while bit < lax.axis_size("dp"):
        bits.append(bit)
        bit *= 2
    return bits


def per_device(
    tokens,
    cotangent,
    doc_lengths,
    time_index,
    attention_norm_gain,
    qkv_weight,
    out_weight,
    feedforward_norm_gain,
    up_weight,
    up_bias,
    down_weight,
    down_bias,
    ada_weight,
    ada_bias,
):
    rows, width = tokens.shape
    core = lax.axis_index("mp") % 2
    slot = lax.axis_index("mp") // 2
    index = lax.axis_index("dp")
    bits = dp_bits()
    place = [core, index % 2, index // 2 % 2, slot] + [index // bit % 2 for bit in bits[2:]]
    place = jnp.stack(place).astype(jnp.int32)
    order = Order()

    def near(value):
        return swap(value, "mp", 1)

    def across(value):
        return swap(value, "mp", 2)

    def relayed(value):
        return swap(value, "dp", 1)

    qkv_turned = qkv_weight.T
    qkv_half = order.done(own_piece(place, qkv_turned, qkv_turned.shape[0] // 2, 1))
    qkv_a = across(qkv_half)
    table, both = order.done(
        enter(
            place,
            time_index,
            order(tokens),
            cotangent,
            ada_weight,
            (ada_bias, attention_norm_gain, feedforward_norm_gain, down_bias),
        )
    )
    both_near = near(both)
    out_weight_x = across(order(out_weight))
    up_half = order.done(own_piece(place, order(up_weight), width // 2, 1))
    up_a = across(up_half)
    quarter = down_weight.shape[0] // 4
    down_part = order.done(own_piece(place, order(down_weight), quarter, 2, up_bias))
    down_a = across(down_part)
    down_lower = order.done(lower_half(order(down_weight)))
    place = order.done(place_after(order(place), qkv_a))
    qkv_b = swap(qkv_a, "dp", 1)

    query, key, value, mixture, entry_one_all = order.done(
        attend_forward(place, doc_lengths, order(both), both_near, (qkv_turned,), True)
    )
    down_straight = across(order(down_lower))
    query_x, key_x, value_x, mixture_x = order.done(
        attend_forward(place, doc_lengths, order(both), both_near, (qkv_a, qkv_b), False)
    )
    branch_own, branch_other = order.done(project_out(place, mixture, order(mixture_x), out_weight, out_weight_x))
    branch_other = near(branch_other)
    grad_one = order.done(hidden_grad(order(both), down_weight))
    up_b = swap(after(up_a, grad_one), "dp", 1)
    middle, entry_two = order.done(
        row_wise(
            enter_second, "enter_second", (order(tokens), branch_own, after(branch_other, up_a)), (table,), (F32, BF16), 0, 3
        )
    )
    entry_two_near = near(entry_two)
    grad_two = order.done(hidden_grad(order(both_near), down_weight))
    down_b = swap(after(down_a, grad_two), "dp", 2)
    entries_two = (entry_two, after(entry_two_near, down_a))

    grad_base, grad_base_near, hidden, bias_sum, up_sum, down_sum = order.done(
        hidden_part(
            place,
            entries_two,
            (order(both), both_near),
            (up_weight, up_bias.reshape(-1, LANES)),
            (grad_one, grad_two),
            False,
        )
    )
    grad_own, grad_other, hidden_x, bias_sum_x, up_kept_x, up_sent_x, down_kept_x, down_sent_x, _, down_weight_x = order.done(
        hidden_part(
            place,
            (order(entries_two[0]), entries_two[1]),
            (both, both_near),
            (up_a, up_b, down_a, down_b, down_straight),
            (grad_base, grad_base_near),
            True,
        )
    )
    grad_other = near(grad_other)
    out_other = order.done(hidden_out(order(hidden), hidden_x, down_weight, down_weight_x, 1, BF16))
    out_other = near(out_other)
    down_got_x = swap(order(down_sent_x), "dp", 1)
    up_got_x = swap(order(up_sent_x), "dp", 2)
    attn_grad, middle_grad, sums_two = order.done(
        row_wise(
            back_second,
            "back_second",
            (order(middle), cotangent, grad_own, grad_other, branch_own, branch_other),
            (table,),
            (BF16, F32),
            4,
            4,
        )
    )
    attn_grad_near = near(attn_grad)
    out_own = order.done(hidden_out(order(hidden), hidden_x, down_weight, down_weight_x, 0, F32))
    mixture_grad, mixture_grad_x, out_sum, out_sum_x = order.done(
        project_back(place, order(attn_grad), after(attn_grad_near, out_other), mixture, mixture_x, out_weight, out_weight_x)
    )
    down_kept, down_sent = order.done(halves(place, order(down_sum), 1))
    down_got = swap(down_sent, "dp", 1)
    up_kept, up_sent = order.done(halves(place, order(up_sum), 2))
    up_got = swap(up_sent, "dp", 2)

    sides = ((query, key, value, mixture, mixture_grad), (query_x, key_x, value_x, mixture_x, mixture_grad_x))

    def backward(head, extras):
        return order.done(
            attend_backward(place, doc_lengths, head, 1, sides, order(entry_one_all), extras)
        )

    def on(value, step=0):
        return swap(value, "dp", bits[2 + step])

    def doubled(value, got):
        for step in range(len(bits) - 2):
            value = order.done(total_of(order(value), got))
            if step + 3 < len(bits):
                got = on(value, step + 1)
        return value

    back_0, first_sum, back_x_0, first_sum_x = backward(0, (out_sum, out_sum_x))
    down_part_x = order.done(total_of(order(down_kept_x), down_got_x))
    down_got_x = across(down_part_x)
    back_1, head_sum, back_x_1, head_sum_x = backward(1, ())
    up_part_x = order.done(total_of(order(up_kept_x), up_got_x))
    up_got_x = across(up_part_x)
    up_part, down_part = order.done(two_totals(order(up_kept), up_got, down_kept, down_got))
    back_2, rest_sum, back_x_2, rest_sum_x = backward(2, (head_sum, head_sum_x))
    rest_kept, rest_kept_x, rest_sent = order.done(pair_halves(place, order(rest_sum), rest_sum_x, 1))
    rest_got = swap(rest_sent, "dp", 1)
    down_kept, down_sent = order.done(summed(place, order(down_part), down_got_x, 2))
    down_got = swap(down_sent, "dp", 2)
    first_own, first_other = order.done(
        entry_back(
            place, (order(back_0), back_1, back_2), (back_x_0, back_x_1, back_x_2), qkv_turned, (qkv_a, qkv_b)
        )
    )
    first_other = near(first_other)
    output, sums_out = order.done(
        row_wise(leave, "leave", (order(middle), cotangent, out_own, out_other), (table,), (BF16,), 2, 3)
    )
    input_gradient, sums_one = order.done(
        row_wise(
            back_first, "back_first", (order(tokens), first_own, first_other, middle_grad), (table,), (F32,), 3, 3
        )
    )
    sums = order.done(tabulate(order(sums_one), sums_two, sums_out, table, bias_sum, bias_sum_x))
    sums_near = near(sums)
    up_kept, up_sent = order.done(summed(place, order(up_part), up_got_x, 1))
    up_got = swap(up_sent, "dp", 1)
    down_value = order.done(total_of(order(down_kept), down_got))
    down_got = on(down_value)
    rows_x, rows_z = rest_kept.shape[0], rest_kept.shape[0] // 2
    rest_part, slots, sent = order.done(
        ride(
            ride_first_kernel,
            "ride_first",
            ((rows_x, width), (TABLE, width), (rows_x + TABLE, width)),
            order(rest_kept),
            rest_kept_x,
            rest_got,
            sums,
            sums_near,
        )
    )
    rest_got = across(sent)
    first_kept, first_kept_x, first_sent = order.done(pair_halves(place, order(first_sum), first_sum_x, 1))
    first_got = swap(first_sent, "dp", 1)
    up_value = order.done(total_of(order(up_kept), up_got))
    up_got = on(up_value)
    rest_value, slots, sent = order.done(
        ride(
            ride_half_kernel,
            "ride_half",
            ((rows_z, width), (2 * TABLE, width), (rows_z + 2 * TABLE, width)),
            place,
            order(rest_part),
            rest_got,
            slots,
        )
    )
    rest_got = swap(sent, "dp", 2)
    slots = order.done(hold(order(slots)))
    for step in range(len(bits) - 1):
        last = step == len(bits) - 2
        held = (2 * slots.shape[0], width)
        outs = ((rows_z, width), held) if last else ((rows_z, width), held, (rows_z + held[0], width))
        results = order.done(
            ride(
                partial(ride_add_kernel, bit=2 if step == 0 else 3 + step),
                "ride_add",
                outs,
                place,
                order(rest_value),
                rest_got,
                slots,
            )
        )
        rest_value, slots = results[:2]
        rest_got = swap(rest_value, "dp", 2) if last else on(results[2], step)
        if step == 0:
            down_value = doubled(down_value, down_got)
            down_got = swap(down_value, "dp", 2)
            first_part_x, first_part = order.done(pair_total(order(first_kept), first_kept_x, first_got)[::-1])
            first_got = across(first_part_x)
            up_value = doubled(up_value, up_got)
            up_got = swap(up_value, "dp", 1)
            first_kept, first_sent = order.done(summed(place, order(first_part), first_got, 2))
            first_got = swap(first_sent, "dp", 2)
            (down_value,) = order.done(lay(place, order(down_value), down_got, 2, BF16))
            down_got = swap(down_value, "dp", 1)
    first_value = order.done(total_of(order(first_kept), first_got))
    first_got = on(first_value)
    (up_value,) = order.done(lay(place, order(up_value), up_got, 1, BF16))
    up_got = swap(up_value, "dp", 2)
    (rest_all,) = order.done(
        ride(
            ride_lay_kernel,
            "ride_lay",
            ((rows_x + slots.shape[0], width),),
            place,
            order(rest_value),
            rest_got,
            slots,
        )
    )
    rest_got = swap(rest_all, "dp", 1)
    first_value = doubled(first_value, first_got)
    first_got = swap(first_value, "dp", 2)
    (down_grad,) = order.done(lay(place, order(down_value), down_got, 1, F32))
    (first_value,) = order.done(lay(place, order(first_value), first_got, 2, BF16))
    first_got = swap(first_value, "dp", 1)
    (up_grad,) = order.done(lay(place, order(up_value), up_got, 2, F32))
    out_rows = out_weight.shape[0]
    out_grad, head_grad = order.done(
        lay(place, order(first_value), first_got, 1, F32, cuts=((0, out_rows), (out_rows, first_sum.shape[0])))
    )
    qkv_grad, ada_grad, totals = order.done(finish(place, order(rest_all), rest_got, head_grad, rows_x))
    return (
        output,
        input_gradient,
        totals[6],
        qkv_grad.T,
        out_grad,
        totals[7],
        up_grad,
        totals[9],
        down_grad,
        totals[8],
        ada_grad,
        totals[:6].reshape(6 * width),
    )


def solution(mesh):
    in_specs = (
        P(("dp", "mp"), None),
        P(("dp", "mp"), None),
        P("dp", None),
        P("dp"),
        P(),
        P(None, "mp"),
        P("mp", None),
        P(),
        P(None, "mp"),
        P("mp"),
        P("mp", None),
        P(),
        P(),
        P(),
    )
    out_specs = (
        P(("dp", "mp"), None),
        P(("dp", "mp"), None),
        P(),
        P(None, "mp"),
        P("mp", None),
        P(),
        P(None, "mp"),
        P("mp"),
        P("mp", None),
        P(),
        P(),
        P(),
    )
    return jax.shard_map(
        per_device, mesh=mesh, in_specs=in_specs, out_specs=out_specs, check_vma=False
    )
```

```python
from functools import partial
import math

import jax
import jax.numpy as jnp
from jax import lax
from jax.experimental import pallas as pl
from jax.experimental.pallas import tpu as pltpu
from jax.sharding import PartitionSpec as P

HEAD_DIM = 64
COND = 128
BLOCK = 256
STEP = 128
LANES = 128
BF16 = jnp.bfloat16
F32 = jnp.float32
TANH_SCALE = math.sqrt(2 / math.pi)
TANH_CUBE = 0.044715


def swap(value, axis, bit):
    size = lax.axis_size(axis)
    return lax.ppermute(value, axis, [(i, i ^ bit) for i in range(size)])


def time_features(time, axis, cond_width):
    half_width = cond_width // 2
    dims = (cond_width, 1) if axis == 0 else (1, cond_width)
    place = lax.broadcasted_iota(jnp.int32, dims, axis)
    second = place >= half_width
    ladder = jnp.where(second, place - half_width, place).astype(F32)
    angles = time.astype(F32) * jnp.exp(ladder * (-math.log(10000.0) / half_width))
    waves = jnp.where(second, jnp.sin(angles), jnp.cos(angles))
    return waves / (1.0 + jnp.exp(-waves))


def standard_score_rows(values):
    center = values - jnp.mean(values, axis=-1, keepdims=True)
    inverse_deviation = lax.rsqrt(jnp.mean(center * center, axis=-1, keepdims=True) + 1e-05)
    return (center * inverse_deviation, inverse_deviation)


def norm_reverse_pass(incoming_gradient, centered_scaled, inverse_deviation):
    return inverse_deviation * (
        incoming_gradient
        - jnp.mean(incoming_gradient, axis=-1, keepdims=True)
        - centered_scaled * jnp.mean(incoming_gradient * centered_scaled, axis=-1, keepdims=True)
    )


def dot(a, b):
    return jnp.dot(a, b, preferred_element_type=F32)


def contract_rows(a, b):
    return lax.dot_general(a, b, (((0,), (0,)), ((), ())), preferred_element_type=F32)


def times_transposed(a, b):
    return lax.dot_general(a, b, (((1,), (1,)), ((), ())), preferred_element_type=F32)


def one_line(lines_ref, first, width):
    return jnp.concatenate([lines_ref[first + k : first + k + 1, :] for k in range(width // LANES)], axis=1)


def in_vmem():
    return pl.BlockSpec(memory_space=pltpu.VMEM)


def in_smem():
    return pl.BlockSpec(memory_space=pltpu.SMEM)


def in_hbm(value):
    return pltpu.with_memory_space_constraint(value, pltpu.HBM)


def kept(dims, kind):
    return pltpu.VMEM(dims, kind)


def shape(dims, kind):
    return jax.ShapeDtypeStruct(dims, kind)


def cost(micros, size):
    return pl.CostEstimate(flops=int((micros + 12) * 1.1e9), bytes_accessed=size, transcendentals=0)


def small_cost(micros=0.001):
    return pl.CostEstimate(flops=int(micros * 1.1e9), bytes_accessed=10**4, transcendentals=0)


def parameters(mebibytes):
    return pltpu.CompilerParams(vmem_limit_bytes=mebibytes * 2**20)


def anywhere():
    return pl.BlockSpec(memory_space=pl.ANY)


def after(value, *tokens):
    return lax.optimization_barrier((value, *tokens))[0]


def rows_at(index, count):
    return pl.ds(pl.multiple_of(index * count, count), count)


def joined(target, pieces, mine, direct=0):
    rows = (target.shape[0] - direct) // 2
    for piece, index in zip(pieces, (mine, 1 - mine)):
        target[rows_at(index, rows), :] = piece[:rows, :]
    if direct:
        target[2 * rows :, :] = pieces[2][...]


def window_sizes(slot_length):
    return tuple(range(2 * STEP, slot_length + 1, STEP))


def block_window(lengths_ref, slot, block, slot_length):
    first = block * BLOCK
    last = first + BLOCK - 1
    end = jnp.int32(0)
    low = jnp.int32(0)
    high = jnp.int32(slot_length)
    for document in range(lengths_ref.shape[1]):
        end = end + lengths_ref[slot, document]
        low = jnp.where(end <= first, jnp.maximum(low, end), low)
        high = jnp.where(end > last, jnp.minimum(high, end), high)
    low = lax.div(low, jnp.int32(STEP)) * STEP
    size = jnp.maximum(lax.div(high - low + (STEP - 1), jnp.int32(STEP)) * STEP, 2 * STEP)
    return pl.multiple_of(jnp.minimum(low, slot_length - size), STEP), size


def mask_features(lengths_ref, slot, first, rows):
    documents = lengths_ref.shape[1]
    place = first + lax.broadcasted_iota(jnp.int32, (rows, HEAD_DIM), 0)
    lanes = lax.broadcasted_iota(jnp.int32, (rows, HEAD_DIM), 1)
    segment = jnp.zeros((rows, HEAD_DIM), jnp.int32)
    end = jnp.int32(0)
    for document in range(documents):
        end = end + lengths_ref[slot, document]
        segment = segment + jnp.where(place >= end, 1, 0)
    same = lanes == segment
    one = (lanes >= documents) & (lanes < documents + 3)
    key = jnp.where((lanes < documents) & jnp.logical_not(same), -1e30, jnp.where(one, 1.0, 0.0))
    return key.astype(BF16), jnp.where(same, 1.0, 0.0).astype(BF16)


def three_parts(value, lanes, at):
    first = value.astype(BF16).astype(F32)
    rest = value - first
    second = rest.astype(BF16).astype(F32)
    third = rest - second
    return jnp.where(lanes == at, first, jnp.where(lanes == at + 1, second, jnp.where(lanes == at + 2, third, 0.0)))


def attend_forward_kernel(place_ref, lengths_ref, own_ref, other_ref, *refs, fetched, keep):
    refs = list(refs)
    weight_refs = [refs.pop(0) for _ in range(2 if fetched else 1)]
    weight_ref = weight_refs[0]
    query_ref, key_ref, value_ref, out_ref = refs[:4]
    refs = refs[4:]
    slot = place_ref[3]
    documents = lengths_ref.shape[1]
    if keep:
        kept_ref = refs.pop(0)
    if fetched:
        joined_ref = refs.pop(0)
        joined(joined_ref, weight_refs, place_ref[1])
        weight_ref = joined_ref
    rows = own_ref.shape[0] // 2
    length = 2 * rows
    heads = weight_ref.shape[0] // (3 * HEAD_DIM)
    core = place_ref[0]
    lanes = lax.broadcasted_iota(jnp.int32, (rows, HEAD_DIM), 1)
    ones = jnp.where(lanes < 3, 1.0, 0.0).astype(BF16)
    for source, at in ((own_ref, core), (other_ref, 1 - core)):
        here = rows_at(at, rows)
        key_extra, query_extra = mask_features(lengths_ref, slot, at * rows, rows)
        if keep:
            kept_ref[here, :] = source[:rows, :]
        qkv = times_transposed(source[:rows, :], weight_ref[...]).astype(BF16)
        for head in range(heads):
            at = 3 * HEAD_DIM * head
            query = qkv[:, at : at + HEAD_DIM] * 0.125
            key = qkv[:, at + HEAD_DIM : at + 2 * HEAD_DIM]
            value = qkv[:, at + 2 * HEAD_DIM : at + 3 * HEAD_DIM]
            query_ref[head, here, :] = jnp.concatenate([query, query_extra], axis=1)
            key_ref[head, here, :] = jnp.concatenate([key, key_extra], axis=1)
            value_ref[head, here, :] = jnp.concatenate([value, ones], axis=1)

    def one_block(block, carry):
        here = rows_at(block, BLOCK)
        start, window = block_window(lengths_ref, slot, block, length)
        for size in window_sizes(length):

            @pl.when(window == size)
            def _():
                every = range(heads)
                span = pl.ds(start, size)
                queries = [query_ref[head, here, :] for head in every]
                scores = [times_transposed(queries[head], key_ref[head, span, :]) for head in every]
                wide = lax.broadcasted_iota(jnp.int32, (BLOCK, LANES), 1)
                mixed = []
                for head in every:
                    highest = jnp.max(scores[head], axis=1, keepdims=True)
                    raised = jnp.exp(scores[head] - highest).astype(BF16)
                    product = dot(raised, value_ref[head, span, :])
                    total = product[:, HEAD_DIM : HEAD_DIM + 1]
                    mixed.append(product[:, :HEAD_DIM] / total)
                    extra = three_parts(highest + jnp.log(total), wide, HEAD_DIM + documents)
                    query_ref[head, here, :] = (queries[head].astype(F32) - extra).astype(BF16)
                out_ref[here, :] = jnp.concatenate(mixed, axis=1).astype(BF16)

        return carry

    lax.fori_loop(0, length // BLOCK, one_block, 0)


def attend_forward(place, lengths, own, other, weights, keep):
    length, width = own.shape
    fetched = len(weights) == 2
    columns = weights[0].shape[0] * len(weights)
    heads = columns // (3 * HEAD_DIM)
    head_wise = kept((heads, length, LANES), BF16)
    outs = [head_wise] * 3 + [kept((length, heads * HEAD_DIM), BF16)]
    if keep:
        outs.append(kept((length, width), BF16))
    return pl.pallas_call(
        partial(attend_forward_kernel, fetched=fetched, keep=keep),
        out_shape=tuple(outs),
        in_specs=[in_smem()] * 2 + [in_vmem()] * (2 + len(weights)),
        out_specs=(in_vmem(),) * len(outs),
        scratch_shapes=[pltpu.VMEM((columns, width), BF16)] if fetched else [],
        compiler_params=parameters(24),
        cost_estimate=cost(9, 2**22),
        name="attend_forward",
    )(place, lengths, own, other, *weights)


def attend_backward_kernel(place_ref, lengths_ref, *refs, first, heads, extra):
    slot = place_ref[3]
    every = range(2 * heads)
    inputs = []
    for side in range(2):
        for head in range(heads):
            arrays = [refs[5 * side + k].at[first + head] for k in range(3)]
            inputs.append((*arrays, refs[5 * side + 3], refs[5 * side + 4], first + head))
    entry_ref = refs[10]
    refs = refs[11:]
    if extra:
        extras = refs[:2]
        refs = refs[2:]
        for side in range(2):
            refs[2 * side + 1][:extra, :] = extras[side][...]
    outs = refs[:4]
    key_turned_ref, upstream_ref, sum_ref, query_grad_ref, right_ref = refs[4:]
    length = entry_ref.shape[0]
    lanes = lax.broadcasted_iota(jnp.int32, (length, HEAD_DIM), 1)
    zero = jnp.zeros((length, HEAD_DIM), BF16)
    for item in every:
        query_ref, key_ref, value_ref, mixed_ref, grad_ref, head = inputs[item]
        columns = slice(head * HEAD_DIM, (head + 1) * HEAD_DIM)
        upstream = grad_ref[:, columns]
        inner = jnp.sum(mixed_ref[:, columns].astype(F32) * upstream.astype(F32), axis=1, keepdims=True)
        upstream_ref[item] = jnp.concatenate([upstream, -three_parts(inner, lanes, 0).astype(BF16)], axis=1)
        key_turned_ref[item] = key_ref[:, :HEAD_DIM].T
        right_ref[item, 0] = jnp.concatenate([upstream, zero], axis=1)
        right_ref[item, 1] = jnp.concatenate([zero, query_ref[:, :HEAD_DIM]], axis=1)
    sum_ref[...] = jnp.zeros_like(sum_ref)

    def one_block(block, carry):
        here = rows_at(block, BLOCK)
        start, window = block_window(lengths_ref, slot, block, length)
        for size in window_sizes(length):

            @pl.when(window == size)
            def _():
                span = pl.ds(start, size)
                queries = [inputs[s][0][here, :] for s in every]
                upstreams = [upstream_ref[s, here, :] for s in every]
                rights = [
                    jnp.concatenate([right_ref[s, 0, here, :], right_ref[s, 1, here, :]], axis=0) for s in every
                ]
                weights = [jnp.exp(times_transposed(inputs[s][1][span, :], queries[s])) for s in every]
                raised = [times_transposed(inputs[s][2][span, :], upstreams[s]) for s in every]
                score_grads = [(a * b).astype(BF16) for a, b in zip(weights, raised)]
                turned = []
                for s in every:
                    left = jnp.concatenate([weights[s].astype(BF16), score_grads[s]], axis=1)
                    sum_ref[s, span, :] += dot(left, rights[s])
                    turned.append(dot(key_turned_ref[s, :, span], score_grads[s]))
                turned = (jnp.concatenate(turned, axis=0) * 0.125).T
                for s in every:
                    query_grad_ref[s, here, :] = turned[:, s * HEAD_DIM : (s + 1) * HEAD_DIM].astype(BF16)

        return carry

    lax.fori_loop(0, length // BLOCK, one_block, 0)
    for side in (1, 0):
        for head in range(heads):
            item = side * heads + head
            sums = sum_ref[item]
            grads = jnp.concatenate(
                [query_grad_ref[item], sums[:, HEAD_DIM:].astype(BF16), sums[:, :HEAD_DIM].astype(BF16)], axis=1
            )
            outs[2 * side][head] = grads
            part = 3 * HEAD_DIM
            outs[2 * side + 1][extra + head * part : extra + (head + 1) * part, :] = contract_rows(grads, entry_ref[...]).astype(BF16)


def attend_backward(place, lengths, first, heads, sides, entry, extras):
    extra = extras[0].shape[0] if extras else 0
    length, width = entry.shape
    flat = [array for side in sides for array in side]
    outs = [kept((heads, length, 3 * HEAD_DIM), BF16), kept((extra + heads * 3 * HEAD_DIM, width), BF16)] * 2
    count = 2 * heads
    return pl.pallas_call(
        partial(attend_backward_kernel, first=first, heads=heads, extra=extra),
        out_shape=tuple(outs),
        in_specs=[in_smem()] * 2 + [in_vmem()] * (11 + len(extras)),
        out_specs=(in_vmem(),) * len(outs),
        scratch_shapes=[
            pltpu.VMEM((count, HEAD_DIM, length), BF16),
            pltpu.VMEM((count, length, LANES), BF16),
            pltpu.VMEM((count, length, LANES), F32),
            pltpu.VMEM((count, length, HEAD_DIM), BF16),
            pltpu.VMEM((count, 2, length, LANES), BF16),
        ],
        compiler_params=parameters(24),
        cost_estimate=cost(9 * heads, 2**22),
        name="attend_backward",
    )(place, lengths, *flat, entry, *extras)


def project_out_kernel(place_ref, mixed_ref, mixed_x_ref, weight_ref, weight_x_ref, own_ref, other_ref):
    rows = own_ref.shape[0]
    for target, at in ((other_ref, 1 - place_ref[0]), (own_ref, place_ref[0])):
        here = rows_at(at, rows)
        total = dot(mixed_ref[here, :], weight_ref[...]) + dot(mixed_x_ref[here, :], weight_x_ref[...])
        target[...] = total.astype(target.dtype)


def project_out(place, mixed, mixed_x, weight, weight_x):
    rows = mixed.shape[0] // 2
    width = weight.shape[1]
    return pl.pallas_call(
        project_out_kernel,
        out_shape=(kept((rows, width), F32), shape((rows, width), BF16)),
        in_specs=[in_smem()] + [in_vmem()] * 4,
        out_specs=(in_vmem(),) * 2,
        compiler_params=parameters(12),
        cost_estimate=cost(2, 2**22),
        name="project_out",
    )(place, mixed, mixed_x, weight, weight_x)


def project_back_kernel(
    place_ref, own_ref, other_ref, mixed_ref, mixed_x_ref, weight_ref, weight_x_ref,
    grad_ref, grad_x_ref, out_ref, out_x_ref, rows_ref,
):
    rows = own_ref.shape[0]
    rows_ref[rows_at(place_ref[0], rows), :] = own_ref[...]
    rows_ref[rows_at(1 - place_ref[0], rows), :] = other_ref[...]
    out_x_ref[...] = contract_rows(mixed_x_ref[...], rows_ref[...]).astype(BF16)
    out_ref[...] = contract_rows(mixed_ref[...], rows_ref[...]).astype(BF16)
    grad_ref[...] = times_transposed(rows_ref[...], weight_ref[...]).astype(BF16)
    grad_x_ref[...] = times_transposed(rows_ref[...], weight_x_ref[...]).astype(BF16)


def project_back(place, own, other, mixed, mixed_x, weight, weight_x):
    rows, width = own.shape
    return pl.pallas_call(
        project_back_kernel,
        out_shape=(kept(mixed.shape, BF16),) * 2 + (kept(weight.shape, BF16),) * 2,
        in_specs=[in_smem()] + [in_vmem()] * 6,
        out_specs=(in_vmem(),) * 4,
        scratch_shapes=[pltpu.VMEM((2 * rows, width), BF16)],
        compiler_params=parameters(14),
        cost_estimate=cost(3, 2**22),
        name="project_back",
    )(place, own, other, mixed, mixed_x, weight, weight_x)


def entry_back_kernel(place_ref, *refs, groups):
    grads = [[ref.at[k] for ref in refs[side * groups : (side + 1) * groups] for k in range(ref.shape[0])] for side in (0, 1)]
    weight_ref, first_ref, second_ref, own_ref, other_ref, joined_ref = refs[2 * groups :]
    rows = own_ref.shape[0]
    joined(joined_ref, (first_ref, second_ref), place_ref[1])
    for target, at in ((other_ref, 1 - place_ref[0]), (own_ref, place_ref[0])):
        here = rows_at(at, rows)
        left = jnp.concatenate([grad[here, :] for grad in grads[0]], axis=1)
        left_x = jnp.concatenate([grad[here, :] for grad in grads[1]], axis=1)
        total = dot(left, weight_ref[...]) + dot(left_x, joined_ref[...])
        target[...] = total.astype(target.dtype)


def entry_back(place, grads, grads_x, weight, weights_x):
    rows = grads[0].shape[1] // 2
    width = weight.shape[1]
    groups = len(grads)
    return pl.pallas_call(
        partial(entry_back_kernel, groups=groups),
        out_shape=(kept((rows, width), F32), shape((rows, width), BF16)),
        in_specs=[in_smem()] + [in_vmem()] * (2 * groups + 3),
        out_specs=(in_vmem(),) * 2,
        scratch_shapes=[pltpu.VMEM(weight.shape, BF16)],
        compiler_params=parameters(16),
        cost_estimate=cost(4, 2**22),
        name="entry_back",
    )(place, *grads, *grads_x, weight, *weights_x)


def hidden_grad(both, down):
    rows = both.shape[0] // 2
    units = down.shape[0]

    def kernel(both_ref, down_ref, out_ref):
        out_ref[...] = times_transposed(both_ref[rows:, :], down_ref[...])

    return pl.pallas_call(
        kernel,
        out_shape=kept((rows, units), F32),
        in_specs=[in_vmem()] * 2,
        out_specs=in_vmem(),
        compiler_params=parameters(8),
        cost_estimate=cost(1, 2**21),
        name="hidden_grad",
    )(both, down)


def hidden_kernel(place_ref, *refs, fetched):
    refs = list(refs)
    entries = refs[:2]
    upstreams = refs[2:4]
    if fetched:
        up_refs, down_refs = refs[4:6], refs[6:9]
        base = refs[9:11]
        refs = refs[11:]
    else:
        up_ref, bias_ref = refs[4:6]
        hidden_grads = refs[6:8]
        refs = refs[8:]
    grads = refs[:2]
    hidden_ref, bias_sum_ref = refs[2:4]
    if fetched:
        up_kept_ref, up_sent_ref, down_kept_ref, down_sent_ref = refs[4:8]
        up_all_ref, down_all_ref = refs[8:10]
        pre_grad_ref, sum_ref = refs[10:12]
        up_sum_ref = down_sum_ref = sum_ref
        direct = down_refs[2].shape[0]
        joined(up_all_ref, up_refs, place_ref[1])
        joined(down_all_ref, down_refs, place_ref[2], direct)
        up_ref, down_ref = up_all_ref, down_all_ref
    else:
        up_sum_ref, down_sum_ref, pre_grad_ref = refs[4:7]
    rows, width = entries[0].shape
    units = up_ref.shape[1]
    bias_sum = [jnp.zeros((1, BLOCK), F32) for _ in range(units // BLOCK)]
    if fetched:
        at = (units - direct) // 2
        bias = down_refs[0][at : at + 16, :].astype(F32)[:1]
    else:
        bias = one_line(bias_ref, 0, units).astype(F32)
    for part in range(2):
        there = slice(part * rows, (part + 1) * rows)
        entry = entries[part][...]
        upstream = upstreams[part][rows:, :]
        for block in range(units // BLOCK):
            cut = slice(block * BLOCK, (block + 1) * BLOCK)
            pre = dot(entry, up_ref[:, cut]) + bias[:, cut]
            given = times_transposed(upstream, down_ref[cut, :]) if fetched else hidden_grads[part][:, cut]
            square = pre * pre
            half = 0.5 + 0.5 * jnp.tanh(pre * (TANH_SCALE + (TANH_SCALE * TANH_CUBE) * square))
            hidden = pre * half
            slope = half + (hidden - hidden * half) * (2 * TANH_SCALE + (6 * TANH_SCALE * TANH_CUBE) * square)
            pre_grad = (given * slope).astype(BF16)
            hidden_ref[there, cut] = hidden.astype(BF16)
            pre_grad_ref[there, cut] = pre_grad
            bias_sum[block] = bias_sum[block] + jnp.sum(pre_grad.astype(F32), axis=0, keepdims=True)
    bias_sum_ref[...] = jnp.zeros_like(bias_sum_ref)
    bias_sum_ref[0:1, :] = jnp.concatenate(bias_sum, axis=1)
    for part in (1, 0):
        grad = times_transposed(pre_grad_ref[part * rows : (part + 1) * rows, :], up_ref[...])
        if fetched:
            grad = grad + base[part][...]
        grads[part][...] = grad.astype(grads[part].dtype)
    half = units // 2
    for block in range(units // BLOCK):
        cut = slice(block * BLOCK, (block + 1) * BLOCK)
        total = contract_rows(entries[0][...], pre_grad_ref[:rows, cut]) + contract_rows(entries[1][...], pre_grad_ref[rows:, cut])
        up_sum_ref[:, cut] = total.astype(BF16)
    if fetched:
        up_sent_ref[...] = sum_ref[rows_at(1 - place_ref[2], width // 2), :]
        up_kept_ref[...] = sum_ref[rows_at(place_ref[2], width // 2), :]
    for block in range(units // BLOCK):
        cut = slice(block * BLOCK, (block + 1) * BLOCK)
        total = contract_rows(hidden_ref[:rows, cut], upstreams[0][rows:, :]) + contract_rows(hidden_ref[rows:, cut], upstreams[1][rows:, :])
        down_sum_ref[cut, :] = total.astype(BF16)
    if fetched:
        down_sent_ref[...] = sum_ref[rows_at(1 - place_ref[1], half), :]
        down_kept_ref[...] = sum_ref[rows_at(place_ref[1], half), :]


def hidden_part(place, entries, upstreams, weights, others, fetched):
    rows, width = entries[0].shape
    units = weights[0].shape[1]
    inputs = [*entries, *upstreams, *weights, *others]
    outs = [kept((rows, width), F32), shape((rows, width), BF16) if fetched else kept((rows, width), F32)]
    outs += [kept((2 * rows, units), BF16), shape((8, units), F32)]
    if fetched:
        outs += [kept((width // 2, units), BF16), shape((width // 2, units), BF16)]
        outs += [kept((units // 2, width), BF16), shape((units // 2, width), BF16)]
        outs += [kept((width, units), BF16), kept((units, width), BF16)]
    else:
        outs += [kept((width, units), BF16), kept((units, width), BF16)]
    return pl.pallas_call(
        partial(hidden_kernel, fetched=fetched),
        out_shape=tuple(outs),
        in_specs=[in_smem()] + [in_vmem()] * len(inputs),
        out_specs=(in_vmem(),) * len(outs),
        scratch_shapes=[pltpu.VMEM((2 * rows, units), BF16)] + [pltpu.VMEM((width, units), BF16)] * fetched,
        compiler_params=parameters(24),
        cost_estimate=cost(10, 2**23),
        name="hidden_part",
    )(place, *inputs)


def hidden_out_kernel(hidden_ref, hidden_x_ref, down_ref, down_x_ref, out_ref, *, part):
    rows = out_ref.shape[0]
    there = slice(part * rows, (part + 1) * rows)
    out = dot(hidden_ref[there, :], down_ref[...]) + dot(hidden_x_ref[there, :], down_x_ref[...])
    out_ref[...] = out.astype(out_ref.dtype)


def hidden_out(hidden, hidden_x, down, down_x, part, kind):
    rows, width = hidden.shape[0] // 2, down.shape[1]
    return pl.pallas_call(
        partial(hidden_out_kernel, part=part),
        out_shape=(kept if kind == F32 else shape)((rows, width), kind),
        in_specs=[in_vmem()] * 4,
        out_specs=in_vmem(),
        compiler_params=parameters(12),
        cost_estimate=cost(2, 2**22),
        name="hidden_out",
    )(hidden, hidden_x, down, down_x)


ROWS = 128


def row_wise(body, name, row_inputs, whole_inputs, row_outs, sums, micros):
    rows, width = row_inputs[0].shape
    outs = [make((rows, width), kind) for make, kind in row_outs]
    if sums:
        outs.append(kept((8, width), F32))

    def kernel(*refs):
        refs = list(refs)
        row_refs = [refs.pop(0) for _ in row_inputs]
        whole_refs = [refs.pop(0) for _ in whole_inputs]

        def tile(step, total):
            here = rows_at(step, ROWS)
            results, terms = body(*[ref[here, :] for ref in row_refs], *whole_refs)
            for ref, result in zip(refs, results):
                ref[here, :] = result.astype(ref.dtype)
            return tuple(
                old + jnp.sum(term.reshape(ROWS // 8, 8, width), axis=0) for old, term in zip(total, terms)
            )

        total = lax.fori_loop(0, rows // ROWS, tile, (jnp.zeros((8, width), F32),) * sums)
        if sums:
            lines = [jnp.sum(term, axis=0, keepdims=True) for term in total]
            refs[-1][...] = jnp.concatenate(lines + [jnp.zeros((8 - sums, width), F32)], axis=0)

    return pl.pallas_call(
        kernel,
        out_shape=tuple(outs),
        in_specs=[in_vmem()] * (len(row_inputs) + len(whole_inputs)),
        out_specs=(in_vmem(),) * len(outs),
        compiler_params=parameters(18),
        cost_estimate=cost(micros, 2**20),
        name=name,
    )(*row_inputs, *whole_inputs)


def enter_kernel(place_ref, time_ref, tokens_ref, cotangent_ref, weight_ref, *refs):
    vectors, (table_ref, both_ref) = refs[:-2], refs[-2:]
    rows, width = tokens_ref.shape
    table_ref[...] = jnp.zeros_like(table_ref)
    row = 0
    for vector in vectors:
        for at in range(0, vector.shape[0], width // LANES):
            table_ref[row : row + 1, :] = one_line(vector, at, width)
            row += 1
    features = time_features(time_ref[place_ref[3]], 0, COND)
    for piece in range(6):
        cut = slice(piece * width, (piece + 1) * width)
        table_ref[piece : piece + 1, :] += jnp.sum(features * weight_ref[:, cut], axis=0, keepdims=True)
    table_ref[row : row + 1, :COND] = time_features(time_ref[place_ref[3]], 1, COND)
    table = table_ref[...]

    def tile(step, carry):
        here = rows_at(step, ROWS)
        scored, _ = standard_score_rows(tokens_ref[here, :].astype(F32))
        entry = scored * table[6:7] * (1.0 + table[1:2]) + table[0:1]
        both_ref[here, :] = entry.astype(BF16)
        there = pl.ds(pl.multiple_of(rows + step * ROWS, ROWS), ROWS)
        both_ref[there, :] = (table[5:6] * cotangent_ref[here, :].astype(F32)).astype(BF16)
        return carry

    lax.fori_loop(0, rows // ROWS, tile, 0)


def enter(place, time_index, tokens, cotangent, weight, vectors):
    vectors = [vector.reshape(-1, LANES) for vector in vectors]
    rows, width = tokens.shape
    return pl.pallas_call(
        enter_kernel,
        out_shape=(shape((16, width), F32), shape((2 * rows, width), BF16)),
        in_specs=[in_smem()] * 2 + [in_vmem()] * (3 + len(vectors)),
        out_specs=(in_vmem(),) * 2,
        compiler_params=parameters(14),
        cost_estimate=cost(4, 2**22),
        name="enter",
    )(place, time_index, in_hbm(tokens), in_hbm(cotangent), in_hbm(weight), *[in_hbm(vector) for vector in vectors])


def enter_second(tokens, branch_own, branch_other, modulation):
    branch = branch_own + branch_other.astype(F32)
    middle = tokens.astype(F32) + modulation[2:3, :] * branch
    scored, _ = standard_score_rows(middle)
    entry = scored * modulation[7:8, :] * (1.0 + modulation[4:5, :]) + modulation[3:4, :]
    return (middle, entry), ()


def leave(middle, cotangent, out_own, out_other, modulation):
    branch = out_own + out_other.astype(F32) + modulation[8:9, :]
    incoming = cotangent.astype(F32)
    branch_grad = (modulation[5:6, :] * incoming).astype(BF16).astype(F32)
    return (middle + modulation[5:6, :] * branch,), (incoming * branch, branch_grad)


def back_second(middle, cotangent, grad_own, grad_other, branch_own, branch_other, modulation):
    gain = modulation[7:8, :]
    scored, inverse = standard_score_rows(middle)
    entry_grad = grad_own + grad_other.astype(F32)
    normed_grad = entry_grad * (1.0 + modulation[4:5, :])
    middle_grad = cotangent.astype(F32) + norm_reverse_pass(normed_grad * gain, scored, inverse)
    branch = branch_own + branch_other.astype(F32)
    terms = (middle_grad * branch, entry_grad, entry_grad * (scored * gain), normed_grad * scored)
    return (modulation[2:3, :] * middle_grad, middle_grad), terms


def back_first(tokens, grad_own, grad_other, middle_grad, modulation):
    gain = modulation[6:7, :]
    scored, inverse = standard_score_rows(tokens.astype(F32))
    entry_grad = grad_own + grad_other.astype(F32)
    normed_grad = entry_grad * (1.0 + modulation[1:2, :])
    grad = middle_grad + norm_reverse_pass(normed_grad * gain, scored, inverse)
    return (grad,), (entry_grad, entry_grad * (scored * gain), normed_grad * scored)


def piece_kernel(place_ref, source_ref, *refs, rows, bit):
    if len(refs) == 2:
        refs[1][rows:, :] = jnp.zeros_like(refs[1][rows:, :])
        refs[1][rows : rows + 1, :] = one_line(refs[0], 0, refs[1].shape[1])
    refs[-1][:rows, :] = source_ref[rows_at(place_ref[bit], rows), :]


def own_piece(place, source, rows, bit, line=None):
    extra = [] if line is None else [line.reshape(-1, LANES)]
    return pl.pallas_call(
        partial(piece_kernel, rows=rows, bit=bit),
        out_shape=shape((rows + 16 * len(extra), source.shape[1]), source.dtype),
        in_specs=[in_smem()] + [in_vmem()] * (1 + len(extra)),
        out_specs=in_vmem(),
        compiler_params=parameters(8),
        cost_estimate=small_cost(),
        name="own_piece",
    )(place, in_hbm(source), *extra)


def lower_half(source):
    rows, width = source.shape

    def kernel(source_ref, out_ref):
        out_ref[...] = source_ref[rows // 2 :, :]

    return pl.pallas_call(
        kernel,
        out_shape=shape((rows // 2, width), source.dtype),
        in_specs=[in_vmem()],
        out_specs=in_vmem(),
        compiler_params=parameters(8),
        cost_estimate=small_cost(),
        name="lower_half",
    )(in_hbm(source))


def sum_kernel(place_ref, a_ref, b_ref, kept_ref, sent_ref, *, bit):
    half = kept_ref.shape[0]
    for out, index in ((sent_ref, 1 - place_ref[bit]), (kept_ref, place_ref[bit])):
        here = rows_at(index, half)
        out[...] = (a_ref[here, :].astype(F32) + b_ref[here, :].astype(F32)).astype(BF16)


def summed(place, a, b, bit):
    rows, width = a.shape
    return pl.pallas_call(
        partial(sum_kernel, bit=bit),
        out_shape=(kept((rows // 2, width), BF16),) * 2,
        in_specs=[in_smem(), in_vmem(), in_vmem()],
        out_specs=(in_vmem(),) * 2,
        compiler_params=parameters(8),
        cost_estimate=small_cost(3),
        name="summed",
    )(place, a, b)


def total_kernel(a_ref, b_ref, out_ref):
    out_ref[...] = (a_ref[...].astype(F32) + b_ref[...].astype(F32)).astype(BF16)


def total_of(a, b):
    return pl.pallas_call(
        total_kernel,
        out_shape=kept(a.shape, BF16),
        in_specs=[in_vmem()] * 2,
        out_specs=in_vmem(),
        compiler_params=parameters(8),
        cost_estimate=small_cost(3),
        name="total_of",
    )(a, b)


def pair_kernel(place_ref, a_ref, b_ref, kept_a_ref, kept_b_ref, sent_ref, *, bit):
    half = kept_a_ref.shape[0]
    mine, other = rows_at(place_ref[bit], half), rows_at(1 - place_ref[bit], half)
    sent_ref[:half, :] = a_ref[other, :]
    sent_ref[half:, :] = b_ref[other, :]
    kept_a_ref[...] = a_ref[mine, :]
    kept_b_ref[...] = b_ref[mine, :]


def pair_halves(place, a, b, bit):
    rows, width = a.shape
    half = kept((rows // 2, width), BF16)
    return pl.pallas_call(
        partial(pair_kernel, bit=bit),
        out_shape=(half, half, kept((rows, width), BF16)),
        in_specs=[in_smem(), in_vmem(), in_vmem()],
        out_specs=(in_vmem(),) * 3,
        compiler_params=parameters(8),
        cost_estimate=small_cost(3),
        name="pair_halves",
    )(place, a, b)


def halves_kernel(place_ref, source_ref, kept_ref, sent_ref, *, bit):
    half = kept_ref.shape[0]
    sent_ref[...] = source_ref[rows_at(1 - place_ref[bit], half), :]
    kept_ref[...] = source_ref[rows_at(place_ref[bit], half), :]


def halves(place, source, bit):
    rows, width = source.shape
    return pl.pallas_call(
        partial(halves_kernel, bit=bit),
        out_shape=(kept((rows // 2, width), BF16),) * 2,
        in_specs=[in_smem(), in_vmem()],
        out_specs=(in_vmem(),) * 2,
        compiler_params=parameters(8),
        cost_estimate=small_cost(3),
        name="halves",
    )(place, source)


def pair_total_kernel(a_ref, b_ref, got_ref, out_a_ref, out_b_ref):
    half = a_ref.shape[0]
    out_b_ref[...] = (b_ref[...].astype(F32) + got_ref[half:, :].astype(F32)).astype(BF16)
    out_a_ref[...] = (a_ref[...].astype(F32) + got_ref[:half, :].astype(F32)).astype(BF16)


def pair_total(a, b, got):
    return pl.pallas_call(
        pair_total_kernel,
        out_shape=(kept(a.shape, BF16),) * 2,
        in_specs=[in_vmem()] * 3,
        out_specs=(in_vmem(),) * 2,
        compiler_params=parameters(8),
        cost_estimate=small_cost(3),
        name="pair_total",
    )(a, b, got)


def two_totals_kernel(a_ref, b_ref, c_ref, d_ref, first_ref, second_ref):
    first_ref[...] = (a_ref[...].astype(F32) + b_ref[...].astype(F32)).astype(BF16)
    second_ref[...] = (c_ref[...].astype(F32) + d_ref[...].astype(F32)).astype(BF16)


def two_totals(a, b, c, d):
    return pl.pallas_call(
        two_totals_kernel,
        out_shape=(kept(a.shape, BF16), kept(c.shape, BF16)),
        in_specs=[in_vmem()] * 4,
        out_specs=(in_vmem(),) * 2,
        compiler_params=parameters(8),
        cost_estimate=small_cost(3),
        name="two_totals",
    )(a, b, c, d)


def send_rows(whole_ref, at, out_ref, out_at, count, sem):
    copy = pltpu.make_async_copy(whole_ref.at[pl.ds(at, count), :], out_ref.at[pl.ds(out_at, count), :], sem)
    copy.start()
    return copy


def lay_and_cut_kernel(place_ref, own_ref, other_ref, behind_ref, first_ref, second_ref, whole_ref, sems, *, bit):
    rows, cut, rest = own_ref.shape[0], first_ref.shape[0], behind_ref.shape[0]
    copies = [send_rows(behind_ref, 0, second_ref, 2 * rows - cut, rest // 2, sems.at[0])]
    copies.append(send_rows(behind_ref, rest // 2, second_ref, 2 * rows - cut + rest // 2, rest - rest // 2, sems.at[1]))
    for ref, index in ((own_ref, place_ref[bit]), (other_ref, 1 - place_ref[bit])):
        whole_ref[rows_at(index, rows), :] = ref[...].astype(whole_ref.dtype)
    copies.append(send_rows(whole_ref, 0, first_ref, 0, cut, sems.at[2]))
    copies.append(send_rows(whole_ref, cut, second_ref, 0, 2 * rows - cut, sems.at[3]))
    for copy in copies:
        copy.wait()


def lay_and_cut(place, own, other, bit, behind, cut):
    rows, width = own.shape
    return pl.pallas_call(
        partial(lay_and_cut_kernel, bit=bit),
        out_shape=(shape((cut, width), F32), shape((2 * rows - cut + behind.shape[0], width), F32)),
        in_specs=[in_smem()] + [in_vmem()] * 3,
        out_specs=(anywhere(),) * 2,
        scratch_shapes=[pltpu.VMEM((2 * rows, width), F32), pltpu.SemaphoreType.DMA((4,))],
        compiler_params=parameters(14),
        cost_estimate=small_cost(3),
        name="lay_and_cut",
    )(place, own, other, behind)


def lay_straight_kernel(place_ref, own_ref, other_ref, out_ref, *, bit):
    rows = own_ref.shape[0]
    for ref, index in ((own_ref, place_ref[bit]), (other_ref, 1 - place_ref[bit])):
        out_ref[rows_at(index, rows), :] = ref[...].astype(out_ref.dtype)


def lay(place, own, other, bit):
    rows, width = own.shape
    return pl.pallas_call(
        partial(lay_straight_kernel, bit=bit),
        out_shape=kept((2 * rows, width), BF16),
        in_specs=[in_smem()] + [in_vmem()] * 2,
        out_specs=in_vmem(),
        compiler_params=parameters(8),
        cost_estimate=small_cost(3),
        name="lay",
    )(place, own, other)


def lay_out_kernel(place_ref, own_ref, other_ref, out_ref, whole_ref, sems, *, bit, parts):
    rows = own_ref.shape[0]
    count = rows // parts
    copies = []
    for which, (ref, index) in enumerate(((own_ref, place_ref[bit]), (other_ref, 1 - place_ref[bit]))):
        for part in range(parts):
            at = which * rows + part * count
            whole_ref[at : at + count, :] = ref[part * count : (part + 1) * count, :].astype(F32)
            target = pl.multiple_of(index * rows + part * count, count)
            copies.append(send_rows(whole_ref, at, out_ref, target, count, sems.at[which * parts + part]))
    for copy in copies:
        copy.wait()


def lay_out(place, own, other, bit):
    rows, width = own.shape
    parts = 3
    return pl.pallas_call(
        partial(lay_out_kernel, bit=bit, parts=parts),
        out_shape=shape((2 * rows, width), F32),
        in_specs=[in_smem()] + [in_vmem()] * 2,
        out_specs=anywhere(),
        scratch_shapes=[pltpu.VMEM((2 * rows, width), F32), pltpu.SemaphoreType.DMA((2 * parts,))],
        compiler_params=parameters(14),
        cost_estimate=small_cost(3),
        name="lay_out",
    )(place, own, other)


TABLE = 16


def tabulate_kernel(first_ref, second_ref, last_ref, table_ref, bias_ref, bias_x_ref, out_ref):
    rows = [first_ref[0:2, :], second_ref[0:3, :], last_ref[0:1, :], first_ref[2:3, :], second_ref[3:4, :], last_ref[1:2, :]]
    rows += [table_ref[9:10, :], bias_ref[0:1, :], bias_x_ref[0:1, :], jnp.zeros((TABLE - 12, out_ref.shape[1]), F32)]
    out_ref[...] = jnp.concatenate(rows, axis=0)


def tabulate(*parts):
    return pl.pallas_call(
        tabulate_kernel,
        out_shape=shape((TABLE, parts[0].shape[1]), F32),
        in_specs=[in_vmem()] * 6,
        out_specs=in_vmem(),
        compiler_params=parameters(8),
        cost_estimate=cost(1, 2**18),
        name="tabulate",
    )(*parts)


def lay_table(out_ref, at, own, other, side):
    rows = own.shape[0]
    out_ref[pl.ds(pl.multiple_of(at + side * rows, TABLE), rows), :] = own
    out_ref[pl.ds(pl.multiple_of(at + (1 - side) * rows, TABLE), rows), :] = other


def ride_first_kernel(kept_ref, kept_x_ref, got_ref, own_ref, near_ref, part_ref, table_ref, out_ref):
    half = kept_ref.shape[0]
    own = own_ref[...]
    row = lax.broadcasted_iota(jnp.int32, own.shape, 0)
    table = jnp.where(row < 9, own + near_ref[...], own).astype(BF16)
    out_ref[:half, :] = (kept_x_ref[...].astype(F32) + got_ref[half:, :].astype(F32)).astype(BF16)
    out_ref[half:, :] = table
    table_ref[...] = table
    part_ref[...] = (kept_ref[...].astype(F32) + got_ref[:half, :].astype(F32)).astype(BF16)


def ride_half_kernel(place_ref, part_ref, got_ref, table_ref, kept_ref, next_ref, out_ref):
    half, rows = kept_ref.shape[0], table_ref.shape[0]
    mine, other = rows_at(place_ref[2], half), rows_at(1 - place_ref[2], half)
    out_ref[:half, :] = (part_ref[other, :].astype(F32) + got_ref[other, :].astype(F32)).astype(BF16)
    kept_ref[...] = (part_ref[mine, :].astype(F32) + got_ref[mine, :].astype(F32)).astype(BF16)
    lay_table(next_ref, 0, table_ref[...], got_ref[2 * half :, :], place_ref[3])
    out_ref[half:, :] = next_ref[...]


def ride_add_kernel(place_ref, value_ref, got_ref, table_ref, sum_ref, next_ref, *outs, bit):
    rows = value_ref.shape[0]
    total = (value_ref[...].astype(F32) + got_ref[:rows, :].astype(F32)).astype(BF16)
    sum_ref[...] = total
    lay_table(next_ref, 0, table_ref[...], got_ref[rows:, :], place_ref[bit])
    for out in outs:
        out[:rows, :] = total
        out[rows:, :] = next_ref[...]


def ride_lay_kernel(place_ref, own_ref, other_ref, table_ref, out_ref):
    rows = own_ref.shape[0]
    for ref, index in ((own_ref, place_ref[2]), (other_ref, 1 - place_ref[2])):
        out_ref[rows_at(index, rows), :] = ref[...]
    out_ref[2 * rows :, :] = table_ref[...]


def ride(kernel, name, outs, *inputs):
    scalars = [in_smem()] if inputs[0].ndim == 1 else []
    return pl.pallas_call(
        kernel,
        out_shape=tuple(kept(dims, BF16) for dims in outs),
        in_specs=scalars + [in_vmem()] * (len(inputs) - len(scalars)),
        out_specs=(in_vmem(),) * len(outs),
        compiler_params=parameters(8),
        cost_estimate=small_cost(3),
        name=name,
    )(*inputs)


def hold_kernel(source_ref, out_ref):
    out_ref[...] = source_ref[...]


def hold(value):
    return pl.pallas_call(
        hold_kernel,
        out_shape=kept(value.shape, value.dtype),
        in_specs=[in_vmem()],
        out_specs=in_vmem(),
        compiler_params=parameters(8),
        cost_estimate=cost(3, 2**18),
        name="hold",
    )(value)


def finish_kernel(place_ref, own_ref, got_ref, sum_ref, grad_ref, totals_ref, line_ref, grad_all_ref, sems, *, half):
    for ref, index in ((own_ref, place_ref[1]), (got_ref, 1 - place_ref[1])):
        sum_ref[pl.ds(pl.multiple_of(index * half, 16), half), :] = ref[:half, :].astype(F32)
    slots, width = (own_ref.shape[0] - half) // TABLE, own_ref.shape[1]
    for ref, index in ((own_ref, place_ref[1]), (got_ref, 1 - place_ref[1])):

        def one_slot(slot, carry, ref=ref, index=index):
            lines = ref[pl.ds(pl.multiple_of(half + slot * TABLE, TABLE), TABLE), :].astype(F32)
            for row in range(12):
                line_ref[row, pl.ds(index * slots + slot, 1), :] = lines[row : row + 1]
            return carry

        lax.fori_loop(0, slots, one_slot, 0)
    features = line_ref[9][:, :COND].astype(BF16)
    totals_ref[...] = jnp.zeros_like(totals_ref)
    copies = []
    for piece in range(9):
        terms = line_ref[piece]
        totals_ref[piece : piece + 1, :] = jnp.sum(terms, axis=0, keepdims=True)
        if piece < 6:
            grad_all_ref[piece] = contract_rows(features, terms.astype(BF16))
            copy = pltpu.make_async_copy(
                grad_all_ref.at[piece], grad_ref.at[:, pl.ds(piece * width, width)], sems.at[piece]
            )
            copy.start()
            copies.append(copy)
    slot = lax.broadcasted_iota(jnp.int32, (2 * slots, width), 0)
    mine = lax.rem(slot, 2) == place_ref[3]
    totals_ref[9:10, :] = jnp.sum(jnp.where(mine, line_ref[10], line_ref[11]), axis=0, keepdims=True)
    for copy in copies:
        copy.wait()


def finish(place, own, got, half):
    width = own.shape[1]
    slots = 2 * (own.shape[0] - half) // TABLE
    return pl.pallas_call(
        partial(finish_kernel, half=half),
        out_shape=(
            kept((2 * half, width), F32),
            shape((COND, 6 * width), F32),
            shape((TABLE, width), F32),
        ),
        in_specs=[in_smem()] + [in_vmem()] * 2,
        out_specs=(in_vmem(), anywhere(), in_vmem()),
        scratch_shapes=[
            pltpu.VMEM((12, slots, width), F32),
            pltpu.VMEM((6, COND, width), F32),
            pltpu.SemaphoreType.DMA((6,)),
        ],
        compiler_params=parameters(20),
        cost_estimate=cost(3, 2**20),
        name="finish",
    )(place, own, got)


class Order:
    def __init__(self):
        self.token = ()

    def __call__(self, value):
        return after(value, *self.token) if self.token else value

    def done(self, result):
        self.token = (result[-1] if isinstance(result, (tuple, list)) else result,)
        return result


def dp_bits():
    bits = []
    bit = 1
    while bit < lax.axis_size("dp"):
        bits.append(bit)
        bit *= 2
    return bits


def per_device(
    tokens,
    cotangent,
    doc_lengths,
    time_index,
    attention_norm_gain,
    qkv_weight,
    out_weight,
    feedforward_norm_gain,
    up_weight,
    up_bias,
    down_weight,
    down_bias,
    ada_weight,
    ada_bias,
):
    rows, width = tokens.shape
    core = lax.axis_index("mp") % 2
    slot = lax.axis_index("mp") // 2
    index = lax.axis_index("dp")
    bits = dp_bits()
    place = [core, index % 2, index // 2 % 2, slot] + [index // bit % 2 for bit in bits[2:]]
    place = jnp.stack(place).astype(jnp.int32)
    order = Order()

    def near(value):
        return swap(value, "mp", 1)

    def across(value):
        return swap(value, "mp", 2)

    def relayed(value):
        return swap(value, "dp", 1)

    qkv_turned = qkv_weight.T
    qkv_half = order.done(own_piece(place, qkv_turned, qkv_turned.shape[0] // 2, 1))
    qkv_a = across(qkv_half)
    table, both = order.done(
        enter(
            place,
            time_index,
            order(tokens),
            cotangent,
            ada_weight,
            (ada_bias, attention_norm_gain, feedforward_norm_gain, down_bias),
        )
    )
    both_near = near(both)
    out_weight_x = across(order(out_weight))
    up_half = order.done(own_piece(place, order(up_weight), width // 2, 1))
    up_a = across(up_half)
    quarter = down_weight.shape[0] // 4
    down_part = order.done(own_piece(place, order(down_weight), quarter, 2, up_bias))
    down_a = across(down_part)
    down_lower = order.done(lower_half(order(down_weight)))
    table = order.done(hold(after(order(table), qkv_a)))
    qkv_b = swap(qkv_a, "dp", 1)

    query, key, value, mixture, entry_one_all = order.done(
        attend_forward(place, doc_lengths, order(both), both_near, (qkv_turned,), True)
    )
    down_straight = across(order(down_lower))
    query_x, key_x, value_x, mixture_x = order.done(
        attend_forward(place, doc_lengths, order(both), both_near, (qkv_a, qkv_b), False)
    )
    branch_own, branch_other = order.done(project_out(place, mixture, order(mixture_x), out_weight, out_weight_x))
    branch_other = near(branch_other)
    grad_one = order.done(hidden_grad(order(both), down_weight))
    up_b = swap(after(up_a, grad_one), "dp", 1)
    middle, entry_two = order.done(
        row_wise(
            enter_second, "enter_second", (order(tokens), branch_own, after(branch_other, up_a)), (table,), ((kept, F32), (shape, BF16)), 0, 3
        )
    )
    entry_two_near = near(entry_two)
    grad_two = order.done(hidden_grad(order(both_near), down_weight))
    down_b = swap(after(down_a, grad_two), "dp", 2)
    entries_two = (entry_two, after(entry_two_near, down_a))

    grad_base, grad_base_near, hidden, bias_sum, up_sum, down_sum = order.done(
        hidden_part(
            place,
            entries_two,
            (order(both), both_near),
            (up_weight, up_bias.reshape(-1, LANES)),
            (grad_one, grad_two),
            False,
        )
    )
    grad_own, grad_other, hidden_x, bias_sum_x, up_kept_x, up_sent_x, down_kept_x, down_sent_x, _, down_weight_x = order.done(
        hidden_part(
            place,
            (order(entries_two[0]), entries_two[1]),
            (both, both_near),
            (up_a, up_b, down_a, down_b, down_straight),
            (grad_base, grad_base_near),
            True,
        )
    )
    grad_other = near(grad_other)
    out_other = order.done(hidden_out(order(hidden), hidden_x, down_weight, down_weight_x, 1, BF16))
    out_other = near(out_other)
    down_got_x = swap(order(down_sent_x), "dp", 1)
    up_got_x = swap(order(up_sent_x), "dp", 2)
    attn_grad, middle_grad, sums_two = order.done(
        row_wise(
            back_second,
            "back_second",
            (order(middle), cotangent, grad_own, grad_other, branch_own, branch_other),
            (table,),
            ((shape, BF16), (kept, F32)),
            4,
            4,
        )
    )
    attn_grad_near = near(attn_grad)
    out_own = order.done(hidden_out(order(hidden), hidden_x, down_weight, down_weight_x, 0, F32))
    mixture_grad, mixture_grad_x, out_sum, out_sum_x = order.done(
        project_back(place, order(attn_grad), after(attn_grad_near, out_other), mixture, mixture_x, out_weight, out_weight_x)
    )
    down_kept, down_sent = order.done(halves(place, order(down_sum), 1))
    down_got = swap(down_sent, "dp", 1)
    up_kept, up_sent = order.done(halves(place, order(up_sum), 2))
    up_got = swap(up_sent, "dp", 2)

    sides = ((query, key, value, mixture, mixture_grad), (query_x, key_x, value_x, mixture_x, mixture_grad_x))

    def backward(head, extras):
        return order.done(
            attend_backward(place, doc_lengths, head, 1, sides, order(entry_one_all), extras)
        )

    def on(value, step=0):
        return swap(value, "dp", bits[2 + step])

    def doubled(value, got):
        for step in range(len(bits) - 2):
            value = order.done(total_of(order(value), got))
            if step + 3 < len(bits):
                got = on(value, step + 1)
        return value

    back_0, first_sum, back_x_0, first_sum_x = backward(0, (out_sum, out_sum_x))
    down_part_x = order.done(total_of(order(down_kept_x), down_got_x))
    down_got_x = across(down_part_x)
    back_1, head_sum, back_x_1, head_sum_x = backward(1, ())
    up_part_x = order.done(total_of(order(up_kept_x), up_got_x))
    up_got_x = across(up_part_x)
    up_part, down_part = order.done(two_totals(order(up_kept), up_got, down_kept, down_got))
    back_2, rest_sum, back_x_2, rest_sum_x = backward(2, (head_sum, head_sum_x))
    rest_kept, rest_kept_x, rest_sent = order.done(pair_halves(place, order(rest_sum), rest_sum_x, 1))
    rest_got = swap(rest_sent, "dp", 1)
    down_kept, down_sent = order.done(summed(place, order(down_part), down_got_x, 2))
    down_got = swap(down_sent, "dp", 2)
    first_own, first_other = order.done(
        entry_back(
            place, (order(back_0), back_1, back_2), (back_x_0, back_x_1, back_x_2), qkv_turned, (qkv_a, qkv_b)
        )
    )
    first_other = near(first_other)
    output, sums_out = order.done(
        row_wise(leave, "leave", (order(middle), cotangent, out_own, out_other), (table,), ((shape, BF16),), 2, 3)
    )
    input_gradient, sums_one = order.done(
        row_wise(
            back_first, "back_first", (order(tokens), first_own, first_other, middle_grad), (table,), ((shape, F32),), 3, 3
        )
    )
    sums = order.done(tabulate(order(sums_one), sums_two, sums_out, table, bias_sum, bias_sum_x))
    sums_near = near(sums)
    up_kept, up_sent = order.done(summed(place, order(up_part), up_got_x, 1))
    up_got = swap(up_sent, "dp", 1)
    down_value = order.done(total_of(order(down_kept), down_got))
    down_got = on(down_value)
    rows_x, rows_z = rest_kept.shape[0], rest_kept.shape[0] // 2
    rest_part, slots, sent = order.done(
        ride(
            ride_first_kernel,
            "ride_first",
            ((rows_x, width), (TABLE, width), (rows_x + TABLE, width)),
            order(rest_kept),
            rest_kept_x,
            rest_got,
            sums,
            sums_near,
        )
    )
    rest_got = across(sent)
    first_kept, first_kept_x, first_sent = order.done(pair_halves(place, order(first_sum), first_sum_x, 1))
    first_got = swap(first_sent, "dp", 1)
    up_value = order.done(total_of(order(up_kept), up_got))
    up_got = on(up_value)
    rest_value, slots, sent = order.done(
        ride(
            ride_half_kernel,
            "ride_half",
            ((rows_z, width), (2 * TABLE, width), (rows_z + 2 * TABLE, width)),
            place,
            order(rest_part),
            rest_got,
            slots,
        )
    )
    rest_got = swap(sent, "dp", 2)
    slots = order.done(hold(order(slots)))
    for step in range(len(bits) - 1):
        last = step == len(bits) - 2
        held = (2 * slots.shape[0], width)
        outs = ((rows_z, width), held) if last else ((rows_z, width), held, (rows_z + held[0], width))
        results = order.done(
            ride(
                partial(ride_add_kernel, bit=2 if step == 0 else 3 + step),
                "ride_add",
                outs,
                place,
                order(rest_value),
                rest_got,
                slots,
            )
        )
        rest_value, slots = results[:2]
        rest_got = swap(rest_value, "dp", 2) if last else on(results[2], step)
        if step == 0:
            down_value = doubled(down_value, down_got)
            down_got = swap(down_value, "dp", 2)
            first_part_x, first_part = order.done(pair_total(order(first_kept), first_kept_x, first_got)[::-1])
            first_got = across(first_part_x)
            up_value = doubled(up_value, up_got)
            up_got = swap(up_value, "dp", 1)
            first_kept, first_sent = order.done(summed(place, order(first_part), first_got, 2))
            first_got = swap(first_sent, "dp", 2)
            down_value = order.done(lay(place, order(down_value), down_got, 2))
            down_got = swap(down_value, "dp", 1)
    first_value = order.done(total_of(order(first_kept), first_got))
    first_got = on(first_value)
    (rest_all,) = order.done(
        ride(
            ride_lay_kernel,
            "ride_lay",
            ((rows_x + slots.shape[0], width),),
            place,
            order(rest_value),
            rest_got,
            slots,
        )
    )
    rest_got = swap(rest_all, "dp", 1)
    first_value = doubled(first_value, first_got)
    first_got = swap(first_value, "dp", 2)
    up_value = order.done(lay(place, order(up_value), up_got, 1))
    up_got = swap(up_value, "dp", 2)
    down_grad = order.done(lay_out(place, order(down_value), down_got, 1))
    first_value = order.done(lay(place, order(first_value), first_got, 2))
    first_got = swap(first_value, "dp", 1)
    rest_total, ada_grad, totals = order.done(finish(place, order(rest_all), rest_got, rows_x))
    up_grad = order.done(lay_out(place, order(up_value), up_got, 2))
    out_rows = out_weight.shape[0]
    out_grad, qkv_grad = order.done(lay_and_cut(place, order(first_value), first_got, 1, rest_total, out_rows))
    return (
        output,
        input_gradient,
        totals[6],
        qkv_grad.T,
        out_grad,
        totals[7],
        up_grad,
        totals[9],
        down_grad,
        totals[8],
        ada_grad,
        totals[:6].reshape(6 * width),
    )


def solution(mesh):
    in_specs = (
        P(("dp", "mp"), None),
        P(("dp", "mp"), None),
        P("dp", None),
        P("dp"),
        P(),
        P(None, "mp"),
        P("mp", None),
        P(),
        P(None, "mp"),
        P("mp"),
        P("mp", None),
        P(),
        P(),
        P(),
    )
    out_specs = (
        P(("dp", "mp"), None),
        P(("dp", "mp"), None),
        P(),
        P(None, "mp"),
        P("mp", None),
        P(),
        P(None, "mp"),
        P("mp"),
        P("mp", None),
        P(),
        P(),
        P(),
    )
    return jax.shard_map(
        per_device, mesh=mesh, in_specs=in_specs, out_specs=out_specs, check_vma=False
    )
```

```python
from functools import partial
import math

import jax
import jax.numpy as jnp
from jax import lax
from jax.experimental import pallas as pl
from jax.experimental.pallas import tpu as pltpu
from jax.sharding import PartitionSpec as P

HEAD_DIM = 64
COND = 128
BLOCK = 256
STEP = 128
LANES = 128
BF16 = jnp.bfloat16
F32 = jnp.float32
TANH_SCALE = math.sqrt(2 / math.pi)
TANH_CUBE = 0.044715


def swap(value, axis, bit):
    size = lax.axis_size(axis)
    return lax.ppermute(value, axis, [(i, i ^ bit) for i in range(size)])


def time_features(time, axis, cond_width):
    half_width = cond_width // 2
    dims = (cond_width, 1) if axis == 0 else (1, cond_width)
    place = lax.broadcasted_iota(jnp.int32, dims, axis)
    second = place >= half_width
    ladder = jnp.where(second, place - half_width, place).astype(F32)
    angles = time.astype(F32) * jnp.exp(ladder * (-math.log(10000.0) / half_width))
    waves = jnp.where(second, jnp.sin(angles), jnp.cos(angles))
    return waves / (1.0 + jnp.exp(-waves))


def standard_score_rows(values):
    center = values - jnp.mean(values, axis=-1, keepdims=True)
    inverse_deviation = lax.rsqrt(jnp.mean(center * center, axis=-1, keepdims=True) + 1e-05)
    return (center * inverse_deviation, inverse_deviation)


def norm_reverse_pass(incoming_gradient, centered_scaled, inverse_deviation):
    return inverse_deviation * (
        incoming_gradient
        - jnp.mean(incoming_gradient, axis=-1, keepdims=True)
        - centered_scaled * jnp.mean(incoming_gradient * centered_scaled, axis=-1, keepdims=True)
    )


def dot(a, b):
    return jnp.dot(a, b, preferred_element_type=F32)


def contract_rows(a, b):
    return lax.dot_general(a, b, (((0,), (0,)), ((), ())), preferred_element_type=F32)


def times_transposed(a, b):
    return lax.dot_general(a, b, (((1,), (1,)), ((), ())), preferred_element_type=F32)


def one_line(lines_ref, first, width):
    return jnp.concatenate([lines_ref[first + k : first + k + 1, :] for k in range(width // LANES)], axis=1)


def in_vmem():
    return pl.BlockSpec(memory_space=pltpu.VMEM)


def in_smem():
    return pl.BlockSpec(memory_space=pltpu.SMEM)


def in_hbm(value):
    return pltpu.with_memory_space_constraint(value, pltpu.HBM)


def kept(dims, kind):
    return pltpu.VMEM(dims, kind)


def shape(dims, kind):
    return jax.ShapeDtypeStruct(dims, kind)


def cost(micros, size):
    return pl.CostEstimate(flops=int((micros + 12) * 1.1e9), bytes_accessed=size, transcendentals=0)


def small_cost(micros=0.001):
    return pl.CostEstimate(flops=int(micros * 1.1e9), bytes_accessed=10**4, transcendentals=0)


def parameters(mebibytes):
    return pltpu.CompilerParams(vmem_limit_bytes=mebibytes * 2**20)


def anywhere():
    return pl.BlockSpec(memory_space=pl.ANY)


def after(value, *tokens):
    return lax.optimization_barrier((value, *tokens))[0]


def rows_at(index, count):
    return pl.ds(pl.multiple_of(index * count, count), count)


def joined(target, pieces, mine, direct=0):
    rows = (target.shape[0] - direct) // 2
    for piece, index in zip(pieces, (mine, 1 - mine)):
        target[rows_at(index, rows), :] = piece[:rows, :]
    if direct:
        target[2 * rows :, :] = pieces[2][...]


def window_sizes(slot_length):
    return tuple(range(2 * STEP, slot_length + 1, STEP))


def block_window(lengths_ref, slot, block, slot_length):
    first = block * BLOCK
    last = first + BLOCK - 1
    end = jnp.int32(0)
    low = jnp.int32(0)
    high = jnp.int32(slot_length)
    for document in range(lengths_ref.shape[1]):
        end = end + lengths_ref[slot, document]
        low = jnp.where(end <= first, jnp.maximum(low, end), low)
        high = jnp.where(end > last, jnp.minimum(high, end), high)
    low = lax.div(low, jnp.int32(STEP)) * STEP
    size = jnp.maximum(lax.div(high - low + (STEP - 1), jnp.int32(STEP)) * STEP, 2 * STEP)
    return pl.multiple_of(jnp.minimum(low, slot_length - size), STEP), size


def mask_features(lengths_ref, slot, first, rows):
    documents = lengths_ref.shape[1]
    place = first + lax.broadcasted_iota(jnp.int32, (rows, HEAD_DIM), 0)
    lanes = lax.broadcasted_iota(jnp.int32, (rows, HEAD_DIM), 1)
    segment = jnp.zeros((rows, HEAD_DIM), jnp.int32)
    end = jnp.int32(0)
    for document in range(documents):
        end = end + lengths_ref[slot, document]
        segment = segment + jnp.where(place >= end, 1, 0)
    same = lanes == segment
    one = (lanes >= documents) & (lanes < documents + 3)
    key = jnp.where((lanes < documents) & jnp.logical_not(same), -1e30, jnp.where(one, 1.0, 0.0))
    return key.astype(BF16), jnp.where(same, 1.0, 0.0).astype(BF16)


def three_parts(value, lanes, at):
    first = value.astype(BF16).astype(F32)
    rest = value - first
    second = rest.astype(BF16).astype(F32)
    third = rest - second
    return jnp.where(lanes == at, first, jnp.where(lanes == at + 1, second, jnp.where(lanes == at + 2, third, 0.0)))


def attend_forward_kernel(place_ref, lengths_ref, own_ref, other_ref, *refs, fetched, keep):
    refs = list(refs)
    weight_refs = [refs.pop(0) for _ in range(2 if fetched else 1)]
    weight_ref = weight_refs[0]
    query_ref, key_ref, value_ref, out_ref = refs[:4]
    refs = refs[4:]
    slot = place_ref[3]
    documents = lengths_ref.shape[1]
    if keep:
        kept_ref = refs.pop(0)
    if fetched:
        joined_ref = refs.pop(0)
        joined(joined_ref, weight_refs, place_ref[1])
        weight_ref = joined_ref
    rows = own_ref.shape[0] // 2
    length = 2 * rows
    heads = weight_ref.shape[0] // (3 * HEAD_DIM)
    core = place_ref[0]
    lanes = lax.broadcasted_iota(jnp.int32, (rows, HEAD_DIM), 1)
    ones = jnp.where(lanes < 3, 1.0, 0.0).astype(BF16)
    for source, at in ((own_ref, core), (other_ref, 1 - core)):
        here = rows_at(at, rows)
        key_extra, query_extra = mask_features(lengths_ref, slot, at * rows, rows)
        if keep:
            kept_ref[here, :] = source[:rows, :]
        qkv = times_transposed(source[:rows, :], weight_ref[...]).astype(BF16)
        for head in range(heads):
            at = 3 * HEAD_DIM * head
            query = qkv[:, at : at + HEAD_DIM] * 0.125
            key = qkv[:, at + HEAD_DIM : at + 2 * HEAD_DIM]
            value = qkv[:, at + 2 * HEAD_DIM : at + 3 * HEAD_DIM]
            query_ref[head, here, :] = jnp.concatenate([query, query_extra], axis=1)
            key_ref[head, here, :] = jnp.concatenate([key, key_extra], axis=1)
            value_ref[head, here, :] = jnp.concatenate([value, ones], axis=1)

    def one_block(block, carry):
        here = rows_at(block, BLOCK)
        start, window = block_window(lengths_ref, slot, block, length)
        for size in window_sizes(length):

            @pl.when(window == size)
            def _():
                every = range(heads)
                span = pl.ds(start, size)
                queries = [query_ref[head, here, :] for head in every]
                scores = [times_transposed(queries[head], key_ref[head, span, :]) for head in every]
                wide = lax.broadcasted_iota(jnp.int32, (BLOCK, LANES), 1)
                mixed = []
                for head in every:
                    highest = jnp.max(scores[head], axis=1, keepdims=True)
                    raised = jnp.exp(scores[head] - highest).astype(BF16)
                    product = dot(raised, value_ref[head, span, :])
                    total = product[:, HEAD_DIM : HEAD_DIM + 1]
                    mixed.append(product[:, :HEAD_DIM] / total)
                    extra = three_parts(highest + jnp.log(total), wide, HEAD_DIM + documents)
                    query_ref[head, here, :] = (queries[head].astype(F32) - extra).astype(BF16)
                out_ref[here, :] = jnp.concatenate(mixed, axis=1).astype(BF16)

        return carry

    lax.fori_loop(0, length // BLOCK, one_block, 0)


def attend_forward(place, lengths, own, other, weights, keep):
    length, width = own.shape
    fetched = len(weights) == 2
    columns = weights[0].shape[0] * len(weights)
    heads = columns // (3 * HEAD_DIM)
    head_wise = kept((heads, length, LANES), BF16)
    outs = [head_wise] * 3 + [kept((length, heads * HEAD_DIM), BF16)]
    if keep:
        outs.append(kept((length, width), BF16))
    return pl.pallas_call(
        partial(attend_forward_kernel, fetched=fetched, keep=keep),
        out_shape=tuple(outs),
        in_specs=[in_smem()] * 2 + [in_vmem()] * (2 + len(weights)),
        out_specs=(in_vmem(),) * len(outs),
        scratch_shapes=[pltpu.VMEM((columns, width), BF16)] if fetched else [],
        compiler_params=parameters(24),
        cost_estimate=cost(9, 2**22),
        name="attend_forward",
    )(place, lengths, own, other, *weights)


def attend_backward_kernel(place_ref, lengths_ref, *refs, first, heads, extra):
    slot = place_ref[3]
    every = range(2 * heads)
    inputs = []
    for side in range(2):
        for head in range(heads):
            arrays = [refs[5 * side + k].at[first + head] for k in range(3)]
            inputs.append((*arrays, refs[5 * side + 3], refs[5 * side + 4], first + head))
    entry_ref = refs[10]
    refs = refs[11:]
    if extra:
        extras = refs[:2]
        refs = refs[2:]
        for side in range(2):
            refs[2 * side + 1][:extra, :] = extras[side][...]
    outs = refs[:4]
    key_turned_ref, upstream_ref, sum_ref, query_grad_ref, right_ref = refs[4:]
    length = entry_ref.shape[0]
    lanes = lax.broadcasted_iota(jnp.int32, (length, HEAD_DIM), 1)
    zero = jnp.zeros((length, HEAD_DIM), BF16)
    for item in every:
        query_ref, key_ref, value_ref, mixed_ref, grad_ref, head = inputs[item]
        columns = slice(head * HEAD_DIM, (head + 1) * HEAD_DIM)
        upstream = grad_ref[:, columns]
        inner = jnp.sum(mixed_ref[:, columns].astype(F32) * upstream.astype(F32), axis=1, keepdims=True)
        upstream_ref[item] = jnp.concatenate([upstream, -three_parts(inner, lanes, 0).astype(BF16)], axis=1)
        key_turned_ref[item] = key_ref[:, :HEAD_DIM].T
        right_ref[item, 0] = jnp.concatenate([upstream, zero], axis=1)
        right_ref[item, 1] = jnp.concatenate([zero, query_ref[:, :HEAD_DIM]], axis=1)
    sum_ref[...] = jnp.zeros_like(sum_ref)

    def one_block(block, carry):
        here = rows_at(block, BLOCK)
        start, window = block_window(lengths_ref, slot, block, length)
        for size in window_sizes(length):

            @pl.when(window == size)
            def _():
                span = pl.ds(start, size)
                queries = [inputs[s][0][here, :] for s in every]
                upstreams = [upstream_ref[s, here, :] for s in every]
                rights = [
                    jnp.concatenate([right_ref[s, 0, here, :], right_ref[s, 1, here, :]], axis=0) for s in every
                ]
                weights = [jnp.exp(times_transposed(inputs[s][1][span, :], queries[s])) for s in every]
                raised = [times_transposed(inputs[s][2][span, :], upstreams[s]) for s in every]
                score_grads = [(a * b).astype(BF16) for a, b in zip(weights, raised)]
                turned = []
                for s in every:
                    left = jnp.concatenate([weights[s].astype(BF16), score_grads[s]], axis=1)
                    sum_ref[s, span, :] += dot(left, rights[s])
                    turned.append(dot(key_turned_ref[s, :, span], score_grads[s]))
                turned = (jnp.concatenate(turned, axis=0) * 0.125).T
                for s in every:
                    query_grad_ref[s, here, :] = turned[:, s * HEAD_DIM : (s + 1) * HEAD_DIM].astype(BF16)

        return carry

    lax.fori_loop(0, length // BLOCK, one_block, 0)
    for side in (1, 0):
        for head in range(heads):
            item = side * heads + head
            sums = sum_ref[item]
            grads = jnp.concatenate(
                [query_grad_ref[item], sums[:, HEAD_DIM:].astype(BF16), sums[:, :HEAD_DIM].astype(BF16)], axis=1
            )
            outs[2 * side][head] = grads
            part = 3 * HEAD_DIM
            outs[2 * side + 1][extra + head * part : extra + (head + 1) * part, :] = contract_rows(grads, entry_ref[...]).astype(BF16)


def attend_backward(place, lengths, first, heads, sides, entry, extras):
    extra = extras[0].shape[0] if extras else 0
    length, width = entry.shape
    flat = [array for side in sides for array in side]
    outs = [kept((heads, length, 3 * HEAD_DIM), BF16), kept((extra + heads * 3 * HEAD_DIM, width), BF16)] * 2
    count = 2 * heads
    return pl.pallas_call(
        partial(attend_backward_kernel, first=first, heads=heads, extra=extra),
        out_shape=tuple(outs),
        in_specs=[in_smem()] * 2 + [in_vmem()] * (11 + len(extras)),
        out_specs=(in_vmem(),) * len(outs),
        scratch_shapes=[
            pltpu.VMEM((count, HEAD_DIM, length), BF16),
            pltpu.VMEM((count, length, LANES), BF16),
            pltpu.VMEM((count, length, LANES), F32),
            pltpu.VMEM((count, length, HEAD_DIM), BF16),
            pltpu.VMEM((count, 2, length, LANES), BF16),
        ],
        compiler_params=parameters(24),
        cost_estimate=cost(9 * heads, 2**22),
        name="attend_backward",
    )(place, lengths, *flat, entry, *extras)


def project_out_kernel(place_ref, mixed_ref, mixed_x_ref, weight_ref, weight_x_ref, own_ref, other_ref):
    rows = own_ref.shape[0]
    for target, at in ((other_ref, 1 - place_ref[0]), (own_ref, place_ref[0])):
        here = rows_at(at, rows)
        total = dot(mixed_ref[here, :], weight_ref[...]) + dot(mixed_x_ref[here, :], weight_x_ref[...])
        target[...] = total.astype(target.dtype)


def project_out(place, mixed, mixed_x, weight, weight_x):
    rows = mixed.shape[0] // 2
    width = weight.shape[1]
    return pl.pallas_call(
        project_out_kernel,
        out_shape=(kept((rows, width), F32), shape((rows, width), BF16)),
        in_specs=[in_smem()] + [in_vmem()] * 4,
        out_specs=(in_vmem(),) * 2,
        compiler_params=parameters(12),
        cost_estimate=cost(2, 2**22),
        name="project_out",
    )(place, mixed, mixed_x, weight, weight_x)


def project_back_kernel(
    place_ref, own_ref, other_ref, mixed_ref, mixed_x_ref, weight_ref, weight_x_ref,
    grad_ref, grad_x_ref, out_ref, out_x_ref, rows_ref,
):
    rows = own_ref.shape[0]
    rows_ref[rows_at(place_ref[0], rows), :] = own_ref[...]
    rows_ref[rows_at(1 - place_ref[0], rows), :] = other_ref[...]
    out_x_ref[...] = contract_rows(mixed_x_ref[...], rows_ref[...]).astype(BF16)
    out_ref[...] = contract_rows(mixed_ref[...], rows_ref[...]).astype(BF16)
    grad_ref[...] = times_transposed(rows_ref[...], weight_ref[...]).astype(BF16)
    grad_x_ref[...] = times_transposed(rows_ref[...], weight_x_ref[...]).astype(BF16)


def project_back(place, own, other, mixed, mixed_x, weight, weight_x):
    rows, width = own.shape
    return pl.pallas_call(
        project_back_kernel,
        out_shape=(kept(mixed.shape, BF16),) * 2 + (kept(weight.shape, BF16),) * 2,
        in_specs=[in_smem()] + [in_vmem()] * 6,
        out_specs=(in_vmem(),) * 4,
        scratch_shapes=[pltpu.VMEM((2 * rows, width), BF16)],
        compiler_params=parameters(14),
        cost_estimate=cost(3, 2**22),
        name="project_back",
    )(place, own, other, mixed, mixed_x, weight, weight_x)


def entry_back_kernel(place_ref, *refs, groups):
    grads = [[ref.at[k] for ref in refs[side * groups : (side + 1) * groups] for k in range(ref.shape[0])] for side in (0, 1)]
    weight_ref, first_ref, second_ref, own_ref, other_ref, joined_ref = refs[2 * groups :]
    rows = own_ref.shape[0]
    joined(joined_ref, (first_ref, second_ref), place_ref[1])
    for target, at in ((other_ref, 1 - place_ref[0]), (own_ref, place_ref[0])):
        here = rows_at(at, rows)
        left = jnp.concatenate([grad[here, :] for grad in grads[0]], axis=1)
        left_x = jnp.concatenate([grad[here, :] for grad in grads[1]], axis=1)
        total = dot(left, weight_ref[...]) + dot(left_x, joined_ref[...])
        target[...] = total.astype(target.dtype)


def entry_back(place, grads, grads_x, weight, weights_x):
    rows = grads[0].shape[1] // 2
    width = weight.shape[1]
    groups = len(grads)
    return pl.pallas_call(
        partial(entry_back_kernel, groups=groups),
        out_shape=(kept((rows, width), F32), shape((rows, width), BF16)),
        in_specs=[in_smem()] + [in_vmem()] * (2 * groups + 3),
        out_specs=(in_vmem(),) * 2,
        scratch_shapes=[pltpu.VMEM(weight.shape, BF16)],
        compiler_params=parameters(16),
        cost_estimate=cost(4, 2**22),
        name="entry_back",
    )(place, *grads, *grads_x, weight, *weights_x)


def hidden_grad(both, down):
    rows = both.shape[0] // 2
    units = down.shape[0]

    def kernel(both_ref, down_ref, out_ref):
        out_ref[...] = times_transposed(both_ref[rows:, :], down_ref[...])

    return pl.pallas_call(
        kernel,
        out_shape=kept((rows, units), F32),
        in_specs=[in_vmem()] * 2,
        out_specs=in_vmem(),
        compiler_params=parameters(8),
        cost_estimate=cost(1, 2**21),
        name="hidden_grad",
    )(both, down)


def hidden_kernel(place_ref, *refs, fetched):
    refs = list(refs)
    entries = refs[:2]
    upstreams = refs[2:4]
    if fetched:
        up_refs, down_refs = refs[4:6], refs[6:9]
        base = refs[9:11]
        refs = refs[11:]
    else:
        up_ref, bias_ref = refs[4:6]
        hidden_grads = refs[6:8]
        refs = refs[8:]
    grads = refs[:2]
    hidden_ref, bias_sum_ref = refs[2:4]
    if fetched:
        up_kept_ref, up_sent_ref, down_kept_ref, down_sent_ref = refs[4:8]
        up_all_ref, down_all_ref = refs[8:10]
        pre_grad_ref, sum_ref = refs[10:12]
        up_sum_ref = down_sum_ref = sum_ref
        direct = down_refs[2].shape[0]
        joined(up_all_ref, up_refs, place_ref[1])
        joined(down_all_ref, down_refs, place_ref[2], direct)
        up_ref, down_ref = up_all_ref, down_all_ref
    else:
        up_sum_ref, down_sum_ref, pre_grad_ref = refs[4:7]
    rows, width = entries[0].shape
    units = up_ref.shape[1]
    bias_sum = [jnp.zeros((1, BLOCK), F32) for _ in range(units // BLOCK)]
    if fetched:
        at = (units - direct) // 2
        bias = down_refs[0][at : at + 16, :].astype(F32)[:1]
    else:
        bias = one_line(bias_ref, 0, units).astype(F32)
    for part in range(2):
        there = slice(part * rows, (part + 1) * rows)
        entry = entries[part][...]
        upstream = upstreams[part][rows:, :]
        for block in range(units // BLOCK):
            cut = slice(block * BLOCK, (block + 1) * BLOCK)
            pre = dot(entry, up_ref[:, cut]) + bias[:, cut]
            given = times_transposed(upstream, down_ref[cut, :]) if fetched else hidden_grads[part][:, cut]
            square = pre * pre
            half = 0.5 + 0.5 * jnp.tanh(pre * (TANH_SCALE + (TANH_SCALE * TANH_CUBE) * square))
            hidden = pre * half
            slope = half + (hidden - hidden * half) * (2 * TANH_SCALE + (6 * TANH_SCALE * TANH_CUBE) * square)
            pre_grad = (given * slope).astype(BF16)
            hidden_ref[there, cut] = hidden.astype(BF16)
            pre_grad_ref[there, cut] = pre_grad
            bias_sum[block] = bias_sum[block] + jnp.sum(pre_grad.astype(F32), axis=0, keepdims=True)
    bias_sum_ref[...] = jnp.zeros_like(bias_sum_ref)
    bias_sum_ref[0:1, :] = jnp.concatenate(bias_sum, axis=1)
    for part in (1, 0):
        grad = times_transposed(pre_grad_ref[part * rows : (part + 1) * rows, :], up_ref[...])
        if fetched:
            grad = grad + base[part][...]
        grads[part][...] = grad.astype(grads[part].dtype)
    half = units // 2
    for block in range(units // BLOCK):
        cut = slice(block * BLOCK, (block + 1) * BLOCK)
        total = contract_rows(entries[0][...], pre_grad_ref[:rows, cut]) + contract_rows(entries[1][...], pre_grad_ref[rows:, cut])
        up_sum_ref[:, cut] = total.astype(BF16)
    if fetched:
        up_sent_ref[...] = sum_ref[rows_at(1 - place_ref[2], width // 2), :]
        up_kept_ref[...] = sum_ref[rows_at(place_ref[2], width // 2), :]
    for block in range(units // BLOCK):
        cut = slice(block * BLOCK, (block + 1) * BLOCK)
        total = contract_rows(hidden_ref[:rows, cut], upstreams[0][rows:, :]) + contract_rows(hidden_ref[rows:, cut], upstreams[1][rows:, :])
        down_sum_ref[cut, :] = total.astype(BF16)
    if fetched:
        down_sent_ref[...] = sum_ref[rows_at(1 - place_ref[1], half), :]
        down_kept_ref[...] = sum_ref[rows_at(place_ref[1], half), :]


def hidden_part(place, entries, upstreams, weights, others, fetched):
    rows, width = entries[0].shape
    units = weights[0].shape[1]
    inputs = [*entries, *upstreams, *weights, *others]
    outs = [kept((rows, width), F32), shape((rows, width), BF16) if fetched else kept((rows, width), F32)]
    outs += [kept((2 * rows, units), BF16), shape((8, units), F32)]
    if fetched:
        outs += [kept((width // 2, units), BF16), shape((width // 2, units), BF16)]
        outs += [kept((units // 2, width), BF16), shape((units // 2, width), BF16)]
        outs += [kept((width, units), BF16), kept((units, width), BF16)]
    else:
        outs += [kept((width, units), BF16), kept((units, width), BF16)]
    return pl.pallas_call(
        partial(hidden_kernel, fetched=fetched),
        out_shape=tuple(outs),
        in_specs=[in_smem()] + [in_vmem()] * len(inputs),
        out_specs=(in_vmem(),) * len(outs),
        scratch_shapes=[pltpu.VMEM((2 * rows, units), BF16)] + [pltpu.VMEM((width, units), BF16)] * fetched,
        compiler_params=parameters(24),
        cost_estimate=cost(10, 2**23),
        name="hidden_part",
    )(place, *inputs)


def hidden_out_kernel(hidden_ref, hidden_x_ref, down_ref, down_x_ref, out_ref, *, part):
    rows = out_ref.shape[0]
    there = slice(part * rows, (part + 1) * rows)
    out = dot(hidden_ref[there, :], down_ref[...]) + dot(hidden_x_ref[there, :], down_x_ref[...])
    out_ref[...] = out.astype(out_ref.dtype)


def hidden_out(hidden, hidden_x, down, down_x, part, kind):
    rows, width = hidden.shape[0] // 2, down.shape[1]
    return pl.pallas_call(
        partial(hidden_out_kernel, part=part),
        out_shape=(kept if kind == F32 else shape)((rows, width), kind),
        in_specs=[in_vmem()] * 4,
        out_specs=in_vmem(),
        compiler_params=parameters(12),
        cost_estimate=cost(2, 2**22),
        name="hidden_out",
    )(hidden, hidden_x, down, down_x)


ROWS = 128


def row_wise(body, name, row_inputs, whole_inputs, row_outs, sums, micros):
    rows, width = row_inputs[0].shape
    outs = [make((rows, width), kind) for make, kind in row_outs]
    if sums:
        outs.append(kept((8, width), F32))

    def kernel(*refs):
        refs = list(refs)
        row_refs = [refs.pop(0) for _ in row_inputs]
        whole_refs = [refs.pop(0) for _ in whole_inputs]

        def tile(step, total):
            here = rows_at(step, ROWS)
            results, terms = body(*[ref[here, :] for ref in row_refs], *whole_refs)
            for ref, result in zip(refs, results):
                ref[here, :] = result.astype(ref.dtype)
            return tuple(
                old + jnp.sum(term.reshape(ROWS // 8, 8, width), axis=0) for old, term in zip(total, terms)
            )

        total = lax.fori_loop(0, rows // ROWS, tile, (jnp.zeros((8, width), F32),) * sums)
        if sums:
            lines = [jnp.sum(term, axis=0, keepdims=True) for term in total]
            refs[-1][...] = jnp.concatenate(lines + [jnp.zeros((8 - sums, width), F32)], axis=0)

    return pl.pallas_call(
        kernel,
        out_shape=tuple(outs),
        in_specs=[in_vmem()] * (len(row_inputs) + len(whole_inputs)),
        out_specs=(in_vmem(),) * len(outs),
        compiler_params=parameters(18),
        cost_estimate=cost(micros, 2**20),
        name=name,
    )(*row_inputs, *whole_inputs)


def enter_kernel(place_ref, time_ref, tokens_ref, cotangent_ref, weight_ref, *refs):
    vectors, (table_ref, both_ref) = refs[:-2], refs[-2:]
    rows, width = tokens_ref.shape
    table_ref[...] = jnp.zeros_like(table_ref)
    row = 0
    for vector in vectors:
        for at in range(0, vector.shape[0], width // LANES):
            table_ref[row : row + 1, :] = one_line(vector, at, width)
            row += 1
    features = time_features(time_ref[place_ref[3]], 0, COND)
    for piece in range(6):
        cut = slice(piece * width, (piece + 1) * width)
        table_ref[piece : piece + 1, :] += jnp.sum(features * weight_ref[:, cut], axis=0, keepdims=True)
    table_ref[row : row + 1, :COND] = time_features(time_ref[place_ref[3]], 1, COND)
    table = table_ref[...]

    def tile(step, carry):
        here = rows_at(step, ROWS)
        scored, _ = standard_score_rows(tokens_ref[here, :].astype(F32))
        entry = scored * table[6:7] * (1.0 + table[1:2]) + table[0:1]
        both_ref[here, :] = entry.astype(BF16)
        there = pl.ds(pl.multiple_of(rows + step * ROWS, ROWS), ROWS)
        both_ref[there, :] = (table[5:6] * cotangent_ref[here, :].astype(F32)).astype(BF16)
        return carry

    lax.fori_loop(0, rows // ROWS, tile, 0)


def enter(place, time_index, tokens, cotangent, weight, vectors):
    vectors = [vector.reshape(-1, LANES) for vector in vectors]
    rows, width = tokens.shape
    return pl.pallas_call(
        enter_kernel,
        out_shape=(shape((16, width), F32), shape((2 * rows, width), BF16)),
        in_specs=[in_smem()] * 2 + [in_vmem()] * (3 + len(vectors)),
        out_specs=(in_vmem(),) * 2,
        compiler_params=parameters(14),
        cost_estimate=cost(4, 2**22),
        name="enter",
    )(place, time_index, in_hbm(tokens), in_hbm(cotangent), in_hbm(weight), *[in_hbm(vector) for vector in vectors])


def enter_second(tokens, branch_own, branch_other, modulation):
    branch = branch_own + branch_other.astype(F32)
    middle = tokens.astype(F32) + modulation[2:3, :] * branch
    scored, _ = standard_score_rows(middle)
    entry = scored * modulation[7:8, :] * (1.0 + modulation[4:5, :]) + modulation[3:4, :]
    return (middle, entry), ()


def leave(middle, cotangent, out_own, out_other, modulation):
    branch = out_own + out_other.astype(F32) + modulation[8:9, :]
    incoming = cotangent.astype(F32)
    branch_grad = (modulation[5:6, :] * incoming).astype(BF16).astype(F32)
    return (middle + modulation[5:6, :] * branch,), (incoming * branch, branch_grad)


def back_second(middle, cotangent, grad_own, grad_other, branch_own, branch_other, modulation):
    gain = modulation[7:8, :]
    scored, inverse = standard_score_rows(middle)
    entry_grad = grad_own + grad_other.astype(F32)
    normed_grad = entry_grad * (1.0 + modulation[4:5, :])
    middle_grad = cotangent.astype(F32) + norm_reverse_pass(normed_grad * gain, scored, inverse)
    branch = branch_own + branch_other.astype(F32)
    terms = (middle_grad * branch, entry_grad, entry_grad * (scored * gain), normed_grad * scored)
    return (modulation[2:3, :] * middle_grad, middle_grad), terms


def back_first(tokens, grad_own, grad_other, middle_grad, modulation):
    gain = modulation[6:7, :]
    scored, inverse = standard_score_rows(tokens.astype(F32))
    entry_grad = grad_own + grad_other.astype(F32)
    normed_grad = entry_grad * (1.0 + modulation[1:2, :])
    grad = middle_grad + norm_reverse_pass(normed_grad * gain, scored, inverse)
    return (grad,), (entry_grad, entry_grad * (scored * gain), normed_grad * scored)


def piece_kernel(place_ref, source_ref, *refs, rows, bit):
    if len(refs) == 2:
        refs[1][rows:, :] = jnp.zeros_like(refs[1][rows:, :])
        refs[1][rows : rows + 1, :] = one_line(refs[0], 0, refs[1].shape[1])
    refs[-1][:rows, :] = source_ref[rows_at(place_ref[bit], rows), :]


def own_piece(place, source, rows, bit, line=None):
    extra = [] if line is None else [line.reshape(-1, LANES)]
    return pl.pallas_call(
        partial(piece_kernel, rows=rows, bit=bit),
        out_shape=shape((rows + 16 * len(extra), source.shape[1]), source.dtype),
        in_specs=[in_smem()] + [in_vmem()] * (1 + len(extra)),
        out_specs=in_vmem(),
        compiler_params=parameters(8),
        cost_estimate=small_cost(),
        name="own_piece",
    )(place, in_hbm(source), *extra)


def lower_half(source):
    rows, width = source.shape

    def kernel(source_ref, out_ref):
        out_ref[...] = source_ref[rows // 2 :, :]

    return pl.pallas_call(
        kernel,
        out_shape=shape((rows // 2, width), source.dtype),
        in_specs=[in_vmem()],
        out_specs=in_vmem(),
        compiler_params=parameters(8),
        cost_estimate=small_cost(),
        name="lower_half",
    )(in_hbm(source))


def sum_kernel(place_ref, a_ref, b_ref, kept_ref, sent_ref, *, bit):
    half = kept_ref.shape[0]
    for out, index in ((sent_ref, 1 - place_ref[bit]), (kept_ref, place_ref[bit])):
        here = rows_at(index, half)
        out[...] = (a_ref[here, :].astype(F32) + b_ref[here, :].astype(F32)).astype(BF16)


def summed(place, a, b, bit):
    rows, width = a.shape
    return pl.pallas_call(
        partial(sum_kernel, bit=bit),
        out_shape=(kept((rows // 2, width), BF16),) * 2,
        in_specs=[in_smem(), in_vmem(), in_vmem()],
        out_specs=(in_vmem(),) * 2,
        compiler_params=parameters(8),
        cost_estimate=small_cost(3),
        name="summed",
    )(place, a, b)


def total_kernel(a_ref, b_ref, out_ref):
    out_ref[...] = (a_ref[...].astype(F32) + b_ref[...].astype(F32)).astype(BF16)


def total_of(a, b):
    return pl.pallas_call(
        total_kernel,
        out_shape=kept(a.shape, BF16),
        in_specs=[in_vmem()] * 2,
        out_specs=in_vmem(),
        compiler_params=parameters(8),
        cost_estimate=small_cost(3),
        name="total_of",
    )(a, b)


def pair_kernel(place_ref, a_ref, b_ref, kept_a_ref, kept_b_ref, sent_ref, *, bit):
    half = kept_a_ref.shape[0]
    mine, other = rows_at(place_ref[bit], half), rows_at(1 - place_ref[bit], half)
    sent_ref[:half, :] = a_ref[other, :]
    sent_ref[half:, :] = b_ref[other, :]
    kept_a_ref[...] = a_ref[mine, :]
    kept_b_ref[...] = b_ref[mine, :]


def pair_halves(place, a, b, bit):
    rows, width = a.shape
    half = kept((rows // 2, width), BF16)
    return pl.pallas_call(
        partial(pair_kernel, bit=bit),
        out_shape=(half, half, kept((rows, width), BF16)),
        in_specs=[in_smem(), in_vmem(), in_vmem()],
        out_specs=(in_vmem(),) * 3,
        compiler_params=parameters(8),
        cost_estimate=small_cost(3),
        name="pair_halves",
    )(place, a, b)


def halves_kernel(place_ref, source_ref, kept_ref, sent_ref, *, bit):
    half = kept_ref.shape[0]
    sent_ref[...] = source_ref[rows_at(1 - place_ref[bit], half), :]
    kept_ref[...] = source_ref[rows_at(place_ref[bit], half), :]


def halves(place, source, bit):
    rows, width = source.shape
    return pl.pallas_call(
        partial(halves_kernel, bit=bit),
        out_shape=(kept((rows // 2, width), BF16),) * 2,
        in_specs=[in_smem(), in_vmem()],
        out_specs=(in_vmem(),) * 2,
        compiler_params=parameters(8),
        cost_estimate=small_cost(3),
        name="halves",
    )(place, source)


def pair_total_kernel(a_ref, b_ref, got_ref, out_a_ref, out_b_ref):
    half = a_ref.shape[0]
    out_b_ref[...] = (b_ref[...].astype(F32) + got_ref[half:, :].astype(F32)).astype(BF16)
    out_a_ref[...] = (a_ref[...].astype(F32) + got_ref[:half, :].astype(F32)).astype(BF16)


def pair_total(a, b, got):
    return pl.pallas_call(
        pair_total_kernel,
        out_shape=(kept(a.shape, BF16),) * 2,
        in_specs=[in_vmem()] * 3,
        out_specs=(in_vmem(),) * 2,
        compiler_params=parameters(8),
        cost_estimate=small_cost(3),
        name="pair_total",
    )(a, b, got)


def two_totals_kernel(a_ref, b_ref, c_ref, d_ref, first_ref, second_ref):
    first_ref[...] = (a_ref[...].astype(F32) + b_ref[...].astype(F32)).astype(BF16)
    second_ref[...] = (c_ref[...].astype(F32) + d_ref[...].astype(F32)).astype(BF16)


def two_totals(a, b, c, d):
    return pl.pallas_call(
        two_totals_kernel,
        out_shape=(kept(a.shape, BF16), kept(c.shape, BF16)),
        in_specs=[in_vmem()] * 4,
        out_specs=(in_vmem(),) * 2,
        compiler_params=parameters(8),
        cost_estimate=small_cost(3),
        name="two_totals",
    )(a, b, c, d)


def send_rows(whole_ref, at, out_ref, out_at, count, sem):
    copy = pltpu.make_async_copy(whole_ref.at[pl.ds(at, count), :], out_ref.at[pl.ds(out_at, count), :], sem)
    copy.start()
    return copy


def lay_and_cut_kernel(place_ref, own_ref, other_ref, behind_ref, first_ref, second_ref, whole_ref, sems, *, bit):
    rows, cut, rest = own_ref.shape[0], first_ref.shape[0], behind_ref.shape[0]
    copies = [send_rows(behind_ref, 0, second_ref, 2 * rows - cut, rest // 2, sems.at[0])]
    copies.append(send_rows(behind_ref, rest // 2, second_ref, 2 * rows - cut + rest // 2, rest - rest // 2, sems.at[1]))
    for ref, index in ((own_ref, place_ref[bit]), (other_ref, 1 - place_ref[bit])):
        whole_ref[rows_at(index, rows), :] = ref[...].astype(whole_ref.dtype)
    copies.append(send_rows(whole_ref, 0, first_ref, 0, cut, sems.at[2]))
    copies.append(send_rows(whole_ref, cut, second_ref, 0, 2 * rows - cut, sems.at[3]))
    for copy in copies:
        copy.wait()


def lay_and_cut(place, own, other, bit, behind, cut):
    rows, width = own.shape
    return pl.pallas_call(
        partial(lay_and_cut_kernel, bit=bit),
        out_shape=(shape((cut, width), F32), shape((2 * rows - cut + behind.shape[0], width), F32)),
        in_specs=[in_smem()] + [in_vmem()] * 3,
        out_specs=(anywhere(),) * 2,
        scratch_shapes=[pltpu.VMEM((2 * rows, width), F32), pltpu.SemaphoreType.DMA((4,))],
        compiler_params=parameters(14),
        cost_estimate=small_cost(3),
        name="lay_and_cut",
    )(place, own, other, behind)


def lay_straight_kernel(place_ref, own_ref, other_ref, out_ref, *, bit):
    rows = own_ref.shape[0]
    for ref, index in ((own_ref, place_ref[bit]), (other_ref, 1 - place_ref[bit])):
        out_ref[rows_at(index, rows), :] = ref[...].astype(out_ref.dtype)


def lay(place, own, other, bit):
    rows, width = own.shape
    return pl.pallas_call(
        partial(lay_straight_kernel, bit=bit),
        out_shape=kept((2 * rows, width), BF16),
        in_specs=[in_smem()] + [in_vmem()] * 2,
        out_specs=in_vmem(),
        compiler_params=parameters(8),
        cost_estimate=small_cost(3),
        name="lay",
    )(place, own, other)


def lay_out_kernel(place_ref, own_ref, other_ref, out_ref, whole_ref, sems, *, bit, parts):
    rows = own_ref.shape[0]
    count = rows // parts
    copies = []
    for which, (ref, index) in enumerate(((own_ref, place_ref[bit]), (other_ref, 1 - place_ref[bit]))):
        for part in range(parts):
            at = which * rows + part * count
            whole_ref[at : at + count, :] = ref[part * count : (part + 1) * count, :].astype(F32)
            target = pl.multiple_of(index * rows + part * count, count)
            copies.append(send_rows(whole_ref, at, out_ref, target, count, sems.at[which * parts + part]))
    for copy in copies:
        copy.wait()


def lay_out(place, own, other, bit):
    rows, width = own.shape
    parts = 3
    return pl.pallas_call(
        partial(lay_out_kernel, bit=bit, parts=parts),
        out_shape=shape((2 * rows, width), F32),
        in_specs=[in_smem()] + [in_vmem()] * 2,
        out_specs=anywhere(),
        scratch_shapes=[pltpu.VMEM((2 * rows, width), F32), pltpu.SemaphoreType.DMA((2 * parts,))],
        compiler_params=parameters(14),
        cost_estimate=small_cost(3),
        name="lay_out",
    )(place, own, other)


def lay_four_kernel(place_ref, *refs):
    parts, (out_ref, whole_ref, sems) = refs[:4], refs[4:]
    rows = parts[0].shape[0]
    copies = []
    for which, ref in enumerate(parts):
        side, turn = which // 2, which % 2
        first = place_ref[1] if side == 0 else 1 - place_ref[1]
        second = place_ref[2] if turn == 0 else 1 - place_ref[2]
        whole_ref[which * rows : (which + 1) * rows, :] = ref[...].astype(F32)
        target = pl.multiple_of((first * 2 + second) * rows, rows)
        copies.append(send_rows(whole_ref, which * rows, out_ref, target, rows, sems.at[which]))
    for copy in copies:
        copy.wait()


def lay_four(place, *parts):
    rows, width = parts[0].shape
    return pl.pallas_call(
        lay_four_kernel,
        out_shape=shape((4 * rows, width), F32),
        in_specs=[in_smem()] + [in_vmem()] * 4,
        out_specs=anywhere(),
        scratch_shapes=[pltpu.VMEM((4 * rows, width), F32), pltpu.SemaphoreType.DMA((4,))],
        compiler_params=parameters(14),
        cost_estimate=small_cost(3),
        name="lay_four",
    )(place, *parts)


TABLE = 16


def tabulate_kernel(first_ref, second_ref, last_ref, table_ref, bias_ref, bias_x_ref, out_ref):
    rows = [first_ref[0:2, :], second_ref[0:3, :], last_ref[0:1, :], first_ref[2:3, :], second_ref[3:4, :], last_ref[1:2, :]]
    rows += [table_ref[9:10, :], bias_ref[0:1, :], bias_x_ref[0:1, :], jnp.zeros((TABLE - 12, out_ref.shape[1]), F32)]
    out_ref[...] = jnp.concatenate(rows, axis=0)


def tabulate(*parts):
    return pl.pallas_call(
        tabulate_kernel,
        out_shape=shape((TABLE, parts[0].shape[1]), F32),
        in_specs=[in_vmem()] * 6,
        out_specs=in_vmem(),
        compiler_params=parameters(8),
        cost_estimate=cost(1, 2**18),
        name="tabulate",
    )(*parts)


def lay_table(out_ref, at, own, other, side):
    rows = own.shape[0]
    out_ref[pl.ds(pl.multiple_of(at + side * rows, TABLE), rows), :] = own
    out_ref[pl.ds(pl.multiple_of(at + (1 - side) * rows, TABLE), rows), :] = other


def ride_first_kernel(kept_ref, kept_x_ref, got_ref, own_ref, near_ref, part_ref, table_ref, out_ref):
    half = kept_ref.shape[0]
    own = own_ref[...]
    row = lax.broadcasted_iota(jnp.int32, own.shape, 0)
    table = jnp.where(row < 9, own + near_ref[...], own).astype(BF16)
    out_ref[:half, :] = (kept_x_ref[...].astype(F32) + got_ref[half:, :].astype(F32)).astype(BF16)
    out_ref[half:, :] = table
    table_ref[...] = table
    part_ref[...] = (kept_ref[...].astype(F32) + got_ref[:half, :].astype(F32)).astype(BF16)


def ride_half_kernel(place_ref, part_ref, got_ref, table_ref, kept_ref, next_ref, out_ref):
    half, rows = kept_ref.shape[0], table_ref.shape[0]
    mine, other = rows_at(place_ref[2], half), rows_at(1 - place_ref[2], half)
    out_ref[:half, :] = (part_ref[other, :].astype(F32) + got_ref[other, :].astype(F32)).astype(BF16)
    kept_ref[...] = (part_ref[mine, :].astype(F32) + got_ref[mine, :].astype(F32)).astype(BF16)
    lay_table(next_ref, 0, table_ref[...], got_ref[2 * half :, :], place_ref[3])
    out_ref[half:, :] = next_ref[...]


def ride_add_kernel(place_ref, value_ref, got_ref, table_ref, sum_ref, next_ref, *outs, bit):
    rows = value_ref.shape[0]
    total = (value_ref[...].astype(F32) + got_ref[:rows, :].astype(F32)).astype(BF16)
    sum_ref[...] = total
    lay_table(next_ref, 0, table_ref[...], got_ref[rows:, :], place_ref[bit])
    for out in outs:
        out[:rows, :] = total
        out[rows:, :] = next_ref[...]


def ride_lay_kernel(place_ref, own_ref, other_ref, table_ref, out_ref):
    rows = own_ref.shape[0]
    for ref, index in ((own_ref, place_ref[2]), (other_ref, 1 - place_ref[2])):
        out_ref[rows_at(index, rows), :] = ref[...]
    out_ref[2 * rows :, :] = table_ref[...]


def ride(kernel, name, outs, *inputs):
    scalars = [in_smem()] if inputs[0].ndim == 1 else []
    return pl.pallas_call(
        kernel,
        out_shape=tuple(kept(dims, BF16) for dims in outs),
        in_specs=scalars + [in_vmem()] * (len(inputs) - len(scalars)),
        out_specs=(in_vmem(),) * len(outs),
        compiler_params=parameters(8),
        cost_estimate=small_cost(3),
        name=name,
    )(*inputs)


def hold_kernel(source_ref, *refs):
    refs[-1][...] = source_ref[...]


def hold(value, *tokens):
    return pl.pallas_call(
        hold_kernel,
        out_shape=kept(value.shape, value.dtype),
        in_specs=[in_vmem()] + [anywhere()] * len(tokens),
        out_specs=in_vmem(),
        compiler_params=parameters(8),
        cost_estimate=small_cost(3) if tokens else cost(3, 2**18),
        name="hold",
    )(value, *tokens)


def put_lines(out_ref, first, row):
    for k in range(row.shape[1] // LANES):
        out_ref[first + k : first + k + 1, :] = row[:, k * LANES : (k + 1) * LANES]


def finish_kernel(place_ref, own_ref, got_ref, sum_ref, grad_ref, bias_ref, one_ref, two_ref, down_ref, up_ref, line_ref, grad_all_ref, sems, *, half):
    for ref, index in ((own_ref, place_ref[1]), (got_ref, 1 - place_ref[1])):
        sum_ref[pl.ds(pl.multiple_of(index * half, 16), half), :] = ref[:half, :].astype(F32)
    slots, width = (own_ref.shape[0] - half) // TABLE, own_ref.shape[1]
    for ref, index in ((own_ref, place_ref[1]), (got_ref, 1 - place_ref[1])):

        def one_slot(slot, carry, ref=ref, index=index):
            lines = ref[pl.ds(pl.multiple_of(half + slot * TABLE, TABLE), TABLE), :].astype(F32)
            for row in range(12):
                line_ref[row, pl.ds(index * slots + slot, 1), :] = lines[row : row + 1]
            return carry

        lax.fori_loop(0, slots, one_slot, 0)
    features = line_ref[9][:, :COND].astype(BF16)
    copies = []
    lines = width // LANES
    targets = [(bias_ref, piece * lines) for piece in range(6)] + [(one_ref, 0), (two_ref, 0), (down_ref, 0)]
    for piece, (target, first) in enumerate(targets):
        terms = line_ref[piece]
        put_lines(target, first, jnp.sum(terms, axis=0, keepdims=True))
        if piece < 6:
            grad_all_ref[piece] = contract_rows(features, terms.astype(BF16))
            copy = pltpu.make_async_copy(
                grad_all_ref.at[piece], grad_ref.at[:, pl.ds(piece * width, width)], sems.at[piece]
            )
            copy.start()
            copies.append(copy)
    slot = lax.broadcasted_iota(jnp.int32, (2 * slots, width), 0)
    mine = lax.rem(slot, 2) == place_ref[3]
    put_lines(up_ref, 0, jnp.sum(jnp.where(mine, line_ref[10], line_ref[11]), axis=0, keepdims=True))
    for copy in copies:
        copy.wait()


def finish(place, own, got, half):
    width = own.shape[1]
    slots = 2 * (own.shape[0] - half) // TABLE
    lines = width // LANES
    return pl.pallas_call(
        partial(finish_kernel, half=half),
        out_shape=(
            kept((2 * half, width), F32),
            shape((COND, 6 * width), F32),
            shape((6 * lines, LANES), F32),
        )
        + (shape((lines, LANES), F32),) * 4,
        in_specs=[in_smem()] + [in_vmem()] * 2,
        out_specs=(in_vmem(), anywhere()) + (in_vmem(),) * 5,
        scratch_shapes=[
            pltpu.VMEM((12, slots, width), F32),
            pltpu.VMEM((6, COND, width), F32),
            pltpu.SemaphoreType.DMA((6,)),
        ],
        compiler_params=parameters(20),
        cost_estimate=cost(3, 2**20),
        name="finish",
    )(place, own, got)


class Order:
    def __init__(self):
        self.token = ()

    def __call__(self, value):
        return after(value, *self.token) if self.token else value

    def done(self, result):
        self.token = (result[-1] if isinstance(result, (tuple, list)) else result,)
        return result


def dp_bits():
    bits = []
    bit = 1
    while bit < lax.axis_size("dp"):
        bits.append(bit)
        bit *= 2
    return bits


def per_device(
    tokens,
    cotangent,
    doc_lengths,
    time_index,
    attention_norm_gain,
    qkv_weight,
    out_weight,
    feedforward_norm_gain,
    up_weight,
    up_bias,
    down_weight,
    down_bias,
    ada_weight,
    ada_bias,
):
    rows, width = tokens.shape
    core = lax.axis_index("mp") % 2
    slot = lax.axis_index("mp") // 2
    index = lax.axis_index("dp")
    bits = dp_bits()
    place = [core, index % 2, index // 2 % 2, slot] + [index // bit % 2 for bit in bits[2:]]
    place = jnp.stack(place).astype(jnp.int32)
    order = Order()

    def near(value):
        return swap(value, "mp", 1)

    def across(value):
        return swap(value, "mp", 2)

    def relayed(value):
        return swap(value, "dp", 1)

    qkv_turned = qkv_weight.T
    qkv_half = order.done(own_piece(place, qkv_turned, qkv_turned.shape[0] // 2, 1))
    qkv_a = across(qkv_half)
    table, both = order.done(
        enter(
            place,
            time_index,
            order(tokens),
            cotangent,
            ada_weight,
            (ada_bias, attention_norm_gain, feedforward_norm_gain, down_bias),
        )
    )
    both_near = near(both)
    out_weight_x = across(order(out_weight))
    up_half = order.done(own_piece(place, order(up_weight), width // 2, 1))
    up_a = across(up_half)
    quarter = down_weight.shape[0] // 4
    down_part = order.done(own_piece(place, order(down_weight), quarter, 2, up_bias))
    down_a = across(down_part)
    down_lower = order.done(lower_half(order(down_weight)))
    table = order.done(hold(after(order(table), qkv_a)))
    qkv_b = swap(qkv_a, "dp", 1)

    query, key, value, mixture, entry_one_all = order.done(
        attend_forward(place, doc_lengths, order(both), both_near, (qkv_turned,), True)
    )
    down_straight = across(order(down_lower))
    query_x, key_x, value_x, mixture_x = order.done(
        attend_forward(place, doc_lengths, order(both), both_near, (qkv_a, qkv_b), False)
    )
    branch_own, branch_other = order.done(project_out(place, mixture, order(mixture_x), out_weight, out_weight_x))
    branch_other = near(branch_other)
    grad_one = order.done(hidden_grad(order(both), down_weight))
    up_b = swap(after(up_a, grad_one), "dp", 1)
    middle, entry_two = order.done(
        row_wise(
            enter_second, "enter_second", (order(tokens), branch_own, after(branch_other, up_a)), (table,), ((kept, F32), (shape, BF16)), 0, 3
        )
    )
    entry_two_near = near(entry_two)
    grad_two = order.done(hidden_grad(order(both_near), down_weight))
    down_b = swap(after(down_a, grad_two), "dp", 2)
    entries_two = (entry_two, after(entry_two_near, down_a))

    grad_base, grad_base_near, hidden, bias_sum, up_sum, down_sum = order.done(
        hidden_part(
            place,
            entries_two,
            (order(both), both_near),
            (up_weight, up_bias.reshape(-1, LANES)),
            (grad_one, grad_two),
            False,
        )
    )
    grad_own, grad_other, hidden_x, bias_sum_x, up_kept_x, up_sent_x, down_kept_x, down_sent_x, _, down_weight_x = order.done(
        hidden_part(
            place,
            (order(entries_two[0]), entries_two[1]),
            (both, both_near),
            (up_a, up_b, down_a, down_b, down_straight),
            (grad_base, grad_base_near),
            True,
        )
    )
    grad_other = near(grad_other)
    out_other = order.done(hidden_out(order(hidden), hidden_x, down_weight, down_weight_x, 1, BF16))
    out_other = near(out_other)
    down_got_x = swap(order(down_sent_x), "dp", 1)
    up_got_x = swap(order(up_sent_x), "dp", 2)
    attn_grad, middle_grad, sums_two = order.done(
        row_wise(
            back_second,
            "back_second",
            (order(middle), cotangent, grad_own, grad_other, branch_own, branch_other),
            (table,),
            ((shape, BF16), (kept, F32)),
            4,
            4,
        )
    )
    attn_grad_near = near(attn_grad)
    out_own = order.done(hidden_out(order(hidden), hidden_x, down_weight, down_weight_x, 0, F32))
    mixture_grad, mixture_grad_x, out_sum, out_sum_x = order.done(
        project_back(place, order(attn_grad), after(attn_grad_near, out_other), mixture, mixture_x, out_weight, out_weight_x)
    )
    down_kept, down_sent = order.done(halves(place, order(down_sum), 1))
    down_got = swap(down_sent, "dp", 1)
    up_kept, up_sent = order.done(halves(place, order(up_sum), 2))
    up_got = swap(up_sent, "dp", 2)

    sides = ((query, key, value, mixture, mixture_grad), (query_x, key_x, value_x, mixture_x, mixture_grad_x))

    def backward(head, extras):
        return order.done(
            attend_backward(place, doc_lengths, head, 1, sides, order(entry_one_all), extras)
        )

    def on(value, step=0):
        return swap(value, "dp", bits[2 + step])

    def doubled(value, got):
        for step in range(len(bits) - 2):
            value = order.done(total_of(order(value), got))
            if step + 3 < len(bits):
                got = on(value, step + 1)
        return value

    back_0, first_sum, back_x_0, first_sum_x = backward(0, (out_sum, out_sum_x))
    down_part_x = order.done(total_of(order(down_kept_x), down_got_x))
    down_got_x = across(down_part_x)
    back_1, head_sum, back_x_1, head_sum_x = backward(1, ())
    up_part_x = order.done(total_of(order(up_kept_x), up_got_x))
    up_got_x = across(up_part_x)
    up_part, down_part = order.done(two_totals(order(up_kept), up_got, down_kept, down_got))
    back_2, rest_sum, back_x_2, rest_sum_x = backward(2, (head_sum, head_sum_x))
    rest_kept, rest_kept_x, rest_sent = order.done(pair_halves(place, order(rest_sum), rest_sum_x, 1))
    rest_got = swap(rest_sent, "dp", 1)
    down_kept, down_sent = order.done(summed(place, order(down_part), down_got_x, 2))
    down_got = swap(down_sent, "dp", 2)
    first_own, first_other = order.done(
        entry_back(
            place, (order(back_0), back_1, back_2), (back_x_0, back_x_1, back_x_2), qkv_turned, (qkv_a, qkv_b)
        )
    )
    first_other = near(first_other)
    output, sums_out = order.done(
        row_wise(leave, "leave", (order(middle), cotangent, out_own, out_other), (table,), ((shape, BF16),), 2, 3)
    )
    input_gradient, sums_one = order.done(
        row_wise(
            back_first, "back_first", (order(tokens), first_own, first_other, middle_grad), (table,), ((shape, F32),), 3, 3
        )
    )
    sums = order.done(tabulate(order(sums_one), sums_two, sums_out, table, bias_sum, bias_sum_x))
    sums_near = near(sums)
    up_kept, up_sent = order.done(summed(place, order(up_part), up_got_x, 1))
    up_got = swap(up_sent, "dp", 1)
    down_value = order.done(total_of(order(down_kept), down_got))
    down_got = on(down_value)
    rows_x, rows_z = rest_kept.shape[0], rest_kept.shape[0] // 2
    rest_part, slots, sent = order.done(
        ride(
            ride_first_kernel,
            "ride_first",
            ((rows_x, width), (TABLE, width), (rows_x + TABLE, width)),
            order(rest_kept),
            rest_kept_x,
            rest_got,
            sums,
            sums_near,
        )
    )
    rest_got = across(sent)
    first_kept, first_kept_x, first_sent = order.done(pair_halves(place, order(first_sum), first_sum_x, 1))
    first_got = swap(first_sent, "dp", 1)
    up_value = order.done(total_of(order(up_kept), up_got))
    up_got = on(up_value)
    rest_value, slots, sent = order.done(
        ride(
            ride_half_kernel,
            "ride_half",
            ((rows_z, width), (2 * TABLE, width), (rows_z + 2 * TABLE, width)),
            place,
            order(rest_part),
            rest_got,
            slots,
        )
    )
    rest_got = swap(sent, "dp", 2)
    slots = order.done(hold(order(slots)))
    for step in range(len(bits) - 1):
        last = step == len(bits) - 2
        held = (2 * slots.shape[0], width)
        outs = ((rows_z, width), held) if last else ((rows_z, width), held, (rows_z + held[0], width))
        results = order.done(
            ride(
                partial(ride_add_kernel, bit=2 if step == 0 else 3 + step),
                "ride_add",
                outs,
                place,
                order(rest_value),
                rest_got,
                slots,
            )
        )
        rest_value, slots = results[:2]
        rest_got = swap(rest_value, "dp", 2) if last else on(results[2], step)
        if step == 0:
            down_value = doubled(down_value, down_got)
            down_got = swap(down_value, "dp", 2)
            down_side = swap(down_value, "dp", 1)
            first_part_x, first_part = order.done(pair_total(order(first_kept), first_kept_x, first_got)[::-1])
            first_got = across(first_part_x)
            up_value = doubled(up_value, up_got)
            up_got = swap(up_value, "dp", 1)
            first_kept, first_sent = order.done(summed(place, order(first_part), first_got, 2))
            first_got = swap(first_sent, "dp", 2)
            down_got = order.done(hold(order(down_got), down_side))
            down_far = swap(down_got, "dp", 1)
    first_value = order.done(total_of(order(first_kept), first_got))
    first_got = on(first_value)
    (rest_all,) = order.done(
        ride(
            ride_lay_kernel,
            "ride_lay",
            ((rows_x + slots.shape[0], width),),
            place,
            order(rest_value),
            rest_got,
            slots,
        )
    )
    rest_got = swap(rest_all, "dp", 1)
    first_value = doubled(first_value, first_got)
    first_got = swap(first_value, "dp", 2)
    up_value = order.done(lay(place, order(up_value), up_got, 1))
    up_got = swap(up_value, "dp", 2)
    down_grad = order.done(lay_four(place, order(down_value), down_got, down_side, down_far))
    first_value = order.done(lay(place, order(first_value), first_got, 2))
    first_got = swap(first_value, "dp", 1)
    rest_total, ada_grad, *totals = order.done(finish(place, order(rest_all), rest_got, rows_x))
    up_grad = order.done(lay_out(place, order(up_value), up_got, 2))
    out_rows = out_weight.shape[0]
    out_grad, qkv_grad = order.done(lay_and_cut(place, order(first_value), first_got, 1, rest_total, out_rows))
    ada_bias_grad, gain_one_grad, gain_two_grad, down_bias_grad, up_bias_grad = [total.reshape(-1) for total in totals]
    return (
        output,
        input_gradient,
        gain_one_grad,
        qkv_grad.T,
        out_grad,
        gain_two_grad,
        up_grad,
        up_bias_grad,
        down_grad,
        down_bias_grad,
        ada_grad,
        ada_bias_grad,
    )


def solution(mesh):
    in_specs = (
        P(("dp", "mp"), None),
        P(("dp", "mp"), None),
        P("dp", None),
        P("dp"),
        P(),
        P(None, "mp"),
        P("mp", None),
        P(),
        P(None, "mp"),
        P("mp"),
        P("mp", None),
        P(),
        P(),
        P(),
    )
    out_specs = (
        P(("dp", "mp"), None),
        P(("dp", "mp"), None),
        P(),
        P(None, "mp"),
        P("mp", None),
        P(),
        P(None, "mp"),
        P("mp"),
        P("mp", None),
        P(),
        P(),
        P(),
    )
    return jax.shard_map(
        per_device, mesh=mesh, in_specs=in_specs, out_specs=out_specs, check_vma=False
    )
```

```python
from functools import partial
import math

import jax
import jax.numpy as jnp
from jax import lax
from jax.experimental import pallas as pl
from jax.experimental.pallas import tpu as pltpu
from jax.sharding import PartitionSpec as P

HEAD_DIM = 64
COND = 128
BLOCK = 256
STEP = 128
LANES = 128
BF16 = jnp.bfloat16
F32 = jnp.float32
TANH_SCALE = math.sqrt(2 / math.pi)
TANH_CUBE = 0.044715


def swap(value, axis, bit):
    size = lax.axis_size(axis)
    return lax.ppermute(value, axis, [(i, i ^ bit) for i in range(size)])


def time_features(time, axis, cond_width):
    half_width = cond_width // 2
    dims = (cond_width, 1) if axis == 0 else (1, cond_width)
    place = lax.broadcasted_iota(jnp.int32, dims, axis)
    second = place >= half_width
    ladder = jnp.where(second, place - half_width, place).astype(F32)
    angles = time.astype(F32) * jnp.exp(ladder * (-math.log(10000.0) / half_width))
    waves = jnp.where(second, jnp.sin(angles), jnp.cos(angles))
    return waves / (1.0 + jnp.exp(-waves))


def standard_score_rows(values):
    center = values - jnp.mean(values, axis=-1, keepdims=True)
    inverse_deviation = lax.rsqrt(jnp.mean(center * center, axis=-1, keepdims=True) + 1e-05)
    return (center * inverse_deviation, inverse_deviation)


def norm_reverse_pass(incoming_gradient, centered_scaled, inverse_deviation):
    return inverse_deviation * (
        incoming_gradient
        - jnp.mean(incoming_gradient, axis=-1, keepdims=True)
        - centered_scaled * jnp.mean(incoming_gradient * centered_scaled, axis=-1, keepdims=True)
    )


def dot(a, b):
    return jnp.dot(a, b, preferred_element_type=F32)


def contract_rows(a, b):
    return lax.dot_general(a, b, (((0,), (0,)), ((), ())), preferred_element_type=F32)


def times_transposed(a, b):
    return lax.dot_general(a, b, (((1,), (1,)), ((), ())), preferred_element_type=F32)


def one_line(lines_ref, first, width):
    return jnp.concatenate([lines_ref[first + k : first + k + 1, :] for k in range(width // LANES)], axis=1)


def in_vmem():
    return pl.BlockSpec(memory_space=pltpu.VMEM)


def in_smem():
    return pl.BlockSpec(memory_space=pltpu.SMEM)


def in_hbm(value):
    return pltpu.with_memory_space_constraint(value, pltpu.HBM)


def kept(dims, kind):
    return pltpu.VMEM(dims, kind)


def shape(dims, kind):
    return jax.ShapeDtypeStruct(dims, kind)


def cost(micros, size):
    return pl.CostEstimate(flops=int((micros + 12) * 1.1e9), bytes_accessed=size, transcendentals=0)


def small_cost(micros=0.001):
    return pl.CostEstimate(flops=int(micros * 1.1e9), bytes_accessed=10**4, transcendentals=0)


def parameters(mebibytes):
    return pltpu.CompilerParams(vmem_limit_bytes=mebibytes * 2**20)


def anywhere():
    return pl.BlockSpec(memory_space=pl.ANY)


def after(value, *tokens):
    return lax.optimization_barrier((value, *tokens))[0]


def rows_at(index, count):
    return pl.ds(pl.multiple_of(index * count, count), count)


def joined(target, pieces, mine, direct=0):
    rows = (target.shape[0] - direct) // 2
    for piece, index in zip(pieces, (mine, 1 - mine)):
        target[rows_at(index, rows), :] = piece[:rows, :]
    if direct:
        target[2 * rows :, :] = pieces[2][...]


def window_sizes(slot_length):
    return tuple(range(2 * STEP, slot_length + 1, STEP))


def block_window(lengths_ref, slot, block, slot_length):
    first = block * BLOCK
    last = first + BLOCK - 1
    end = jnp.int32(0)
    low = jnp.int32(0)
    high = jnp.int32(slot_length)
    for document in range(lengths_ref.shape[1]):
        end = end + lengths_ref[slot, document]
        low = jnp.where(end <= first, jnp.maximum(low, end), low)
        high = jnp.where(end > last, jnp.minimum(high, end), high)
    low = lax.div(low, jnp.int32(STEP)) * STEP
    size = jnp.maximum(lax.div(high - low + (STEP - 1), jnp.int32(STEP)) * STEP, 2 * STEP)
    return pl.multiple_of(jnp.minimum(low, slot_length - size), STEP), size


def mask_features(lengths_ref, slot, first, rows):
    documents = lengths_ref.shape[1]
    place = first + lax.broadcasted_iota(jnp.int32, (rows, HEAD_DIM), 0)
    lanes = lax.broadcasted_iota(jnp.int32, (rows, HEAD_DIM), 1)
    segment = jnp.zeros((rows, HEAD_DIM), jnp.int32)
    end = jnp.int32(0)
    for document in range(documents):
        end = end + lengths_ref[slot, document]
        segment = segment + jnp.where(place >= end, 1, 0)
    same = lanes == segment
    one = (lanes >= documents) & (lanes < documents + 3)
    key = jnp.where((lanes < documents) & jnp.logical_not(same), -1e30, jnp.where(one, 1.0, 0.0))
    return key.astype(BF16), jnp.where(same, 1.0, 0.0).astype(BF16)


def three_parts(value, lanes, at):
    first = value.astype(BF16).astype(F32)
    rest = value - first
    second = rest.astype(BF16).astype(F32)
    third = rest - second
    return jnp.where(lanes == at, first, jnp.where(lanes == at + 1, second, jnp.where(lanes == at + 2, third, 0.0)))


def attend_forward_kernel(place_ref, lengths_ref, own_ref, other_ref, *refs, fetched, keep):
    refs = list(refs)
    weight_refs = [refs.pop(0) for _ in range(2 if fetched else 1)]
    weight_ref = weight_refs[0]
    query_ref, key_ref, value_ref, out_ref = refs[:4]
    refs = refs[4:]
    slot = place_ref[3]
    documents = lengths_ref.shape[1]
    if keep:
        kept_ref = refs.pop(0)
    if fetched:
        joined_ref = refs.pop(0)
        joined(joined_ref, weight_refs, place_ref[1])
        weight_ref = joined_ref
    rows = own_ref.shape[0] // 2
    length = 2 * rows
    heads = weight_ref.shape[0] // (3 * HEAD_DIM)
    core = place_ref[0]
    lanes = lax.broadcasted_iota(jnp.int32, (rows, HEAD_DIM), 1)
    ones = jnp.where(lanes < 3, 1.0, 0.0).astype(BF16)
    for source, at in ((own_ref, core), (other_ref, 1 - core)):
        here = rows_at(at, rows)
        key_extra, query_extra = mask_features(lengths_ref, slot, at * rows, rows)
        if keep:
            kept_ref[here, :] = source[:rows, :]
        qkv = times_transposed(source[:rows, :], weight_ref[...]).astype(BF16)
        for head in range(heads):
            at = 3 * HEAD_DIM * head
            query = qkv[:, at : at + HEAD_DIM] * 0.125
            key = qkv[:, at + HEAD_DIM : at + 2 * HEAD_DIM]
            value = qkv[:, at + 2 * HEAD_DIM : at + 3 * HEAD_DIM]
            query_ref[head, here, :] = jnp.concatenate([query, query_extra], axis=1)
            key_ref[head, here, :] = jnp.concatenate([key, key_extra], axis=1)
            value_ref[head, here, :] = jnp.concatenate([value, ones], axis=1)

    def one_block(block, carry):
        here = rows_at(block, BLOCK)
        start, window = block_window(lengths_ref, slot, block, length)
        for size in window_sizes(length):

            @pl.when(window == size)
            def _():
                every = range(heads)
                span = pl.ds(start, size)
                queries = [query_ref[head, here, :] for head in every]
                scores = [times_transposed(queries[head], key_ref[head, span, :]) for head in every]
                wide = lax.broadcasted_iota(jnp.int32, (BLOCK, LANES), 1)
                mixed = []
                for head in every:
                    highest = jnp.max(scores[head], axis=1, keepdims=True)
                    raised = jnp.exp(scores[head] - highest).astype(BF16)
                    product = dot(raised, value_ref[head, span, :])
                    total = product[:, HEAD_DIM : HEAD_DIM + 1]
                    mixed.append(product[:, :HEAD_DIM] / total)
                    extra = three_parts(highest + jnp.log(total), wide, HEAD_DIM + documents)
                    query_ref[head, here, :] = (queries[head].astype(F32) - extra).astype(BF16)
                out_ref[here, :] = jnp.concatenate(mixed, axis=1).astype(BF16)

        return carry

    lax.fori_loop(0, length // BLOCK, one_block, 0)


def attend_forward(place, lengths, own, other, weights, keep):
    length, width = own.shape
    fetched = len(weights) == 2
    columns = weights[0].shape[0] * len(weights)
    heads = columns // (3 * HEAD_DIM)
    head_wise = kept((heads, length, LANES), BF16)
    outs = [head_wise] * 3 + [kept((length, heads * HEAD_DIM), BF16)]
    if keep:
        outs.append(kept((length, width), BF16))
    return pl.pallas_call(
        partial(attend_forward_kernel, fetched=fetched, keep=keep),
        out_shape=tuple(outs),
        in_specs=[in_smem()] * 2 + [in_vmem()] * (2 + len(weights)),
        out_specs=(in_vmem(),) * len(outs),
        scratch_shapes=[pltpu.VMEM((columns, width), BF16)] if fetched else [],
        compiler_params=parameters(24),
        cost_estimate=cost(9, 2**22),
        name="attend_forward",
    )(place, lengths, own, other, *weights)


def attend_backward_kernel(place_ref, lengths_ref, *refs, first, heads, extra):
    slot = place_ref[3]
    every = range(2 * heads)
    inputs = []
    for side in range(2):
        for head in range(heads):
            arrays = [refs[5 * side + k].at[first + head] for k in range(3)]
            inputs.append((*arrays, refs[5 * side + 3], refs[5 * side + 4], first + head))
    entry_ref = refs[10]
    refs = refs[11:]
    if extra:
        extras = refs[:2]
        refs = refs[2:]
        for side in range(2):
            refs[2 * side + 1][:extra, :] = extras[side][...]
    outs = refs[:4]
    key_turned_ref, upstream_ref, sum_ref, query_grad_ref, right_ref = refs[4:]
    length = entry_ref.shape[0]
    lanes = lax.broadcasted_iota(jnp.int32, (length, HEAD_DIM), 1)
    zero = jnp.zeros((length, HEAD_DIM), BF16)
    for item in every:
        query_ref, key_ref, value_ref, mixed_ref, grad_ref, head = inputs[item]
        columns = slice(head * HEAD_DIM, (head + 1) * HEAD_DIM)
        upstream = grad_ref[:, columns]
        inner = jnp.sum(mixed_ref[:, columns].astype(F32) * upstream.astype(F32), axis=1, keepdims=True)
        upstream_ref[item] = jnp.concatenate([upstream, -three_parts(inner, lanes, 0).astype(BF16)], axis=1)
        key_turned_ref[item] = key_ref[:, :HEAD_DIM].T
        right_ref[item, 0] = jnp.concatenate([upstream, zero], axis=1)
        right_ref[item, 1] = jnp.concatenate([zero, query_ref[:, :HEAD_DIM]], axis=1)
    sum_ref[...] = jnp.zeros_like(sum_ref)

    def one_block(block, carry):
        here = rows_at(block, BLOCK)
        start, window = block_window(lengths_ref, slot, block, length)
        for size in window_sizes(length):

            @pl.when(window == size)
            def _():
                span = pl.ds(start, size)
                queries = [inputs[s][0][here, :] for s in every]
                upstreams = [upstream_ref[s, here, :] for s in every]
                rights = [
                    jnp.concatenate([right_ref[s, 0, here, :], right_ref[s, 1, here, :]], axis=0) for s in every
                ]
                weights = [jnp.exp(times_transposed(inputs[s][1][span, :], queries[s])) for s in every]
                raised = [times_transposed(inputs[s][2][span, :], upstreams[s]) for s in every]
                score_grads = [(a * b).astype(BF16) for a, b in zip(weights, raised)]
                turned = []
                for s in every:
                    left = jnp.concatenate([weights[s].astype(BF16), score_grads[s]], axis=1)
                    sum_ref[s, span, :] += dot(left, rights[s])
                    turned.append(dot(key_turned_ref[s, :, span], score_grads[s]))
                turned = (jnp.concatenate(turned, axis=0) * 0.125).T
                for s in every:
                    query_grad_ref[s, here, :] = turned[:, s * HEAD_DIM : (s + 1) * HEAD_DIM].astype(BF16)

        return carry

    lax.fori_loop(0, length // BLOCK, one_block, 0)
    for side in (1, 0):
        for head in range(heads):
            item = side * heads + head
            sums = sum_ref[item]
            grads = jnp.concatenate(
                [query_grad_ref[item], sums[:, HEAD_DIM:].astype(BF16), sums[:, :HEAD_DIM].astype(BF16)], axis=1
            )
            outs[2 * side][head] = grads
            part = 3 * HEAD_DIM
            outs[2 * side + 1][extra + head * part : extra + (head + 1) * part, :] = contract_rows(grads, entry_ref[...]).astype(BF16)


def attend_backward(place, lengths, first, heads, sides, entry, extras):
    extra = extras[0].shape[0] if extras else 0
    length, width = entry.shape
    flat = [array for side in sides for array in side]
    outs = [kept((heads, length, 3 * HEAD_DIM), BF16), kept((extra + heads * 3 * HEAD_DIM, width), BF16)] * 2
    count = 2 * heads
    return pl.pallas_call(
        partial(attend_backward_kernel, first=first, heads=heads, extra=extra),
        out_shape=tuple(outs),
        in_specs=[in_smem()] * 2 + [in_vmem()] * (11 + len(extras)),
        out_specs=(in_vmem(),) * len(outs),
        scratch_shapes=[
            pltpu.VMEM((count, HEAD_DIM, length), BF16),
            pltpu.VMEM((count, length, LANES), BF16),
            pltpu.VMEM((count, length, LANES), F32),
            pltpu.VMEM((count, length, HEAD_DIM), BF16),
            pltpu.VMEM((count, 2, length, LANES), BF16),
        ],
        compiler_params=parameters(24),
        cost_estimate=cost(9 * heads, 2**22),
        name="attend_backward",
    )(place, lengths, *flat, entry, *extras)


def project_out_kernel(place_ref, mixed_ref, mixed_x_ref, weight_ref, weight_x_ref, own_ref, other_ref):
    rows = own_ref.shape[0]
    for target, at in ((other_ref, 1 - place_ref[0]), (own_ref, place_ref[0])):
        here = rows_at(at, rows)
        total = dot(mixed_ref[here, :], weight_ref[...]) + dot(mixed_x_ref[here, :], weight_x_ref[...])
        target[...] = total.astype(target.dtype)


def project_out(place, mixed, mixed_x, weight, weight_x):
    rows = mixed.shape[0] // 2
    width = weight.shape[1]
    return pl.pallas_call(
        project_out_kernel,
        out_shape=(kept((rows, width), F32), shape((rows, width), BF16)),
        in_specs=[in_smem()] + [in_vmem()] * 4,
        out_specs=(in_vmem(),) * 2,
        compiler_params=parameters(12),
        cost_estimate=cost(2, 2**22),
        name="project_out",
    )(place, mixed, mixed_x, weight, weight_x)


def project_back_kernel(
    place_ref, own_ref, other_ref, mixed_ref, mixed_x_ref, weight_ref, weight_x_ref,
    grad_ref, grad_x_ref, out_ref, out_x_ref, rows_ref,
):
    rows = own_ref.shape[0]
    rows_ref[rows_at(place_ref[0], rows), :] = own_ref[...]
    rows_ref[rows_at(1 - place_ref[0], rows), :] = other_ref[...]
    out_x_ref[...] = contract_rows(mixed_x_ref[...], rows_ref[...]).astype(BF16)
    out_ref[...] = contract_rows(mixed_ref[...], rows_ref[...]).astype(BF16)
    grad_ref[...] = times_transposed(rows_ref[...], weight_ref[...]).astype(BF16)
    grad_x_ref[...] = times_transposed(rows_ref[...], weight_x_ref[...]).astype(BF16)


def project_back(place, own, other, mixed, mixed_x, weight, weight_x):
    rows, width = own.shape
    return pl.pallas_call(
        project_back_kernel,
        out_shape=(kept(mixed.shape, BF16),) * 2 + (kept(weight.shape, BF16),) * 2,
        in_specs=[in_smem()] + [in_vmem()] * 6,
        out_specs=(in_vmem(),) * 4,
        scratch_shapes=[pltpu.VMEM((2 * rows, width), BF16)],
        compiler_params=parameters(14),
        cost_estimate=cost(3, 2**22),
        name="project_back",
    )(place, own, other, mixed, mixed_x, weight, weight_x)


def entry_back_kernel(place_ref, *refs, groups):
    grads = [[ref.at[k] for ref in refs[side * groups : (side + 1) * groups] for k in range(ref.shape[0])] for side in (0, 1)]
    weight_ref, first_ref, second_ref, own_ref, other_ref, joined_ref = refs[2 * groups :]
    rows = own_ref.shape[0]
    joined(joined_ref, (first_ref, second_ref), place_ref[1])
    for target, at in ((other_ref, 1 - place_ref[0]), (own_ref, place_ref[0])):
        here = rows_at(at, rows)
        left = jnp.concatenate([grad[here, :] for grad in grads[0]], axis=1)
        left_x = jnp.concatenate([grad[here, :] for grad in grads[1]], axis=1)
        total = dot(left, weight_ref[...]) + dot(left_x, joined_ref[...])
        target[...] = total.astype(target.dtype)


def entry_back(place, grads, grads_x, weight, weights_x):
    rows = grads[0].shape[1] // 2
    width = weight.shape[1]
    groups = len(grads)
    return pl.pallas_call(
        partial(entry_back_kernel, groups=groups),
        out_shape=(kept((rows, width), F32), shape((rows, width), BF16)),
        in_specs=[in_smem()] + [in_vmem()] * (2 * groups + 3),
        out_specs=(in_vmem(),) * 2,
        scratch_shapes=[pltpu.VMEM(weight.shape, BF16)],
        compiler_params=parameters(16),
        cost_estimate=cost(4, 2**22),
        name="entry_back",
    )(place, *grads, *grads_x, weight, *weights_x)


def hidden_grad(both, down):
    rows = both.shape[0] // 2
    units = down.shape[0]

    def kernel(both_ref, down_ref, out_ref):
        out_ref[...] = times_transposed(both_ref[rows:, :], down_ref[...])

    return pl.pallas_call(
        kernel,
        out_shape=kept((rows, units), F32),
        in_specs=[in_vmem()] * 2,
        out_specs=in_vmem(),
        compiler_params=parameters(8),
        cost_estimate=cost(1, 2**21),
        name="hidden_grad",
    )(both, down)


def hidden_kernel(place_ref, *refs, fetched):
    refs = list(refs)
    entries = refs[:2]
    upstreams = refs[2:4]
    if fetched:
        up_refs, down_refs = refs[4:6], refs[6:9]
        base = refs[9:11]
        refs = refs[11:]
    else:
        up_ref, bias_ref = refs[4:6]
        hidden_grads = refs[6:8]
        refs = refs[8:]
    grads = refs[:2]
    hidden_ref, bias_sum_ref = refs[2:4]
    if fetched:
        up_kept_ref, up_sent_ref, down_kept_ref, down_sent_ref = refs[4:8]
        up_all_ref, down_all_ref = refs[8:10]
        pre_grad_ref, sum_ref = refs[10:12]
        up_sum_ref = down_sum_ref = sum_ref
        direct = down_refs[2].shape[0]
        joined(up_all_ref, up_refs, place_ref[1])
        joined(down_all_ref, down_refs, place_ref[2], direct)
        up_ref, down_ref = up_all_ref, down_all_ref
    else:
        up_sum_ref, down_sum_ref, pre_grad_ref = refs[4:7]
    rows, width = entries[0].shape
    units = up_ref.shape[1]
    bias_sum = [jnp.zeros((1, BLOCK), F32) for _ in range(units // BLOCK)]
    if fetched:
        at = (units - direct) // 2
        bias = down_refs[0][at : at + 16, :].astype(F32)[:1]
    else:
        bias = one_line(bias_ref, 0, units).astype(F32)
    for part in range(2):
        there = slice(part * rows, (part + 1) * rows)
        entry = entries[part][...]
        upstream = upstreams[part][rows:, :]
        for block in range(units // BLOCK):
            cut = slice(block * BLOCK, (block + 1) * BLOCK)
            pre = dot(entry, up_ref[:, cut]) + bias[:, cut]
            given = times_transposed(upstream, down_ref[cut, :]) if fetched else hidden_grads[part][:, cut]
            square = pre * pre
            half = 0.5 + 0.5 * jnp.tanh(pre * (TANH_SCALE + (TANH_SCALE * TANH_CUBE) * square))
            hidden = pre * half
            slope = half + (hidden - hidden * half) * (2 * TANH_SCALE + (6 * TANH_SCALE * TANH_CUBE) * square)
            pre_grad = (given * slope).astype(BF16)
            hidden_ref[there, cut] = hidden.astype(BF16)
            pre_grad_ref[there, cut] = pre_grad
            bias_sum[block] = bias_sum[block] + jnp.sum(pre_grad.astype(F32), axis=0, keepdims=True)
    bias_sum_ref[...] = jnp.zeros_like(bias_sum_ref)
    bias_sum_ref[0:1, :] = jnp.concatenate(bias_sum, axis=1)
    for part in (1, 0):
        grad = times_transposed(pre_grad_ref[part * rows : (part + 1) * rows, :], up_ref[...])
        if fetched:
            grad = grad + base[part][...]
        grads[part][...] = grad.astype(grads[part].dtype)
    half = units // 2
    for block in range(units // BLOCK):
        cut = slice(block * BLOCK, (block + 1) * BLOCK)
        total = contract_rows(entries[0][...], pre_grad_ref[:rows, cut]) + contract_rows(entries[1][...], pre_grad_ref[rows:, cut])
        up_sum_ref[:, cut] = total.astype(BF16)
    if fetched:
        up_sent_ref[...] = sum_ref[rows_at(1 - place_ref[2], width // 2), :]
        up_kept_ref[...] = sum_ref[rows_at(place_ref[2], width // 2), :]
    for block in range(units // BLOCK):
        cut = slice(block * BLOCK, (block + 1) * BLOCK)
        total = contract_rows(hidden_ref[:rows, cut], upstreams[0][rows:, :]) + contract_rows(hidden_ref[rows:, cut], upstreams[1][rows:, :])
        down_sum_ref[cut, :] = total.astype(BF16)
    if fetched:
        down_sent_ref[...] = sum_ref[rows_at(1 - place_ref[1], half), :]
        down_kept_ref[...] = sum_ref[rows_at(place_ref[1], half), :]


def hidden_part(place, entries, upstreams, weights, others, fetched):
    rows, width = entries[0].shape
    units = weights[0].shape[1]
    inputs = [*entries, *upstreams, *weights, *others]
    outs = [kept((rows, width), F32), shape((rows, width), BF16) if fetched else kept((rows, width), F32)]
    outs += [kept((2 * rows, units), BF16), shape((8, units), F32)]
    if fetched:
        outs += [kept((width // 2, units), BF16), shape((width // 2, units), BF16)]
        outs += [kept((units // 2, width), BF16), shape((units // 2, width), BF16)]
        outs += [kept((width, units), BF16), kept((units, width), BF16)]
    else:
        outs += [kept((width, units), BF16), kept((units, width), BF16)]
    return pl.pallas_call(
        partial(hidden_kernel, fetched=fetched),
        out_shape=tuple(outs),
        in_specs=[in_smem()] + [in_vmem()] * len(inputs),
        out_specs=(in_vmem(),) * len(outs),
        scratch_shapes=[pltpu.VMEM((2 * rows, units), BF16)] + [pltpu.VMEM((width, units), BF16)] * fetched,
        compiler_params=parameters(24),
        cost_estimate=cost(10, 2**23),
        name="hidden_part",
    )(place, *inputs)


def hidden_out_kernel(hidden_ref, hidden_x_ref, down_ref, down_x_ref, out_ref, *, part):
    rows = out_ref.shape[0]
    there = slice(part * rows, (part + 1) * rows)
    out = dot(hidden_ref[there, :], down_ref[...]) + dot(hidden_x_ref[there, :], down_x_ref[...])
    out_ref[...] = out.astype(out_ref.dtype)


def hidden_out(hidden, hidden_x, down, down_x, part, kind):
    rows, width = hidden.shape[0] // 2, down.shape[1]
    return pl.pallas_call(
        partial(hidden_out_kernel, part=part),
        out_shape=(kept if kind == F32 else shape)((rows, width), kind),
        in_specs=[in_vmem()] * 4,
        out_specs=in_vmem(),
        compiler_params=parameters(12),
        cost_estimate=cost(2, 2**22),
        name="hidden_out",
    )(hidden, hidden_x, down, down_x)


ROWS = 256


def row_wise(body, name, row_inputs, whole_inputs, row_outs, sums, micros):
    rows, width = row_inputs[0].shape
    outs = [make((rows, width), kind) for make, kind in row_outs]
    if sums:
        outs.append(kept((8, width), F32))

    def kernel(*refs):
        refs = list(refs)
        row_refs = [refs.pop(0) for _ in row_inputs]
        whole_refs = [refs.pop(0) for _ in whole_inputs]

        def tile(step, total):
            here = rows_at(step, ROWS)
            results, terms = body(*[ref[here, :] for ref in row_refs], *whole_refs)
            for ref, result in zip(refs, results):
                ref[here, :] = result.astype(ref.dtype)
            return tuple(
                old + jnp.sum(term.reshape(ROWS // 8, 8, width), axis=0) for old, term in zip(total, terms)
            )

        total = lax.fori_loop(0, rows // ROWS, tile, (jnp.zeros((8, width), F32),) * sums)
        if sums:
            lines = [jnp.sum(term, axis=0, keepdims=True) for term in total]
            refs[-1][...] = jnp.concatenate(lines + [jnp.zeros((8 - sums, width), F32)], axis=0)

    return pl.pallas_call(
        kernel,
        out_shape=tuple(outs),
        in_specs=[in_vmem()] * (len(row_inputs) + len(whole_inputs)),
        out_specs=(in_vmem(),) * len(outs),
        compiler_params=parameters(18),
        cost_estimate=cost(micros, 2**20),
        name=name,
    )(*row_inputs, *whole_inputs)


def enter_kernel(place_ref, time_ref, tokens_ref, cotangent_ref, weight_ref, *refs):
    vectors, (table_ref, both_ref) = refs[:-2], refs[-2:]
    rows, width = tokens_ref.shape
    table_ref[...] = jnp.zeros_like(table_ref)
    row = 0
    for vector in vectors:
        for at in range(0, vector.shape[0], width // LANES):
            table_ref[row : row + 1, :] = one_line(vector, at, width)
            row += 1
    features = time_features(time_ref[place_ref[3]], 0, COND)
    for piece in range(6):
        cut = slice(piece * width, (piece + 1) * width)
        table_ref[piece : piece + 1, :] += jnp.sum(features * weight_ref[:, cut], axis=0, keepdims=True)
    table_ref[row : row + 1, :COND] = time_features(time_ref[place_ref[3]], 1, COND)
    table = table_ref[...]

    def tile(step, carry):
        here = rows_at(step, ROWS)
        scored, _ = standard_score_rows(tokens_ref[here, :].astype(F32))
        entry = scored * table[6:7] * (1.0 + table[1:2]) + table[0:1]
        both_ref[here, :] = entry.astype(BF16)
        there = pl.ds(pl.multiple_of(rows + step * ROWS, ROWS), ROWS)
        both_ref[there, :] = (table[5:6] * cotangent_ref[here, :].astype(F32)).astype(BF16)
        return carry

    lax.fori_loop(0, rows // ROWS, tile, 0)


def enter(place, time_index, tokens, cotangent, weight, vectors):
    vectors = [vector.reshape(-1, LANES) for vector in vectors]
    rows, width = tokens.shape
    return pl.pallas_call(
        enter_kernel,
        out_shape=(shape((16, width), F32), shape((2 * rows, width), BF16)),
        in_specs=[in_smem()] * 2 + [in_vmem()] * (3 + len(vectors)),
        out_specs=(in_vmem(),) * 2,
        compiler_params=parameters(14),
        cost_estimate=cost(4, 2**22),
        name="enter",
    )(place, time_index, in_hbm(tokens), in_hbm(cotangent), in_hbm(weight), *[in_hbm(vector) for vector in vectors])


def enter_second(tokens, branch_own, branch_other, modulation):
    branch = branch_own + branch_other.astype(F32)
    middle = tokens.astype(F32) + modulation[2:3, :] * branch
    scored, _ = standard_score_rows(middle)
    entry = scored * modulation[7:8, :] * (1.0 + modulation[4:5, :]) + modulation[3:4, :]
    return (middle, entry), ()


def leave(middle, cotangent, out_own, out_other, modulation):
    branch = out_own + out_other.astype(F32) + modulation[8:9, :]
    incoming = cotangent.astype(F32)
    branch_grad = (modulation[5:6, :] * incoming).astype(BF16).astype(F32)
    return (middle + modulation[5:6, :] * branch,), (incoming * branch, branch_grad)


def back_second(middle, cotangent, grad_own, grad_other, branch_own, branch_other, modulation):
    gain = modulation[7:8, :]
    scored, inverse = standard_score_rows(middle)
    entry_grad = grad_own + grad_other.astype(F32)
    normed_grad = entry_grad * (1.0 + modulation[4:5, :])
    middle_grad = cotangent.astype(F32) + norm_reverse_pass(normed_grad * gain, scored, inverse)
    branch = branch_own + branch_other.astype(F32)
    terms = (middle_grad * branch, entry_grad, entry_grad * (scored * gain), normed_grad * scored)
    return (modulation[2:3, :] * middle_grad, middle_grad), terms


def back_first(tokens, grad_own, grad_other, middle_grad, modulation):
    gain = modulation[6:7, :]
    scored, inverse = standard_score_rows(tokens.astype(F32))
    entry_grad = grad_own + grad_other.astype(F32)
    normed_grad = entry_grad * (1.0 + modulation[1:2, :])
    grad = middle_grad + norm_reverse_pass(normed_grad * gain, scored, inverse)
    return (grad,), (entry_grad, entry_grad * (scored * gain), normed_grad * scored)


def piece_kernel(place_ref, source_ref, *refs, rows, bit):
    if len(refs) == 2:
        refs[1][rows:, :] = jnp.zeros_like(refs[1][rows:, :])
        refs[1][rows : rows + 1, :] = one_line(refs[0], 0, refs[1].shape[1])
    refs[-1][:rows, :] = source_ref[rows_at(place_ref[bit], rows), :]


def own_piece(place, source, rows, bit, line=None):
    extra = [] if line is None else [line.reshape(-1, LANES)]
    return pl.pallas_call(
        partial(piece_kernel, rows=rows, bit=bit),
        out_shape=shape((rows + 16 * len(extra), source.shape[1]), source.dtype),
        in_specs=[in_smem()] + [in_vmem()] * (1 + len(extra)),
        out_specs=in_vmem(),
        compiler_params=parameters(8),
        cost_estimate=small_cost(),
        name="own_piece",
    )(place, in_hbm(source), *extra)


def lower_half(source):
    rows, width = source.shape

    def kernel(source_ref, out_ref):
        out_ref[...] = source_ref[rows // 2 :, :]

    return pl.pallas_call(
        kernel,
        out_shape=shape((rows // 2, width), source.dtype),
        in_specs=[in_vmem()],
        out_specs=in_vmem(),
        compiler_params=parameters(8),
        cost_estimate=small_cost(),
        name="lower_half",
    )(in_hbm(source))


def sum_kernel(place_ref, a_ref, b_ref, kept_ref, sent_ref, *, bit):
    half = kept_ref.shape[0]
    for out, index in ((sent_ref, 1 - place_ref[bit]), (kept_ref, place_ref[bit])):
        here = rows_at(index, half)
        out[...] = (a_ref[here, :].astype(F32) + b_ref[here, :].astype(F32)).astype(BF16)


def summed(place, a, b, bit):
    rows, width = a.shape
    return pl.pallas_call(
        partial(sum_kernel, bit=bit),
        out_shape=(kept((rows // 2, width), BF16),) * 2,
        in_specs=[in_smem(), in_vmem(), in_vmem()],
        out_specs=(in_vmem(),) * 2,
        compiler_params=parameters(8),
        cost_estimate=small_cost(3),
        name="summed",
    )(place, a, b)


def total_kernel(a_ref, b_ref, out_ref):
    out_ref[...] = (a_ref[...].astype(F32) + b_ref[...].astype(F32)).astype(BF16)


def total_of(a, b):
    return pl.pallas_call(
        total_kernel,
        out_shape=kept(a.shape, BF16),
        in_specs=[in_vmem()] * 2,
        out_specs=in_vmem(),
        compiler_params=parameters(8),
        cost_estimate=small_cost(3),
        name="total_of",
    )(a, b)


def pair_kernel(place_ref, a_ref, b_ref, kept_a_ref, kept_b_ref, sent_ref, *, bit):
    half = kept_a_ref.shape[0]
    mine, other = rows_at(place_ref[bit], half), rows_at(1 - place_ref[bit], half)
    sent_ref[:half, :] = a_ref[other, :]
    sent_ref[half:, :] = b_ref[other, :]
    kept_a_ref[...] = a_ref[mine, :]
    kept_b_ref[...] = b_ref[mine, :]


def pair_halves(place, a, b, bit):
    rows, width = a.shape
    half = kept((rows // 2, width), BF16)
    return pl.pallas_call(
        partial(pair_kernel, bit=bit),
        out_shape=(half, half, kept((rows, width), BF16)),
        in_specs=[in_smem(), in_vmem(), in_vmem()],
        out_specs=(in_vmem(),) * 3,
        compiler_params=parameters(8),
        cost_estimate=small_cost(3),
        name="pair_halves",
    )(place, a, b)


def halves_kernel(place_ref, source_ref, kept_ref, sent_ref, *, bit):
    half = kept_ref.shape[0]
    sent_ref[...] = source_ref[rows_at(1 - place_ref[bit], half), :]
    kept_ref[...] = source_ref[rows_at(place_ref[bit], half), :]


def halves(place, source, bit):
    rows, width = source.shape
    return pl.pallas_call(
        partial(halves_kernel, bit=bit),
        out_shape=(kept((rows // 2, width), BF16),) * 2,
        in_specs=[in_smem(), in_vmem()],
        out_specs=(in_vmem(),) * 2,
        compiler_params=parameters(8),
        cost_estimate=small_cost(3),
        name="halves",
    )(place, source)


def pair_total_kernel(a_ref, b_ref, got_ref, out_a_ref, out_b_ref):
    half = a_ref.shape[0]
    out_b_ref[...] = (b_ref[...].astype(F32) + got_ref[half:, :].astype(F32)).astype(BF16)
    out_a_ref[...] = (a_ref[...].astype(F32) + got_ref[:half, :].astype(F32)).astype(BF16)


def pair_total(a, b, got):
    return pl.pallas_call(
        pair_total_kernel,
        out_shape=(kept(a.shape, BF16),) * 2,
        in_specs=[in_vmem()] * 3,
        out_specs=(in_vmem(),) * 2,
        compiler_params=parameters(8),
        cost_estimate=small_cost(3),
        name="pair_total",
    )(a, b, got)


def two_totals_kernel(a_ref, b_ref, c_ref, d_ref, first_ref, second_ref):
    first_ref[...] = (a_ref[...].astype(F32) + b_ref[...].astype(F32)).astype(BF16)
    second_ref[...] = (c_ref[...].astype(F32) + d_ref[...].astype(F32)).astype(BF16)


def two_totals(a, b, c, d):
    return pl.pallas_call(
        two_totals_kernel,
        out_shape=(kept(a.shape, BF16), kept(c.shape, BF16)),
        in_specs=[in_vmem()] * 4,
        out_specs=(in_vmem(),) * 2,
        compiler_params=parameters(8),
        cost_estimate=small_cost(3),
        name="two_totals",
    )(a, b, c, d)


def send_rows(whole_ref, at, out_ref, out_at, count, sem):
    copy = pltpu.make_async_copy(whole_ref.at[pl.ds(at, count), :], out_ref.at[pl.ds(out_at, count), :], sem)
    copy.start()
    return copy


def lay_and_cut_kernel(place_ref, own_ref, other_ref, behind_ref, first_ref, second_ref, whole_ref, sems, *, bit):
    rows, cut, rest = own_ref.shape[0], first_ref.shape[0], behind_ref.shape[0]
    copies = [send_rows(behind_ref, 0, second_ref, 2 * rows - cut, rest // 2, sems.at[0])]
    copies.append(send_rows(behind_ref, rest // 2, second_ref, 2 * rows - cut + rest // 2, rest - rest // 2, sems.at[1]))
    for ref, index in ((own_ref, place_ref[bit]), (other_ref, 1 - place_ref[bit])):
        whole_ref[rows_at(index, rows), :] = ref[...].astype(whole_ref.dtype)
    copies.append(send_rows(whole_ref, 0, first_ref, 0, cut, sems.at[2]))
    copies.append(send_rows(whole_ref, cut, second_ref, 0, 2 * rows - cut, sems.at[3]))
    for copy in copies:
        copy.wait()


def lay_and_cut(place, own, other, bit, behind, cut):
    rows, width = own.shape
    return pl.pallas_call(
        partial(lay_and_cut_kernel, bit=bit),
        out_shape=(shape((cut, width), F32), shape((2 * rows - cut + behind.shape[0], width), F32)),
        in_specs=[in_smem()] + [in_vmem()] * 3,
        out_specs=(anywhere(),) * 2,
        scratch_shapes=[pltpu.VMEM((2 * rows, width), F32), pltpu.SemaphoreType.DMA((4,))],
        compiler_params=parameters(14),
        cost_estimate=small_cost(3),
        name="lay_and_cut",
    )(place, own, other, behind)


def lay_straight_kernel(place_ref, own_ref, other_ref, out_ref, *, bit):
    rows = own_ref.shape[0]
    for ref, index in ((own_ref, place_ref[bit]), (other_ref, 1 - place_ref[bit])):
        out_ref[rows_at(index, rows), :] = ref[...].astype(out_ref.dtype)


def lay(place, own, other, bit):
    rows, width = own.shape
    return pl.pallas_call(
        partial(lay_straight_kernel, bit=bit),
        out_shape=kept((2 * rows, width), BF16),
        in_specs=[in_smem()] + [in_vmem()] * 2,
        out_specs=in_vmem(),
        compiler_params=parameters(8),
        cost_estimate=small_cost(3),
        name="lay",
    )(place, own, other)


def lay_out_kernel(place_ref, own_ref, other_ref, out_ref, whole_ref, sems, *, bit, parts):
    rows = own_ref.shape[0]
    count = rows // parts
    copies = []
    for which, (ref, index) in enumerate(((own_ref, place_ref[bit]), (other_ref, 1 - place_ref[bit]))):
        for part in range(parts):
            at = which * rows + part * count
            whole_ref[at : at + count, :] = ref[part * count : (part + 1) * count, :].astype(F32)
            target = pl.multiple_of(index * rows + part * count, count)
            copies.append(send_rows(whole_ref, at, out_ref, target, count, sems.at[which * parts + part]))
    for copy in copies:
        copy.wait()


def lay_out(place, own, other, bit):
    rows, width = own.shape
    parts = 3
    return pl.pallas_call(
        partial(lay_out_kernel, bit=bit, parts=parts),
        out_shape=shape((2 * rows, width), F32),
        in_specs=[in_smem()] + [in_vmem()] * 2,
        out_specs=anywhere(),
        scratch_shapes=[pltpu.VMEM((2 * rows, width), F32), pltpu.SemaphoreType.DMA((2 * parts,))],
        compiler_params=parameters(14),
        cost_estimate=small_cost(3),
        name="lay_out",
    )(place, own, other)


def lay_four_kernel(place_ref, *refs):
    parts, (out_ref, whole_ref, sems) = refs[:4], refs[4:]
    rows = parts[0].shape[0]
    copies = []
    for which, ref in enumerate(parts):
        side, turn = which // 2, which % 2
        first = place_ref[1] if side == 0 else 1 - place_ref[1]
        second = place_ref[2] if turn == 0 else 1 - place_ref[2]
        whole_ref[which * rows : (which + 1) * rows, :] = ref[...].astype(F32)
        target = pl.multiple_of((first * 2 + second) * rows, rows)
        copies.append(send_rows(whole_ref, which * rows, out_ref, target, rows, sems.at[which]))
    for copy in copies:
        copy.wait()


def lay_four(place, *parts):
    rows, width = parts[0].shape
    return pl.pallas_call(
        lay_four_kernel,
        out_shape=shape((4 * rows, width), F32),
        in_specs=[in_smem()] + [in_vmem()] * 4,
        out_specs=anywhere(),
        scratch_shapes=[pltpu.VMEM((4 * rows, width), F32), pltpu.SemaphoreType.DMA((4,))],
        compiler_params=parameters(14),
        cost_estimate=small_cost(3),
        name="lay_four",
    )(place, *parts)


TABLE = 16


def tabulate_kernel(first_ref, second_ref, last_ref, table_ref, bias_ref, bias_x_ref, out_ref):
    rows = [first_ref[0:2, :], second_ref[0:3, :], last_ref[0:1, :], first_ref[2:3, :], second_ref[3:4, :], last_ref[1:2, :]]
    rows += [table_ref[9:10, :], bias_ref[0:1, :], bias_x_ref[0:1, :], jnp.zeros((TABLE - 12, out_ref.shape[1]), F32)]
    out_ref[...] = jnp.concatenate(rows, axis=0)


def tabulate(*parts):
    return pl.pallas_call(
        tabulate_kernel,
        out_shape=shape((TABLE, parts[0].shape[1]), F32),
        in_specs=[in_vmem()] * 6,
        out_specs=in_vmem(),
        compiler_params=parameters(8),
        cost_estimate=cost(1, 2**18),
        name="tabulate",
    )(*parts)


def lay_table(out_ref, at, own, other, side):
    rows = own.shape[0]
    out_ref[pl.ds(pl.multiple_of(at + side * rows, TABLE), rows), :] = own
    out_ref[pl.ds(pl.multiple_of(at + (1 - side) * rows, TABLE), rows), :] = other


def ride_first_kernel(kept_ref, kept_x_ref, got_ref, own_ref, near_ref, part_ref, table_ref, out_ref):
    half = kept_ref.shape[0]
    own = own_ref[...]
    row = lax.broadcasted_iota(jnp.int32, own.shape, 0)
    table = jnp.where(row < 9, own + near_ref[...], own).astype(BF16)
    out_ref[:half, :] = (kept_x_ref[...].astype(F32) + got_ref[half:, :].astype(F32)).astype(BF16)
    out_ref[half:, :] = table
    table_ref[...] = table
    part_ref[...] = (kept_ref[...].astype(F32) + got_ref[:half, :].astype(F32)).astype(BF16)


def ride_half_kernel(place_ref, part_ref, got_ref, table_ref, kept_ref, next_ref, out_ref):
    half, rows = kept_ref.shape[0], table_ref.shape[0]
    mine, other = rows_at(place_ref[2], half), rows_at(1 - place_ref[2], half)
    out_ref[:half, :] = (part_ref[other, :].astype(F32) + got_ref[other, :].astype(F32)).astype(BF16)
    kept_ref[...] = (part_ref[mine, :].astype(F32) + got_ref[mine, :].astype(F32)).astype(BF16)
    lay_table(next_ref, 0, table_ref[...], got_ref[2 * half :, :], place_ref[3])
    out_ref[half:, :] = next_ref[...]


def ride_add_kernel(place_ref, value_ref, got_ref, table_ref, sum_ref, next_ref, *outs, bit):
    rows = value_ref.shape[0]
    total = (value_ref[...].astype(F32) + got_ref[:rows, :].astype(F32)).astype(BF16)
    sum_ref[...] = total
    lay_table(next_ref, 0, table_ref[...], got_ref[rows:, :], place_ref[bit])
    for out in outs:
        out[:rows, :] = total
        out[rows:, :] = next_ref[...]


def ride_lay_kernel(place_ref, own_ref, other_ref, table_ref, out_ref):
    rows = own_ref.shape[0]
    for ref, index in ((own_ref, place_ref[2]), (other_ref, 1 - place_ref[2])):
        out_ref[rows_at(index, rows), :] = ref[...]
    out_ref[2 * rows :, :] = table_ref[...]


def ride(kernel, name, outs, *inputs):
    scalars = [in_smem()] if inputs[0].ndim == 1 else []
    return pl.pallas_call(
        kernel,
        out_shape=tuple(kept(dims, BF16) for dims in outs),
        in_specs=scalars + [in_vmem()] * (len(inputs) - len(scalars)),
        out_specs=(in_vmem(),) * len(outs),
        compiler_params=parameters(8),
        cost_estimate=small_cost(3),
        name=name,
    )(*inputs)


def hold_kernel(source_ref, *refs):
    refs[-1][...] = source_ref[...]


def hold(value, *tokens):
    return pl.pallas_call(
        hold_kernel,
        out_shape=kept(value.shape, value.dtype),
        in_specs=[in_vmem()] + [anywhere()] * len(tokens),
        out_specs=in_vmem(),
        compiler_params=parameters(8),
        cost_estimate=small_cost(3) if tokens else cost(3, 2**18),
        name="hold",
    )(value, *tokens)


def put_lines(out_ref, first, row):
    for k in range(row.shape[1] // LANES):
        out_ref[first + k : first + k + 1, :] = row[:, k * LANES : (k + 1) * LANES]


def finish_kernel(place_ref, own_ref, got_ref, sum_ref, grad_ref, bias_ref, one_ref, two_ref, down_ref, up_ref, line_ref, grad_all_ref, sems, *, half):
    for ref, index in ((own_ref, place_ref[1]), (got_ref, 1 - place_ref[1])):
        sum_ref[pl.ds(pl.multiple_of(index * half, 16), half), :] = ref[:half, :].astype(F32)
    slots, width = (own_ref.shape[0] - half) // TABLE, own_ref.shape[1]
    for ref, index in ((own_ref, place_ref[1]), (got_ref, 1 - place_ref[1])):

        def one_slot(slot, carry, ref=ref, index=index):
            lines = ref[pl.ds(pl.multiple_of(half + slot * TABLE, TABLE), TABLE), :].astype(F32)
            for row in range(12):
                line_ref[row, pl.ds(index * slots + slot, 1), :] = lines[row : row + 1]
            return carry

        lax.fori_loop(0, slots, one_slot, 0)
    features = line_ref[9][:, :COND].astype(BF16)
    copies = []
    lines = width // LANES
    targets = [(bias_ref, piece * lines) for piece in range(6)] + [(one_ref, 0), (two_ref, 0), (down_ref, 0)]
    for piece, (target, first) in enumerate(targets):
        terms = line_ref[piece]
        put_lines(target, first, jnp.sum(terms, axis=0, keepdims=True))
        if piece < 6:
            grad_all_ref[piece] = contract_rows(features, terms.astype(BF16))
            copy = pltpu.make_async_copy(
                grad_all_ref.at[piece], grad_ref.at[:, pl.ds(piece * width, width)], sems.at[piece]
            )
            copy.start()
            copies.append(copy)
    slot = lax.broadcasted_iota(jnp.int32, (2 * slots, width), 0)
    mine = lax.rem(slot, 2) == place_ref[3]
    put_lines(up_ref, 0, jnp.sum(jnp.where(mine, line_ref[10], line_ref[11]), axis=0, keepdims=True))
    for copy in copies:
        copy.wait()


def finish(place, own, got, half):
    width = own.shape[1]
    slots = 2 * (own.shape[0] - half) // TABLE
    lines = width // LANES
    return pl.pallas_call(
        partial(finish_kernel, half=half),
        out_shape=(
            kept((2 * half, width), F32),
            shape((COND, 6 * width), F32),
            shape((6 * lines, LANES), F32),
        )
        + (shape((lines, LANES), F32),) * 4,
        in_specs=[in_smem()] + [in_vmem()] * 2,
        out_specs=(in_vmem(), anywhere()) + (in_vmem(),) * 5,
        scratch_shapes=[
            pltpu.VMEM((12, slots, width), F32),
            pltpu.VMEM((6, COND, width), F32),
            pltpu.SemaphoreType.DMA((6,)),
        ],
        compiler_params=parameters(20),
        cost_estimate=cost(3, 2**20),
        name="finish",
    )(place, own, got)


class Order:
    def __init__(self):
        self.token = ()

    def __call__(self, value):
        return after(value, *self.token) if self.token else value

    def done(self, result):
        self.token = (result[-1] if isinstance(result, (tuple, list)) else result,)
        return result


def dp_bits():
    bits = []
    bit = 1
    while bit < lax.axis_size("dp"):
        bits.append(bit)
        bit *= 2
    return bits


def per_device(
    tokens,
    cotangent,
    doc_lengths,
    time_index,
    attention_norm_gain,
    qkv_weight,
    out_weight,
    feedforward_norm_gain,
    up_weight,
    up_bias,
    down_weight,
    down_bias,
    ada_weight,
    ada_bias,
):
    rows, width = tokens.shape
    core = lax.axis_index("mp") % 2
    slot = lax.axis_index("mp") // 2
    index = lax.axis_index("dp")
    bits = dp_bits()
    place = [core, index % 2, index // 2 % 2, slot] + [index // bit % 2 for bit in bits[2:]]
    place = jnp.stack(place).astype(jnp.int32)
    order = Order()

    def near(value):
        return swap(value, "mp", 1)

    def across(value):
        return swap(value, "mp", 2)

    def relayed(value):
        return swap(value, "dp", 1)

    qkv_turned = qkv_weight.T
    qkv_half = order.done(own_piece(place, qkv_turned, qkv_turned.shape[0] // 2, 1))
    qkv_a = across(qkv_half)
    table, both = order.done(
        enter(
            place,
            time_index,
            order(tokens),
            cotangent,
            ada_weight,
            (ada_bias, attention_norm_gain, feedforward_norm_gain, down_bias),
        )
    )
    both_near = near(both)
    out_weight_x = across(order(out_weight))
    up_half = order.done(own_piece(place, order(up_weight), width // 2, 1))
    up_a = across(up_half)
    quarter = down_weight.shape[0] // 4
    down_part = order.done(own_piece(place, order(down_weight), quarter, 2, up_bias))
    down_a = across(down_part)
    down_lower = order.done(lower_half(order(down_weight)))
    table = order.done(hold(after(order(table), qkv_a)))
    qkv_b = swap(qkv_a, "dp", 1)

    query, key, value, mixture, entry_one_all = order.done(
        attend_forward(place, doc_lengths, order(both), both_near, (qkv_turned,), True)
    )
    down_straight = across(order(down_lower))
    query_x, key_x, value_x, mixture_x = order.done(
        attend_forward(place, doc_lengths, order(both), both_near, (qkv_a, qkv_b), False)
    )
    branch_own, branch_other = order.done(project_out(place, mixture, order(mixture_x), out_weight, out_weight_x))
    branch_other = near(branch_other)
    grad_one = order.done(hidden_grad(order(both), down_weight))
    up_b = swap(after(up_a, grad_one), "dp", 1)
    middle, entry_two = order.done(
        row_wise(
            enter_second, "enter_second", (order(tokens), branch_own, after(branch_other, up_a)), (table,), ((kept, F32), (shape, BF16)), 0, 3
        )
    )
    entry_two_near = near(entry_two)
    grad_two = order.done(hidden_grad(order(both_near), down_weight))
    down_b = swap(after(down_a, grad_two), "dp", 2)
    entries_two = (entry_two, after(entry_two_near, down_a))

    grad_base, grad_base_near, hidden, bias_sum, up_sum, down_sum = order.done(
        hidden_part(
            place,
            entries_two,
            (order(both), both_near),
            (up_weight, up_bias.reshape(-1, LANES)),
            (grad_one, grad_two),
            False,
        )
    )
    grad_own, grad_other, hidden_x, bias_sum_x, up_kept_x, up_sent_x, down_kept_x, down_sent_x, _, down_weight_x = order.done(
        hidden_part(
            place,
            (order(entries_two[0]), entries_two[1]),
            (both, both_near),
            (up_a, up_b, down_a, down_b, down_straight),
            (grad_base, grad_base_near),
            True,
        )
    )
    grad_other = near(grad_other)
    out_other = order.done(hidden_out(order(hidden), hidden_x, down_weight, down_weight_x, 1, BF16))
    out_other = near(out_other)
    down_got_x = swap(order(down_sent_x), "dp", 1)
    up_got_x = swap(order(up_sent_x), "dp", 2)
    attn_grad, middle_grad, sums_two = order.done(
        row_wise(
            back_second,
            "back_second",
            (order(middle), cotangent, grad_own, grad_other, branch_own, branch_other),
            (table,),
            ((shape, BF16), (kept, F32)),
            4,
            4,
        )
    )
    attn_grad_near = near(attn_grad)
    out_own = order.done(hidden_out(order(hidden), hidden_x, down_weight, down_weight_x, 0, F32))
    mixture_grad, mixture_grad_x, out_sum, out_sum_x = order.done(
        project_back(place, order(attn_grad), after(attn_grad_near, out_other), mixture, mixture_x, out_weight, out_weight_x)
    )
    down_kept, down_sent = order.done(halves(place, order(down_sum), 1))
    down_got = swap(down_sent, "dp", 1)
    up_kept, up_sent = order.done(halves(place, order(up_sum), 2))
    up_got = swap(up_sent, "dp", 2)

    sides = ((query, key, value, mixture, mixture_grad), (query_x, key_x, value_x, mixture_x, mixture_grad_x))

    def backward(head, extras):
        return order.done(
            attend_backward(place, doc_lengths, head, 1, sides, order(entry_one_all), extras)
        )

    def on(value, step=0):
        return swap(value, "dp", bits[2 + step])

    def doubled(value, got):
        for step in range(len(bits) - 2):
            value = order.done(total_of(order(value), got))
            if step + 3 < len(bits):
                got = on(value, step + 1)
        return value

    back_0, first_sum, back_x_0, first_sum_x = backward(0, (out_sum, out_sum_x))
    down_part_x = order.done(total_of(order(down_kept_x), down_got_x))
    down_got_x = across(down_part_x)
    back_1, head_sum, back_x_1, head_sum_x = backward(1, ())
    up_part_x = order.done(total_of(order(up_kept_x), up_got_x))
    up_got_x = across(up_part_x)
    up_part, down_part = order.done(two_totals(order(up_kept), up_got, down_kept, down_got))
    back_2, rest_sum, back_x_2, rest_sum_x = backward(2, (head_sum, head_sum_x))
    rest_kept, rest_kept_x, rest_sent = order.done(pair_halves(place, order(rest_sum), rest_sum_x, 1))
    rest_got = swap(rest_sent, "dp", 1)
    down_kept, down_sent = order.done(summed(place, order(down_part), down_got_x, 2))
    down_got = swap(down_sent, "dp", 2)
    first_own, first_other = order.done(
        entry_back(
            place, (order(back_0), back_1, back_2), (back_x_0, back_x_1, back_x_2), qkv_turned, (qkv_a, qkv_b)
        )
    )
    first_other = near(first_other)
    output, sums_out = order.done(
        row_wise(leave, "leave", (order(middle), cotangent, out_own, out_other), (table,), ((shape, BF16),), 2, 3)
    )
    input_gradient, sums_one = order.done(
        row_wise(
            back_first, "back_first", (order(tokens), first_own, first_other, middle_grad), (table,), ((shape, F32),), 3, 3
        )
    )
    sums = order.done(tabulate(order(sums_one), sums_two, sums_out, table, bias_sum, bias_sum_x))
    sums_near = near(sums)
    up_kept, up_sent = order.done(summed(place, order(up_part), up_got_x, 1))
    up_got = swap(up_sent, "dp", 1)
    down_value = order.done(total_of(order(down_kept), down_got))
    down_got = on(down_value)
    rows_x, rows_z = rest_kept.shape[0], rest_kept.shape[0] // 2
    rest_part, slots, sent = order.done(
        ride(
            ride_first_kernel,
            "ride_first",
            ((rows_x, width), (TABLE, width), (rows_x + TABLE, width)),
            order(rest_kept),
            rest_kept_x,
            rest_got,
            sums,
            sums_near,
        )
    )
    rest_got = across(sent)
    first_kept, first_kept_x, first_sent = order.done(pair_halves(place, order(first_sum), first_sum_x, 1))
    first_got = swap(first_sent, "dp", 1)
    up_value = order.done(total_of(order(up_kept), up_got))
    up_got = on(up_value)
    rest_value, slots, sent = order.done(
        ride(
            ride_half_kernel,
            "ride_half",
            ((rows_z, width), (2 * TABLE, width), (rows_z + 2 * TABLE, width)),
            place,
            order(rest_part),
            rest_got,
            slots,
        )
    )
    rest_got = swap(sent, "dp", 2)
    slots = order.done(hold(order(slots)))
    for step in range(len(bits) - 1):
        last = step == len(bits) - 2
        held = (2 * slots.shape[0], width)
        outs = ((rows_z, width), held) if last else ((rows_z, width), held, (rows_z + held[0], width))
        results = order.done(
            ride(
                partial(ride_add_kernel, bit=2 if step == 0 else 3 + step),
                "ride_add",
                outs,
                place,
                order(rest_value),
                rest_got,
                slots,
            )
        )
        rest_value, slots = results[:2]
        rest_got = swap(rest_value, "dp", 2) if last else on(results[2], step)
        if step == 0:
            down_value = doubled(down_value, down_got)
            down_got = swap(down_value, "dp", 2)
            down_side = swap(down_value, "dp", 1)
            first_part_x, first_part = order.done(pair_total(order(first_kept), first_kept_x, first_got)[::-1])
            first_got = across(first_part_x)
            up_value = doubled(up_value, up_got)
            up_got = swap(up_value, "dp", 1)
            first_kept, first_sent = order.done(summed(place, order(first_part), first_got, 2))
            first_got = swap(first_sent, "dp", 2)
            down_got = order.done(hold(order(down_got), down_side))
            down_far = swap(down_got, "dp", 1)
    first_value = order.done(total_of(order(first_kept), first_got))
    first_got = on(first_value)
    (rest_all,) = order.done(
        ride(
            ride_lay_kernel,
            "ride_lay",
            ((rows_x + slots.shape[0], width),),
            place,
            order(rest_value),
            rest_got,
            slots,
        )
    )
    rest_got = swap(rest_all, "dp", 1)
    first_value = doubled(first_value, first_got)
    first_got = swap(first_value, "dp", 2)
    up_value = order.done(lay(place, order(up_value), up_got, 1))
    up_got = swap(up_value, "dp", 2)
    down_grad = order.done(lay_four(place, order(down_value), down_got, down_side, down_far))
    first_value = order.done(lay(place, order(first_value), first_got, 2))
    first_got = swap(first_value, "dp", 1)
    rest_total, ada_grad, *totals = order.done(finish(place, order(rest_all), rest_got, rows_x))
    up_grad = order.done(lay_out(place, order(up_value), up_got, 2))
    out_rows = out_weight.shape[0]
    out_grad, qkv_grad = order.done(lay_and_cut(place, order(first_value), first_got, 1, rest_total, out_rows))
    ada_bias_grad, gain_one_grad, gain_two_grad, down_bias_grad, up_bias_grad = [total.reshape(-1) for total in totals]
    return (
        output,
        input_gradient,
        gain_one_grad,
        qkv_grad.T,
        out_grad,
        gain_two_grad,
        up_grad,
        up_bias_grad,
        down_grad,
        down_bias_grad,
        ada_grad,
        ada_bias_grad,
    )


def solution(mesh):
    in_specs = (
        P(("dp", "mp"), None),
        P(("dp", "mp"), None),
        P("dp", None),
        P("dp"),
        P(),
        P(None, "mp"),
        P("mp", None),
        P(),
        P(None, "mp"),
        P("mp"),
        P("mp", None),
        P(),
        P(),
        P(),
    )
    out_specs = (
        P(("dp", "mp"), None),
        P(("dp", "mp"), None),
        P(),
        P(None, "mp"),
        P("mp", None),
        P(),
        P(None, "mp"),
        P("mp"),
        P("mp", None),
        P(),
        P(),
        P(),
    )
    return jax.shard_map(
        per_device, mesh=mesh, in_specs=in_specs, out_specs=out_specs, check_vma=False
    )
```
